128 devices in a mesh: row: 8 (over z, core), col: 16 (over y, x).
Axes of the slice: x: 4, y: 4, z: 4, core: 2. Of those that a mesh axis runs over, the one named last changes fastest.
Arguments:
- front_entries: float32 [16384, 16384], P('row', 'col'), may hold values from -6 to 6
- children: float32 [20480, 10240], P('row', 'col'), may hold values from -6 to 6
- child_maps: int32 [2, 80], replicated, may hold values from 0 to 127, as said below
- pivots: int32 [1024], replicated, may hold values from 0 to 16383, as said below
- diag_inverses: float32 [2, 512, 512], replicated, may hold values from -0.005859375 to 0.005859375
Outputs:
- factored: float32 [16384, 16384], P('row', 'col')
The draws below stay inside these ranges and needn't reach their ends.
Inputs may be any that keep to these rules, and one draw needn't show every extreme that they name: For each child the front blocks are distinct, and child_maps[h, i] equals i modulo 16: a child block lies in the same block-column of the device grid as its front block. `pivots`: distinct front rows.
All inputs are finite; a program needn't handle non-finite values.
Results may differ from the reference program's by a relative error of at most 0.0001.
Values sent between devices are 32-bit elements; how exact they have to be, the bound alone decides.
No kernel may reach another device: no remote copies, remote signals or barrier semaphores. Data moves between devices by JAX's collectives and lax.ppermute only.
A program may use at most 128 MiB of HBM per device.

```python
import jax
import jax.numpy as jnp
from jax import lax

FRONT = 16384
CHILD = 10240
BLK = 128
PANEL = 512
N_ROW = 8
N_COL = 16


def draw_child_maps(key, part):
    key = jax.random.fold_in(key, 11)
    classes = N_COL
    front_per = FRONT // BLK // classes
    child_per = CHILD // BLK // classes
    scores = jax.random.randint(key, (2, classes, front_per), 0, 2 ** 20) * front_per
    scores = scores + jnp.arange(front_per, dtype=jnp.int32)[None, None, :]
    scores = scores.at[:, :, front_per - 1].set(-1)
    scores = scores.at[:, 0, 0].set(-2)
    order = jnp.argsort(scores, axis=-1)[:, :, :child_per].astype(jnp.int32)
    blocks = jnp.arange(classes, dtype=jnp.int32)[None, :, None] + classes * order
    return blocks.transpose(0, 2, 1).reshape(2, child_per * classes).astype(jnp.int32)


def draw_pivots(key, part):
    key = jax.random.fold_in(key, 23)
    first_key, second_key = jax.random.split(key)
    middle = jax.random.permutation(first_key, jnp.arange(1, FRONT - 1, dtype=jnp.int32))[:2 * PANEL - 2]
    rows = jnp.concatenate([jnp.array([0, FRONT - 1], dtype=jnp.int32), middle.astype(jnp.int32)])
    return jax.random.permutation(second_key, rows).astype(jnp.int32)


def level_of(rng, dims, pieces, low, top_value):
    loudness = 1.0
    for dim, blocks in pieces:
        heights = jax.random.uniform(jax.random.fold_in(jax.random.fold_in(rng, 6), dim), (blocks,), jnp.float32, low / len(pieces), top_value / len(pieces))
        loudness = loudness * jnp.repeat(jnp.exp(heights), dims[dim] // blocks).reshape((-1,) + (1,) * (len(dims) - 1 - dim))
    return loudness


def centred(key, dims, width, bound, shards=(), kind=jnp.bfloat16):
    drawn = jax.random.normal(key, dims, jnp.float32) * width
    if len(shards) > 0:
        drawn = level_of(key, dims, shards, -0.22, 0.18) * drawn
    return jnp.clip(drawn, min=-bound, max=bound).astype(kind)


def setup_inputs(seed: int = 0) -> dict:
    streams_of = jax.random.split(jax.random.key(seed), 6)
    return {
        "front_entries": centred(streams_of[0], (FRONT, FRONT), 1.0, 6.0, ((0, 8), (1, 16)), jnp.float32),
        "children": centred(streams_of[1], (2 * CHILD, CHILD), 1.0, 6.0, ((0, 8), (1, 16)), jnp.float32),
        "child_maps": draw_child_maps(jax.random.fold_in(streams_of[5], 71), 0),
        "pivots": draw_pivots(jax.random.fold_in(streams_of[5], 71), 0),
        "diag_inverses": centred(streams_of[4], (2, PANEL, PANEL), (4 * PANEL * PANEL) ** -0.5, 0.005859375, (), jnp.float32),
    }


def to_natural(stored, parts_r, parts_c):
    size_r, size_c = stored.shape
    grid = stored.reshape(parts_r, size_r // BLK // parts_r, BLK, parts_c, size_c // BLK // parts_c, BLK)
    return grid.transpose(1, 0, 2, 4, 3, 5).reshape(size_r, size_c)


def to_storage(natural, parts_r, parts_c):
    size_r, size_c = natural.shape
    grid = natural.reshape(size_r // BLK // parts_r, parts_r, BLK, size_c // BLK // parts_c, parts_c, BLK)
    return grid.transpose(1, 0, 2, 4, 3, 5).reshape(size_r, size_c)


def reference(front_entries, children, child_maps, pivots, diag_inverses):
    front = to_natural(front_entries, N_ROW, N_COL)
    offsets = jnp.arange(BLK, dtype=jnp.int32)
    for half in range(2):
        child = to_natural(children[half * CHILD:(half + 1) * CHILD], N_ROW // 2, N_COL)
        index = (child_maps[half][:, None] * BLK + offsets[None, :]).reshape(-1).astype(jnp.int32)
        spread = jnp.zeros((CHILD, FRONT), jnp.float32).at[:, index].add(child)
        front = front.at[index, :].add(spread)
    positions = jnp.arange(FRONT, dtype=jnp.int32)
    for step in range(2):
        used = pivots[:(step + 1) * PANEL]
        chosen = pivots[step * PANEL:(step + 1) * PANEL]
        upper = jnp.where(positions[None, :] >= (step + 1) * PANEL, front[chosen, :], jnp.float32(0.0))
        panel = front[:, step * PANEL:(step + 1) * PANEL]
        lower = jnp.dot(panel, diag_inverses[step], precision=lax.Precision.HIGHEST, preferred_element_type=jnp.float32)
        active = jnp.all(positions[:, None] != used[None, :], axis=1)
        update = jnp.dot(lower, upper, precision=lax.Precision.HIGHEST, preferred_element_type=jnp.float32)
        front = front - jnp.where(active[:, None], update, jnp.float32(0.0))
        fresh = jnp.where(active[:, None], lower, panel)
        front = front.at[:, step * PANEL:(step + 1) * PANEL].set(fresh)
    return to_storage(front, N_ROW, N_COL)
```

```python
import functools

import jax
import jax.numpy as jnp
from jax import lax
from jax.experimental import pallas as pl
from jax.experimental.pallas import tpu as pltpu
from jax.sharding import PartitionSpec as P

BLK = 128
PANEL = 512
MIB = 1 << 20
F32 = jnp.float32
BF16 = jnp.bfloat16
SMEM = pl.BlockSpec(memory_space=pltpu.SMEM)
VMEM = pl.BlockSpec(memory_space=pltpu.VMEM)
ANY = pl.BlockSpec(memory_space=pl.ANY)
KEPT_AT = 0
GOT_AT = 16
KEPT_COL = 32
GOT_COL = 40
ROW, COL, SIDE = 48, 49, 50


def split(x):
    high = x.astype(BF16)
    return high, (x - high.astype(F32)).astype(BF16)


def dot3(a, b):
    dot = functools.partial(jnp.dot, preferred_element_type=F32)
    return dot(a[0], b[0]) + (dot(a[0], b[1]) + dot(a[1], b[0]))


def params(mib):
    return pltpu.CompilerParams(vmem_limit_bytes=mib * MIB)


def cost(flops, moved):
    return pl.CostEstimate(flops=flops, bytes_accessed=moved, transcendentals=0)


def first_block(maps, child, here_col):
    place, found = jnp.int32(0), jnp.int32(0)
    for d in range(5):
        hit = (maps[child, d * 16 + here_col] // 16 == 0).astype(jnp.int32)
        place, found = place + d * hit, found + hit
    return place, found


def prepare_kernel(maps, front, pieces, first, rest, panel, table, kept, sem):
    here_row, here_col = lax.axis_index("row"), lax.axis_index("col")
    side = here_row // 4
    other = 1 - side
    place, found = first_block(maps, side, here_col)
    got_place, _ = first_block(maps, other, here_col)

    def columns(d):
        return pl.ds(pl.multiple_of(d * BLK, BLK), BLK)

    copies = [
        pltpu.make_async_copy(pieces.at[:, other, :, columns(place)], first, sem.at[0]),
        pltpu.make_async_copy(pieces.at[:, side, :, columns(place)], kept, sem.at[1]),
        pltpu.make_async_copy(front.at[:, pl.ds(0, BLK)], panel, sem.at[2]),
    ]
    for j in range(4):
        d = j + (j >= place).astype(jnp.int32)
        copies.append(
            pltpu.make_async_copy(pieces.at[:, other, :, columns(d)], rest.at[j], sem.at[3 + j])
        )
    for copy in copies:
        copy.start()
    for kk in range(16):
        table[KEPT_AT + kk] = -1
        table[GOT_AT + kk] = -1
    for m in range(10):
        table[KEPT_AT + maps[side, m * 8 + here_row] // 8] = m
        table[GOT_AT + maps[other, m * 8 + here_row] // 8] = m
    for d in range(5):
        table[KEPT_COL + d] = maps[side, d * 16 + here_col] // 16
    table[GOT_COL] = maps[other, got_place * 16 + here_col] // 16
    for j in range(4):
        d = j + (j >= got_place).astype(jnp.int32)
        table[GOT_COL + 1 + j] = maps[other, d * 16 + here_col] // 16
    table[ROW] = here_row
    table[COL] = here_col
    table[SIDE] = side
    copies[1].wait()
    copies[2].wait()

    @pl.when(found > 0)
    def _():
        for m in range(10):
            at = pl.multiple_of(maps[side, m * 8 + here_row] // 8 * BLK, BLK)
            panel[pl.ds(at, BLK), :] += kept[m]

    copies[0].wait()
    for copy in copies[3:]:
        copy.wait()


def prepare(maps, front, pieces):
    return pl.pallas_call(
        prepare_kernel,
        out_shape=[
            jax.ShapeDtypeStruct((10, BLK, BLK), F32),
            jax.ShapeDtypeStruct((4, 10, BLK, BLK), F32),
            jax.ShapeDtypeStruct((2048, BLK), F32),
            jax.ShapeDtypeStruct((64,), jnp.int32),
        ],
        in_specs=[SMEM, ANY, ANY],
        out_specs=[ANY, ANY, VMEM, SMEM],
        scratch_shapes=[pltpu.VMEM((10, BLK, BLK), F32), pltpu.SemaphoreType.DMA((7,))],
        compiler_params=params(8),
        cost_estimate=cost(0, 9 * MIB),
        name="prepare",
    )(maps, front, pieces)


def pivot_kernel(
    maps, pivots, front, children, own, away, corner, marks, spread, inverse, sem, child_sem
):
    here_row, here_col = lax.axis_index("row"), lax.axis_index("col")
    side, quarter = here_row // 4, here_row % 4
    core = here_row % 2
    own[...] = jnp.zeros_like(own)
    away[...] = jnp.zeros_like(away)
    marks[...] = jnp.zeros_like(marks)
    spread[...] = jnp.zeros_like(spread)

    def clear(b, carry):
        inverse[b] = -1
        return carry

    lax.fori_loop(0, 128, clear, 0, unroll=16)
    for k in range(20):
        inverse[maps[side, 4 * k + quarter]] = k

    started = jnp.int32(0), jnp.int32(0)
    for half in range(2):

        def visit(p, counts, half=half):
            pivot = pivots[half * PANEL + p]
            block, offset = pivot >> 7, pivot & 127
            child_block = inverse[block]
            mine = (block & 7) == here_row
            shared = ((block & 3) == quarter) & (child_block >= 0)

            @pl.when(mine)
            def _():
                at = (block >> 3) * BLK + offset
                marks[pl.ds(at, 1), :] = jnp.full((1, BLK), half + 1, F32)

                @pl.when(core == half)
                def _():
                    pltpu.make_async_copy(
                        front.at[pl.ds(at, 1), :], own.at[pl.ds(p, 1), :], sem
                    ).start()

                @pl.when(core != half)
                def _():
                    pltpu.make_async_copy(
                        front.at[pl.ds(at, 1), :], away.at[pl.ds(p, 1), :], sem
                    ).start()

            @pl.when(shared)
            def _():
                pltpu.make_async_copy(
                    children.at[pl.ds(child_block * BLK + offset, 1), :],
                    spread.at[half ^ core, pl.ds(p, 1), :],
                    child_sem,
                ).start()

            return counts[0] + mine.astype(jnp.int32), counts[1] + shared.astype(jnp.int32)

        started = lax.fori_loop(0, PANEL, visit, started, unroll=4)

    def wait_front(_, carry):
        pltpu.make_async_copy(front.at[pl.ds(0, 1), :], own.at[pl.ds(0, 1), :], sem).wait()
        return carry

    def wait_child(_, carry):
        pltpu.make_async_copy(
            children.at[pl.ds(0, 1), :], spread.at[0, pl.ds(0, 1), :], child_sem
        ).wait()
        return carry

    lax.fori_loop(0, started[0], wait_front, 0)
    lax.fori_loop(0, started[1], wait_child, 0)
    for d in range(5):
        to = pl.ds(pl.multiple_of(maps[side, d * 16 + here_col] // 16 * BLK, BLK), BLK)
        own[:, to] += spread[0, :, d * BLK : (d + 1) * BLK]
        away[:, to] += spread[1, :, d * BLK : (d + 1) * BLK]
    wanted = jnp.where(here_col < 4, 1, 0)
    corner[...] = jnp.where(wanted == core, own[:, :BLK], away[:, :BLK])


def pivot_terms(maps, pivots, front, children):
    return pl.pallas_call(
        pivot_kernel,
        out_shape=[
            jax.ShapeDtypeStruct((PANEL, 1024), F32),
            jax.ShapeDtypeStruct((PANEL, 1024), F32),
            jax.ShapeDtypeStruct((PANEL, BLK), F32),
            jax.ShapeDtypeStruct((2048, BLK), F32),
        ],
        in_specs=[SMEM, SMEM, ANY, ANY],
        out_specs=[VMEM, VMEM, VMEM, VMEM],
        scratch_shapes=[
            pltpu.VMEM((2, PANEL, 640), F32),
            pltpu.SMEM((128,), jnp.int32),
            pltpu.SemaphoreType.DMA(()),
            pltpu.SemaphoreType.DMA(()),
        ],
        compiler_params=params(20),
        cost_estimate=cost(0, 24 * MIB),
        name="pivot_terms",
    )(maps, pivots, front, children)


def panel_kernel(table, panel, got, corner, top, bottom):
    top[:1024, :] = panel[:1024, :]
    bottom[:1024, :] = panel[1024:, :]

    @pl.when(table[GOT_COL] == 0)
    def _():
        for kk in range(16):
            m = table[GOT_AT + kk]
            half = top if kk < 8 else bottom
            at = kk % 8 * BLK

            @pl.when(m >= 0)
            def _(half=half, at=at, m=m):
                half[at : at + BLK, :] += got[m]

    top[1024:, :] = corner[:256, :]
    bottom[1024:, :] = corner[256:, :]


def whole_panel(table, panel, got, corner):
    shape = jax.ShapeDtypeStruct((1280, BLK), F32)
    return pl.pallas_call(
        panel_kernel,
        out_shape=[shape, shape],
        in_specs=[SMEM, VMEM, VMEM, VMEM],
        out_specs=[VMEM, VMEM],
        compiler_params=params(12),
        cost_estimate=cost(0, 3 * MIB),
        name="whole_panel",
    )(table, panel, got, corner)


def lower_kernel(
    table, tiles, corners, inverses, marks, high, low, picked, cross, inv_h, inv_l, next_h, next_l
):
    def beside(ref, blocks):
        return jnp.concatenate([ref[b] for b in blocks], axis=1)

    @pl.when(pl.program_id(0) == 0)
    def _():
        for p in range(2):
            inv_h[p], inv_l[p] = split(inverses[p])
        next_h[:256], next_l[:256] = split(beside(corners, range(4, 8)))
        next_h[256:], next_l[256:] = split(beside(corners, range(8, 12)))
        inverse = inv_h[0], inv_l[0]
        cross[:256] = dot3(split(beside(corners, range(0, 4))), inverse)
        cross[256:] = dot3(split(beside(corners, range(12, 16))), inverse)

    col = table[COL]
    slot = col % 4
    for half in range(2):
        mark = jnp.concatenate([marks[half]] * 4, axis=1)
        first = beside(tiles, range(0, 4) if half == 0 else range(12, 16))
        second = beside(tiles, range(4, 8) if half == 0 else range(8, 12))
        lower = dot3(split(first), (inv_h[0], inv_l[0]))
        lower = jnp.where(mark != 1, lower, 0.0)
        terms = split(lower)
        high[half, :, :PANEL], low[half, :, :PANEL] = terms
        second = second - dot3(terms, (next_h[...], next_l[...]))
        later = dot3(split(second), (inv_h[1], inv_l[1]))
        later = jnp.where(mark == 0, later, 0.0)
        high[half, :, PANEL:], low[half, :, PANEL:] = split(later)
        chosen = jnp.where(col < 4, lower, later)
        out = chosen[:, :BLK]
        for s in range(1, 4):
            out = jnp.where(slot == s, chosen[:, s * BLK : (s + 1) * BLK], out)
        picked[half] = out


def lowers(table, gathered, inverses, marks):
    return pl.pallas_call(
        lower_kernel,
        out_shape=[
            jax.ShapeDtypeStruct((2, 1024, 1024), BF16),
            jax.ShapeDtypeStruct((2, 1024, 1024), BF16),
            jax.ShapeDtypeStruct((2, 1024, BLK), F32),
            jax.ShapeDtypeStruct((PANEL, PANEL), F32),
        ],
        grid_spec=pltpu.PrefetchScalarGridSpec(
            num_scalar_prefetch=1,
            grid=(4,),
            in_specs=[
                pl.BlockSpec((16, 256, BLK), lambda t, s: (0, t, 0)),
                pl.BlockSpec((16, 256, BLK), lambda t, s: (0, 4, 0)),
                pl.BlockSpec((2, PANEL, PANEL), lambda t, s: (0, 0, 0)),
                pl.BlockSpec((2, 256, BLK), lambda t, s: (0, t, 0)),
            ],
            out_specs=[
                pl.BlockSpec((2, 256, 1024), lambda t, s: (0, t, 0)),
                pl.BlockSpec((2, 256, 1024), lambda t, s: (0, t, 0)),
                pl.BlockSpec((2, 256, BLK), lambda t, s: (0, t, 0)),
                pl.BlockSpec((PANEL, PANEL), lambda t, s: (0, 0)),
            ],
            scratch_shapes=[
                pltpu.VMEM((2, PANEL, PANEL), BF16),
                pltpu.VMEM((2, PANEL, PANEL), BF16),
                pltpu.VMEM((PANEL, PANEL), BF16),
                pltpu.VMEM((PANEL, PANEL), BF16),
            ],
        ),
        compiler_params=params(44),
        cost_estimate=cost(3 * 6 * 2048 * PANEL * PANEL, 24 * MIB),
        name="lowers",
    )(table, gathered, gathered, inverses, marks.reshape(2, 1024, BLK))


def update_kernel(
    table, front, kept_a, kept_b, got0_a, got0_b, got_a, got_b, high, low, picked, marks,
    own, swapped, cross, out, upper_h, upper_l,
):
    step = pl.program_id(0)
    here_row, col = table[ROW], table[COL]

    @pl.when(step == 0)
    def _():
        core = here_row % 2
        lane = lax.broadcasted_iota(jnp.int32, (PANEL, 1024), 1)
        inside = lane < BLK
        first = jnp.where(core == 0, own[...], swapped[...])
        first = jnp.where(inside & (col < 4), 0.0, first)
        terms = split(first)
        upper_h[:PANEL], upper_l[:PANEL] = terms
        second = jnp.where(core == 0, swapped[...], own[...])
        second = second - dot3(split(cross[...]), terms)
        second = jnp.where(inside & (col < 8), 0.0, second)
        upper_h[PANEL:], upper_l[PANEL:] = split(second)

    change = dot3((high[...], low[...]), (upper_h[...], upper_l[...]))
    out[...] = front[...] - change
    for part in range(2):
        rows = slice(part * BLK, (part + 1) * BLK)
        kept = kept_a if part == 0 else kept_b
        got0 = got0_a if part == 0 else got0_b
        got = got_a if part == 0 else got_b

        @pl.when(table[KEPT_AT + 2 * step + part] >= 0)
        def _(rows=rows, kept=kept):
            for d in range(5):
                to = pl.ds(pl.multiple_of(table[KEPT_COL + d] * BLK, BLK), BLK)
                out[rows, to] += kept[0, 0, :, d * BLK : (d + 1) * BLK]

        @pl.when(table[GOT_AT + 2 * step + part] >= 0)
        def _(rows=rows, got0=got0, got=got):
            for j in range(5):
                to = pl.ds(pl.multiple_of(table[GOT_COL + j] * BLK, BLK), BLK)
                out[rows, to] += got0[0] if j == 0 else got[j - 1, 0]

    @pl.when(col < 8)
    def _():
        active = jnp.where(col < 4, (marks[...] != 1).astype(F32), (marks[...] == 0).astype(F32))
        out[:, :BLK] = jnp.where(active > 0, picked[...], out[:, :BLK])


def update(table, front, pieces, got0, got, high, low, picked, marks, own, swapped, cross):
    def kept_at(part):
        return lambda t, s: (jnp.maximum(s[KEPT_AT + 2 * t + part], 0), s[SIDE], 0, 0)

    def got0_at(part):
        return lambda t, s: (jnp.maximum(s[GOT_AT + 2 * t + part], 0), 0, 0)

    def got_at(part):
        return lambda t, s: (0, jnp.maximum(s[GOT_AT + 2 * t + part], 0), 0, 0)

    tile = pl.BlockSpec((256, 1024), lambda t, s: (t, 0))
    narrow = pl.BlockSpec((256, BLK), lambda t, s: (t, 0))
    whole = pl.BlockSpec((PANEL, 1024), lambda t, s: (0, 0))
    return pl.pallas_call(
        update_kernel,
        out_shape=jax.ShapeDtypeStruct((2048, 1024), F32),
        grid_spec=pltpu.PrefetchScalarGridSpec(
            num_scalar_prefetch=1,
            grid=(8,),
            in_specs=[
                tile,
                pl.BlockSpec((1, 1, BLK, 640), kept_at(0)),
                pl.BlockSpec((1, 1, BLK, 640), kept_at(1)),
                pl.BlockSpec((1, BLK, BLK), got0_at(0)),
                pl.BlockSpec((1, BLK, BLK), got0_at(1)),
                pl.BlockSpec((4, 1, BLK, BLK), got_at(0)),
                pl.BlockSpec((4, 1, BLK, BLK), got_at(1)),
                tile,
                tile,
                narrow,
                narrow,
                whole,
                whole,
                pl.BlockSpec((PANEL, PANEL), lambda t, s: (0, 0)),
            ],
            out_specs=tile,
            scratch_shapes=[pltpu.VMEM((1024, 1024), BF16), pltpu.VMEM((1024, 1024), BF16)],
        ),
        compiler_params=params(48),
        cost_estimate=cost(6 * 2048 * 1024 * 1024, 40 * MIB),
        name="update",
    )(
        table, front, pieces, pieces, got0, got0, got, got,
        high.reshape(2048, 1024), low.reshape(2048, 1024), picked.reshape(2048, BLK), marks,
        own, swapped, cross,
    )


def swap(block, axis, partner, count):
    return lax.ppermute(block, axis, [(i, partner(i)) for i in range(count)])


def next_core(i):
    return i ^ 1


def even_chip(i):
    return i ^ 2


def odd_chip(i):
    return (3 - i // 2) * 2 + i % 2


def row_sum(own, away, here_row):
    chip = here_row // 2
    even_bit = (chip ^ (chip >> 1)) & 1
    odd_bit = chip >> 1
    total = own + swap(away, "row", next_core, 8)
    parts = []
    for which in range(2):
        steps = [(even_chip, even_bit), (odd_chip, odd_bit)]
        if which:
            steps.reverse()
        part = total[which * 256 : (which + 1) * 256]
        for partner, bit in steps:
            size = part.shape[0] // 2
            leave = jnp.where(bit == 0, part[size:], part[:size])
            stay = jnp.where(bit == 0, part[:size], part[size:])
            part = stay + swap(leave, "row", partner, 8)
        for partner, bit in steps[::-1]:
            came = swap(part, "row", partner, 8)
            part = jnp.concatenate(
                [jnp.where(bit == 0, part, came), jnp.where(bit == 0, came, part)], axis=0
            )
        parts.append(part)
    half = jnp.concatenate(parts, axis=0)
    return half, swap(half, "row", next_core, 8)


def local(front, children, child_maps, pivots, diag_inverses):
    here_row, here_col = lax.axis_index("row"), lax.axis_index("col")
    pieces = children.reshape(10, 2, BLK, 640)
    first, rest, panel, table = prepare(child_maps, front, pieces)
    across = functools.partial(swap, axis="row", partner=lambda i: i ^ 4, count=8)
    got0 = across(first)
    own, away, corner, marks = pivot_terms(child_maps, pivots, front, children)
    corner = lax.psum(corner, "row")
    rest, got0 = lax.optimization_barrier((rest, got0))
    got = across(rest)
    top, bottom = whole_panel(table, panel, got0, corner)
    folded = lax.ppermute(bottom, "col", [(c, (3 - c // 4) * 4 + c % 4) for c in range(8)])
    gathered = lax.all_gather(jnp.where(here_col < 8, top, folded), "col")
    half, swapped = row_sum(own, away, here_row)
    high, low, picked, cross = lowers(table, gathered, diag_inverses, marks)
    return update(
        table, front, pieces, got0, got, high, low, picked, marks, half, swapped, cross
    )


def solution(mesh):
    return jax.shard_map(
        local,
        mesh=mesh,
        in_specs=(P("row", "col"), P("row", "col"), P(), P(), P()),
        out_specs=P("row", "col"),
        check_vma=False,
    )
```

```python
import functools

import jax
import jax.numpy as jnp
from jax import lax
from jax.experimental import pallas as pl
from jax.experimental.pallas import tpu as pltpu
from jax.sharding import PartitionSpec as P

BLK = 128
PANEL = 512
MIB = 1 << 20
F32 = jnp.float32
BF16 = jnp.bfloat16
SMEM = pl.BlockSpec(memory_space=pltpu.SMEM)
VMEM = pl.BlockSpec(memory_space=pltpu.VMEM)
HBM = pl.BlockSpec(memory_space=pltpu.HBM)
KEPT_AT = 0
GOT_AT = 16
KEPT_COL = 32
GOT_COL = 40
ROW, COL, SIDE = 48, 49, 50
GOT_ROW = 52


def split(x):
    high = x.astype(BF16)
    return high, (x - high.astype(F32)).astype(BF16)


def dot3(a, b):
    rows = a[0].shape[0]
    both = jnp.dot(jnp.concatenate(a, axis=0), b[0], preferred_element_type=F32)
    return both[:rows] + (both[rows:] + jnp.dot(a[0], b[1], preferred_element_type=F32))


def params(mib):
    return pltpu.CompilerParams(vmem_limit_bytes=mib * MIB)


def in_hbm(x):
    return pltpu.with_memory_space_constraint(x, pltpu.HBM)


def cost(flops, moved):
    return pl.CostEstimate(flops=flops, bytes_accessed=moved, transcendentals=0)


def first_block(maps, child, here_col):
    place, found = jnp.int32(0), jnp.int32(0)
    for d in range(5):
        hit = (maps[child, d * 16 + here_col] // 16 == 0).astype(jnp.int32)
        place, found = place + d * hit, found + hit
    return place, found


def prepare_kernel(
    maps, pivots, front, pieces, first, rest_a, rest_b, rest_c, rest_d, panel, own, away, table,
    sending, kept, total, sem,
):
    here_row, here_col = lax.axis_index("row"), lax.axis_index("col")
    side, core = here_row // 4, here_row % 2
    other = 1 - side
    place, found = first_block(maps, side, here_col)
    got_place, _ = first_block(maps, other, here_col)

    def columns(d):
        return pl.ds(pl.multiple_of(d * BLK, BLK), BLK)

    reads = [
        pltpu.make_async_copy(pieces.at[:, other], sending, sem.at[0]),
        pltpu.make_async_copy(pieces.at[:, side, :, columns(place)], kept, sem.at[1]),
        pltpu.make_async_copy(front.at[:, pl.ds(0, BLK)], panel, sem.at[2]),
    ]
    writes = []
    for j, target in enumerate((rest_a, rest_b, rest_c, rest_d)):
        d = j + (j >= place).astype(jnp.int32)
        writes.append(pltpu.make_async_copy(sending.at[:, :, columns(d)], target, sem.at[3 + j]))
    for copy in reads:
        copy.start()
    for kk in range(16):
        table[KEPT_AT + kk] = -1
        table[GOT_AT + kk] = -1
    for m in range(10):
        table[KEPT_AT + maps[side, m * 8 + here_row] // 8] = m
        target = maps[other, m * 8 + here_row] // 8
        table[GOT_AT + target] = m
        table[GOT_ROW + m] = target
    for d in range(5):
        table[KEPT_COL + d] = maps[side, d * 16 + here_col] // 16
    table[GOT_COL] = maps[other, got_place * 16 + here_col] // 16
    for j in range(4):
        d = j + (j >= got_place).astype(jnp.int32)
        table[GOT_COL + 1 + j] = maps[other, d * 16 + here_col] // 16
    table[ROW] = here_row
    table[COL] = here_col
    table[SIDE] = side
    turned = pivots[...].T
    wanted = jnp.concatenate(
        [jnp.where(here_col < 4, turned[:, 4 + k : 5 + k], turned[:, k : k + 1]) for k in range(4)],
        axis=0,
    )
    block, offset = wanted >> 7, wanted & 127
    mine = jnp.where((block & 7) == here_row, (block >> 3) * BLK + offset, -1)
    sent = jnp.full_like(mine, -1)
    for m in range(10):
        hit = (block == maps[side, m * 8 + (here_row ^ 4)]) & (found > 0)
        sent = jnp.where(hit, m * BLK + offset, sent)
    reads[0].wait()
    for copy in writes:
        copy.start()
    first[...] = sending[:, :, columns(place)]
    reads[1].wait()
    reads[2].wait()

    @pl.when(found > 0)
    def _():
        for m in range(10):
            at = pl.multiple_of(maps[side, m * 8 + here_row] // 8 * BLK, BLK)
            panel[pl.ds(at, BLK), :] += kept[m]

    def rows_of(index, values, base):
        lane = lax.broadcasted_iota(jnp.int32, (PANEL, values.shape[0]), 1) + base
        chosen = jnp.where(lane == index, 1.0, 0.0).astype(BF16)
        both = jnp.concatenate(split(values), axis=1)
        return jnp.dot(chosen, both, preferred_element_type=F32)

    terms = jnp.zeros((PANEL, 2 * BLK), F32)
    for k in range(8):
        terms += rows_of(mine, panel[k * 256 : (k + 1) * 256, :], k * 256)
    for k in range(5):
        values = first[2 * k : 2 * k + 2].reshape(256, BLK)
        terms += rows_of(sent, values, k * 256)
    total[...] = terms[:, :BLK] + terms[:, BLK:]
    own[...] = total[pl.ds(pl.multiple_of(core * 256, 256), 256), :]
    away[...] = total[pl.ds(pl.multiple_of((1 - core) * 256, 256), 256), :]
    for copy in writes:
        copy.wait()


def prepare(maps, pivots, front, pieces):
    column = jax.ShapeDtypeStruct((10, BLK, BLK), F32)
    return pl.pallas_call(
        prepare_kernel,
        out_shape=[
            column,
            column,
            column,
            column,
            column,
            jax.ShapeDtypeStruct((2048, BLK), F32),
            jax.ShapeDtypeStruct((256, BLK), F32),
            jax.ShapeDtypeStruct((256, BLK), F32),
            jax.ShapeDtypeStruct((64,), jnp.int32),
        ],
        in_specs=[SMEM, VMEM, HBM, HBM],
        out_specs=[VMEM, HBM, HBM, HBM, HBM, VMEM, VMEM, VMEM, SMEM],
        scratch_shapes=[
            pltpu.VMEM((10, BLK, 640), F32),
            pltpu.VMEM((10, BLK, BLK), F32),
            pltpu.VMEM((PANEL, BLK), F32),
            pltpu.SemaphoreType.DMA((7,)),
        ],
        compiler_params=params(24),
        cost_estimate=cost(0, 9 * MIB),
        name="prepare",
    )(maps, pivots.reshape(8, BLK), in_hbm(front), in_hbm(pieces))


def pivot_kernel(mine_half, maps, pivots, front, children, *refs):
    rows, marks, spread, inverse, front_list, child_list, sem, child_sem = refs[-8:]
    rows[...] = jnp.zeros_like(rows)
    marks[...] = refs[0][...] if mine_half else jnp.zeros_like(marks)
    here_row, here_col = lax.axis_index("row"), lax.axis_index("col")
    side, quarter, core = here_row // 4, here_row % 4, here_row % 2
    half = core if mine_half else 1 - core
    spread[...] = jnp.zeros_like(spread)

    def clear(b, carry):
        inverse[b] = -1
        return carry

    lax.fori_loop(0, 128, clear, 0, unroll=16)
    for k in range(20):
        inverse[maps[side, 4 * k + quarter]] = k

    def visit(p, counts):
        pivot = pivots[half * PANEL + p]
        block, offset = pivot >> 7, pivot & 127
        child_block = inverse[block]
        mine = (block & 7) == here_row
        shared = ((block & 3) == quarter) & (child_block >= 0)
        front_list[counts[0]] = (((block >> 3) * BLK + offset) << 9) | p
        child_list[counts[1]] = ((child_block * BLK + offset) << 9) | p
        return counts[0] + mine.astype(jnp.int32), counts[1] + shared.astype(jnp.int32)

    counts = lax.fori_loop(0, PANEL, visit, (jnp.int32(0), jnp.int32(0)), unroll=8)
    mark = jnp.full((1, BLK), half + 1, jnp.int32).astype(F32)

    def take_front(n, carry):
        at, p = front_list[n] >> 9, front_list[n] & 511
        pltpu.make_async_copy(front.at[pl.ds(at, 1), :], rows.at[pl.ds(p, 1), :], sem).start()
        marks[pl.ds(at, 1), :] = mark
        return carry

    def take_child(n, carry):
        at, p = child_list[n] >> 9, child_list[n] & 511
        pltpu.make_async_copy(
            children.at[pl.ds(at, 1), :], spread.at[pl.ds(p, 1), :], child_sem
        ).start()
        return carry

    def wait(source, target, semaphore, count):
        def some(size):
            def body(_, carry):
                pltpu.make_async_copy(
                    source.at[pl.ds(0, size), :], target.at[pl.ds(0, size), :], semaphore
                ).wait()
                return carry

            return body

        lax.fori_loop(0, count // 16, some(16), 0)
        lax.fori_loop(0, count % 16, some(1), 0)

    lax.fori_loop(0, counts[0], take_front, 0)
    lax.fori_loop(0, counts[1], take_child, 0)
    wait(front, rows, sem, counts[0])
    wait(children, spread, child_sem, counts[1])
    for d in range(5):
        to = pl.ds(pl.multiple_of(maps[side, d * 16 + here_col] // 16 * BLK, BLK), BLK)
        rows[:, to] += spread[:, d * BLK : (d + 1) * BLK]


def pivot_terms(maps, pivots, front, children, *before):
    mine_half = len(before) > 0
    return pl.pallas_call(
        functools.partial(pivot_kernel, mine_half),
        out_shape=[
            jax.ShapeDtypeStruct((PANEL, 1024), F32),
            jax.ShapeDtypeStruct((2048, BLK), F32),
        ],
        in_specs=[SMEM, SMEM, HBM, HBM] + [VMEM] * len(before),
        out_specs=[VMEM, VMEM],
        scratch_shapes=[
            pltpu.VMEM((PANEL, 640), F32),
            pltpu.SMEM((128,), jnp.int32),
            pltpu.SMEM((PANEL + 1,), jnp.int32),
            pltpu.SMEM((PANEL + 1,), jnp.int32),
            pltpu.SemaphoreType.DMA(()),
            pltpu.SemaphoreType.DMA(()),
        ],
        compiler_params=params(12),
        cost_estimate=cost(0, 24 * MIB),
        name="pivot_terms_mine" if mine_half else "pivot_terms_other",
    )(maps, pivots, in_hbm(front), in_hbm(children), *before)


def panel_kernel(table, panel, got, top, bottom):
    top[...] = panel[:1024, :]
    bottom[...] = panel[1024:, :]

    @pl.when(table[GOT_COL] == 0)
    def _():
        for kk in range(16):
            m = table[GOT_AT + kk]
            half = top if kk < 8 else bottom
            at = kk % 8 * BLK

            @pl.when(m >= 0)
            def _(half=half, at=at, m=m):
                half[at : at + BLK, :] += got[m]


def whole_panel(table, panel, got):
    shape = jax.ShapeDtypeStruct((1024, BLK), F32)
    return pl.pallas_call(
        panel_kernel,
        out_shape=[shape, shape],
        in_specs=[SMEM, VMEM, VMEM],
        out_specs=[VMEM, VMEM],
        compiler_params=params(12),
        cost_estimate=cost(0, 3 * MIB),
        name="whole_panel",
    )(table, panel, got)


def flips(delta):
    return (delta & 1) ^ (delta >> 1), delta >> 1


def corner_kernel(table, own, swapped, inverses, factor_h, factor_l, cross):
    here_row, here_col = table[ROW], table[COL]
    core, x, y = here_row % 2, here_col % 4, here_col // 4
    mine = (y ^ (y >> 1)) & 1

    def corner(panel, half):
        blocks = []
        for xx in range(4):
            one, three = flips(xx ^ x)
            pair = mine ^ panel
            slot = jnp.where(half == 0, pair | (one << 1) | (three << 2), one | (three << 1) | (pair << 2))
            blocks.append(jnp.where(core == half, own[slot], swapped[slot]))
        return jnp.concatenate(blocks, axis=1)

    for p in range(2):
        factor_h[p], factor_l[p] = split(inverses[p])
    for half in range(2):
        rows = slice(half * 256, (half + 1) * 256)
        factor_h[2, rows, :], factor_l[2, rows, :] = split(corner(1, half))
        cross[rows, :] = dot3(split(corner(0, half)), (factor_h[0], factor_l[0]))


def corners(table, own, swapped, inverses):
    return pl.pallas_call(
        corner_kernel,
        out_shape=[
            jax.ShapeDtypeStruct((3, PANEL, PANEL), BF16),
            jax.ShapeDtypeStruct((3, PANEL, PANEL), BF16),
            jax.ShapeDtypeStruct((PANEL, PANEL), F32),
        ],
        in_specs=[SMEM, VMEM, VMEM, VMEM],
        out_specs=[VMEM] * 3,
        compiler_params=params(20),
        cost_estimate=cost(6 * PANEL**3, 8 * MIB),
        name="corners",
    )(table, own, swapped, inverses)


def upper_kernel(table, own, swapped, cross, high, low):
    here_row, col = table[ROW], table[COL]
    core = here_row % 2
    inside = lax.broadcasted_iota(jnp.int32, (PANEL, 1024), 1) < BLK
    first = jnp.where(core == 0, own[...], swapped[...])
    first = jnp.where(inside & (col < 4), 0.0, first)
    terms = split(first)
    high[:PANEL], low[:PANEL] = terms
    second = jnp.where(core == 0, swapped[...], own[...])
    second = second - dot3(split(cross[...]), terms)
    second = jnp.where(inside & (col < 8), 0.0, second)
    high[PANEL:], low[PANEL:] = split(second)


def uppers(table, own, swapped, cross):
    shape = jax.ShapeDtypeStruct((1024, 1024), BF16)
    return pl.pallas_call(
        upper_kernel,
        out_shape=[shape, shape],
        in_specs=[SMEM, VMEM, VMEM, VMEM],
        out_specs=[VMEM, VMEM],
        compiler_params=params(28),
        cost_estimate=cost(6 * PANEL * PANEL * 1024, 9 * MIB),
        name="uppers",
    )(table, own, swapped, cross)


def block_at(base, part, t, s):
    return jnp.maximum(s[base + part // 2 * 8 + 2 * t + part % 2], 0)


TILE = pl.BlockSpec((2, 256, 1024), lambda t, s: (0, t, 0))


def extend_kernel(columns, table, front, *refs):
    out, refs = refs[-1], refs[:-1]
    kept, *got = (refs[4 * k : 4 * k + 4] for k in range(1 + columns))
    step = pl.program_id(0)
    out[...] = front[...]
    for part in range(4):
        half, rest = part // 2, part % 2
        span = slice(rest * BLK, (rest + 1) * BLK)
        kk = half * 8 + 2 * step + rest

        @pl.when(table[KEPT_AT + kk] >= 0)
        def _(half=half, span=span, part=part):
            for d in range(5):
                to = pl.ds(pl.multiple_of(table[KEPT_COL + d] * BLK, BLK), BLK)
                out[half, span, to] += kept[part][0, 0, :, d * BLK : (d + 1) * BLK]

        @pl.when(table[GOT_AT + kk] >= 0)
        def _(half=half, span=span, part=part):
            for j in range(columns):
                to = pl.ds(pl.multiple_of(table[GOT_COL + j] * BLK, BLK), BLK)
                out[half, span, to] += got[j][part][0]


def extend(table, front, pieces, got):
    def kept_at(part):
        return lambda t, s: (block_at(KEPT_AT, part, t, s), s[SIDE], 0, 0)

    def got_at(part):
        return lambda t, s: (block_at(GOT_AT, part, t, s), 0, 0)

    kept_specs = [pl.BlockSpec((1, 1, BLK, 640), kept_at(part)) for part in range(4)]
    got_specs = [pl.BlockSpec((1, BLK, BLK), got_at(part)) for part in range(4)]
    return pl.pallas_call(
        functools.partial(extend_kernel, len(got)),
        out_shape=pltpu.HBM((2, 1024, 1024), F32),
        grid_spec=pltpu.PrefetchScalarGridSpec(
            num_scalar_prefetch=1,
            grid=(4,),
            in_specs=[TILE, *kept_specs, *got_specs * len(got)],
            out_specs=TILE,
        ),
        compiler_params=params(20),
        cost_estimate=cost(0, 22 * MIB),
        name="extend",
    )(table, in_hbm(front.reshape(2, 1024, 1024)), *[in_hbm(pieces)] * 4, *[g for g in got for _ in range(4)])


ORDERS = ((1, 3, 4, 12), (3, 1, 12, 4)), ((4, 12, 1, 3), (12, 4, 3, 1))


def update_kernel(table, front, *refs):
    blocks = refs[:4], refs[4:8]
    factor_h, factor_l, upper_h, upper_l, marks, out, panels, lower_h, lower_l = refs[8:]
    step = pl.program_id(0)
    col, core = table[COL], table[ROW] % 2

    def assemble(which):
        held, came, held_far, came_far = blocks[which]
        for c in range(16):
            one_x, three_x = flips((c ^ col) & 3)
            one_y, three_y = flips((c ^ col) >> 2)
            bits = {1: one_x, 3: three_x, 4: one_y, 12: three_y}
            even, odd = (ORDERS[q][which] for q in range(2))
            flip = [jnp.where(core == 0, bits[e], bits[o]) for e, o in zip(even, odd)]
            slot = flip[0] | (flip[1] << 1)
            later, far = flip[2] == 1, flip[3] == 1
            near_block = jnp.where(later, came[slot], held[slot])
            far_block = jnp.where(later, came_far[slot], held_far[slot])
            block = jnp.where(far, far_block, near_block)
            y, x = c // 4, c % 4
            rows = slice(0, 256) if y < 2 else slice(256, PANEL)
            panels[min(y, 3 - y), rows, x * BLK : (x + 1) * BLK] = block

    for which in range(2):
        pl.when(step // 2 == which)(functools.partial(assemble, which))

    mark = jnp.concatenate([marks[...].reshape(PANEL, BLK)] * 4, axis=1)
    lower = dot3(split(panels[0]), (factor_h[0], factor_l[0]))
    lower = jnp.where(mark != 1, lower, 0.0)
    terms = split(lower)
    lower_h[:, :PANEL], lower_l[:, :PANEL] = terms
    second = panels[1] - dot3(terms, (factor_h[2], factor_l[2]))
    later = dot3(split(second), (factor_h[1], factor_l[1]))
    later = jnp.where(mark == 0, later, 0.0)
    lower_h[:, PANEL:], lower_l[:, PANEL:] = split(later)
    change = dot3((lower_h[...], lower_l[...]), (upper_h[...], upper_l[...]))
    out[...] = front[...] - change.reshape(2, 256, 1024)

    @pl.when(col < 8)
    def _():
        chosen = jnp.where(col < 4, lower, later)
        fresh = chosen[:, :BLK]
        for s in range(1, 4):
            fresh = jnp.where(col % 4 == s, chosen[:, s * BLK : (s + 1) * BLK], fresh)
        active = jnp.where(col < 4, (marks[...] != 1).astype(F32), (marks[...] == 0).astype(F32))
        out[:, :, :BLK] = jnp.where(active > 0, fresh.reshape(2, 256, BLK), out[:, :, :BLK])


def update(table, front, blocks, factors, upper, marks):
    def whole(x):
        return pl.BlockSpec(x.shape, lambda t, s: (0,) * x.ndim, pipeline_mode=pl.Buffered(1))

    first = pl.BlockSpec((4, 256, BLK), lambda t, s: (0, jnp.minimum(t, 1), 0))
    second = pl.BlockSpec((4, 256, BLK), lambda t, s: (0, jnp.maximum(t - 2, 0), 0))
    constants = *factors, *upper
    return pl.pallas_call(
        update_kernel,
        out_shape=pltpu.HBM((2, 1024, 1024), F32),
        grid_spec=pltpu.PrefetchScalarGridSpec(
            num_scalar_prefetch=1,
            grid=(4,),
            in_specs=[
                TILE,
                *[first] * 4,
                *[second] * 4,
                *[whole(x) for x in constants],
                pl.BlockSpec((2, 256, BLK), lambda t, s: (0, t, 0)),
            ],
            out_specs=TILE,
            scratch_shapes=[
                pltpu.VMEM((2, PANEL, PANEL), F32),
                pltpu.VMEM((PANEL, 1024), BF16),
                pltpu.VMEM((PANEL, 1024), BF16),
            ],
        ),
        compiler_params=params(34),
        cost_estimate=cost(6 * 2048 * 1024 * 1024 + 3 * 6 * 2048 * PANEL * PANEL, 36 * MIB),
        name="update",
    )(table, in_hbm(front), *blocks[0], *blocks[1], *constants, marks.reshape(2, 1024, BLK))


def finish_kernel(table, front, got_b, got_c, got_d, out, held, read_sem, write_sem):
    del front
    got = got_b, got_c, got_d
    copies = []
    for j in range(3):
        for m in range(10):
            rows = pl.ds(pl.multiple_of(table[GOT_ROW + m] * BLK, BLK), BLK)
            columns = pl.ds(pl.multiple_of(table[GOT_COL + 2 + j] * BLK, BLK), BLK)
            there, here = out.at[rows, columns], held.at[j, m]
            copies.append(
                (
                    pltpu.make_async_copy(there, here, read_sem.at[j, m]),
                    pltpu.make_async_copy(here, there, write_sem.at[j, m]),
                )
            )
    for read, _ in copies:
        read.start()
    for n, (read, write) in enumerate(copies):
        read.wait()
        held[n // 10, n % 10] += got[n // 10][n % 10]
        write.start()
    for _, write in copies:
        write.wait()


def finish(table, front, *got):
    return pl.pallas_call(
        finish_kernel,
        out_shape=jax.ShapeDtypeStruct((2048, 1024), F32),
        in_specs=[SMEM, HBM, VMEM, VMEM, VMEM],
        out_specs=HBM,
        scratch_shapes=[
            pltpu.VMEM((3, 10, BLK, BLK), F32),
            pltpu.SemaphoreType.DMA((3, 10)),
            pltpu.SemaphoreType.DMA((3, 10)),
        ],
        input_output_aliases={1: 0},
        compiler_params=params(8),
        cost_estimate=cost(0, 6 * MIB),
        name="finish",
    )(table, front, *got)


def swap(block, axis, partner):
    count = lax.axis_size(axis)
    return lax.ppermute(block, axis, [(i, partner(i)) for i in range(count)])


def fold(block, here_col):
    came = lax.ppermute(block[1], "col", [(c, c ^ 12) for c in range(8)])
    return jnp.where(here_col < 8, block[0], came)


def local(front, children, child_maps, pivots, diag_inverses):
    here_row, here_col = lax.axis_index("row"), lax.axis_index("col")
    chip = here_row // 2
    together = lax.optimization_barrier
    pieces = children.reshape(10, 2, BLK, 640)

    def by_row(block, mask):
        return swap(block, "row", lambda i: i ^ mask)

    def by_col(block, mask):
        return swap(block, "col", lambda i: i ^ mask)

    bits = (chip ^ (chip >> 1)) & 1, chip >> 1
    rings = [[(r, r ^ ((2, 6), (6, 2))[r % 2][k]) for r in range(8)] for k in range(2)]
    bits = [jnp.where(here_row % 2 == 0, bits[k], bits[1 - k]) for k in range(2)]

    def halve(terms, step):
        size = terms[0].shape[0] // 2

        def half(bit):
            return sum(lax.dynamic_slice_in_dim(term, bit * size, size, 0) for term in terms)

        came = lax.ppermute(half(1 - bits[step]), "row", rings[step])
        return half(bits[step]) + came

    def double(part, step):
        came = lax.ppermute(part, "row", rings[step])
        low, high = jnp.where(bits[step] == 0, part, came), jnp.where(bits[step] == 0, came, part)
        return jnp.concatenate([low, high], axis=0)

    def gather_step(block, which, step):
        route = [
            (r * 16 + c, r * 16 + (c ^ ORDERS[r % 2][which][step]))
            for r in range(8)
            for c in range(16)
        ]
        return lax.ppermute(block, ("row", "col"), route)

    first, rest_a, rest_b, rest_c, rest_d, panel, corner, away, table = prepare(
        child_maps, pivots, front, pieces
    )
    got0 = by_row(first, 4)
    corner = corner + by_row(away, 1)
    corner = corner + (by_row(corner, 2) + (by_row(corner, 6) + by_row(corner, 4)))
    away_rows, marks = pivot_terms(child_maps, pivots, front, children)
    got0, away_rows, rest_a, marks, corner = together((got0, away_rows, rest_a, marks, corner))

    top, bottom = whole_panel(table, panel, got0)
    mine = fold((top, bottom), here_col)
    corner = fold((corner, corner), here_col)[None]
    got_a = by_row(rest_a, 4)
    own_rows, marks = pivot_terms(child_maps, pivots, front, children, marks)
    total = own_rows, by_row(away_rows, 1)
    mine, corner, total, got_a, rest_b = together((mine, corner, total, got_a, rest_b))

    def corner_step(block, step):
        masks = ((4, 1, 3), (1, 3, 4))
        route = [
            (r * 16 + c, r * 16 + (c ^ masks[r % 2][step])) for r in range(8) for c in range(16)
        ]
        return jnp.concatenate([block, lax.ppermute(block, ("row", "col"), route)], axis=0)

    held = [mine[None, :PANEL], mine[None, PANEL:]]
    for k in range(2):
        came = [gather_step(held[w], w, k) for w in range(2)]
        held = [jnp.concatenate([h, c], axis=0) for h, c in zip(held, came)]
        corner = corner_step(corner, k)
        total = halve(total if k == 0 else (total,), k)
        held, corner, total = together((held, corner, total))
    came = [gather_step(held[w], w, 2) for w in range(2)]
    corner = corner_step(corner, 2)
    total = double(total, 1)
    came, corner, total = together((came, corner, total))
    held_far = [gather_step(held[w], w, 3) for w in range(2)]
    factors = corners(table, corner, by_row(corner, 1), diag_inverses)
    total = double(total, 0)
    came, held_far, total, rest_b = together((came, held_far, total, rest_b))
    came_far = [gather_step(came[w], w, 3) for w in range(2)]
    got_b = by_row(rest_b, 4)
    upper = uppers(table, total, by_row(total, 1), factors[2])
    front = extend(table, front, pieces, (got0, got_a))
    came_far, got_b, rest_c, rest_d = together((came_far, got_b, rest_c, rest_d))
    got_c = by_row(rest_c, 4)
    got_d = by_row(rest_d, 4)
    blocks = [(held[w], came[w], held_far[w], came_far[w]) for w in range(2)]
    front = update(table, front, blocks, factors[:2], upper, marks)
    return finish(table, front.reshape(2048, 1024), got_b, got_c, got_d)


def solution(mesh):
    return jax.shard_map(
        local,
        mesh=mesh,
        in_specs=(P("row", "col"), P("row", "col"), P(), P(), P()),
        out_specs=P("row", "col"),
        check_vma=False,
    )
```

```python
import functools

import jax
import jax.numpy as jnp
from jax import lax
from jax.experimental import pallas as pl
from jax.experimental.pallas import tpu as pltpu
from jax.sharding import PartitionSpec as P

BLK = 128
PANEL = 512
MIB = 1 << 20
F32 = jnp.float32
BF16 = jnp.bfloat16
SMEM = pl.BlockSpec(memory_space=pltpu.SMEM)
VMEM = pl.BlockSpec(memory_space=pltpu.VMEM)
HBM = pl.BlockSpec(memory_space=pltpu.HBM)
KEPT_AT = 0
GOT_AT = 16
KEPT_COL = 32
GOT_COL = 40
ROW, COL, SIDE = 48, 49, 50
GOT_ROW = 52


def split(x):
    high = x.astype(BF16)
    return high, (x - high.astype(F32)).astype(BF16)


def dot3(a, b):
    rows = a[0].shape[0]
    both = jnp.dot(jnp.concatenate(a, axis=0), b[0], preferred_element_type=F32)
    return both[:rows] + (both[rows:] + jnp.dot(a[0], b[1], preferred_element_type=F32))


def params(mib):
    return pltpu.CompilerParams(vmem_limit_bytes=mib * MIB)


def in_hbm(x):
    return pltpu.with_memory_space_constraint(x, pltpu.HBM)


def cost(flops, moved):
    return pl.CostEstimate(flops=flops, bytes_accessed=moved, transcendentals=0)


def first_block(maps, child, here_col):
    place, found = jnp.int32(0), jnp.int32(0)
    for d in range(5):
        hit = (maps[child, d * 16 + here_col] // 16 == 0).astype(jnp.int32)
        place, found = place + d * hit, found + hit
    return place, found


def prepare_kernel(
    maps, pivots, front, pieces, first, rest_a, rest_b, rest_c, rest_d, rest_e, panel, own, away, table,
    sending, kept, total, sem,
):
    here_row, here_col = lax.axis_index("row"), lax.axis_index("col")
    side, core = here_row // 4, here_row % 2
    other = 1 - side
    place, found = first_block(maps, side, here_col)
    got_place, _ = first_block(maps, other, here_col)

    def columns(d):
        return pl.ds(pl.multiple_of(d * BLK, BLK), BLK)

    reads = [
        pltpu.make_async_copy(pieces.at[:, other], sending, sem.at[0]),
        pltpu.make_async_copy(pieces.at[:, side, :, columns(place)], kept, sem.at[1]),
        pltpu.make_async_copy(front.at[:, pl.ds(0, BLK)], panel, sem.at[2]),
    ]
    writes = []
    targets = (0, 0, rest_a), (1, 0, rest_b), (1, 5, rest_c), (2, 0, rest_d), (3, 0, rest_e)
    for n, (j, start, target) in enumerate(targets):
        d = j + (j >= place).astype(jnp.int32)
        source = sending.at[pl.ds(start, target.shape[0]), :, columns(d)]
        writes.append(pltpu.make_async_copy(source, target, sem.at[3 + n]))
    for copy in reads:
        copy.start()
    for kk in range(16):
        table[KEPT_AT + kk] = -1
        table[GOT_AT + kk] = -1
    for m in range(10):
        table[KEPT_AT + maps[side, m * 8 + here_row] // 8] = m
        target = maps[other, m * 8 + here_row] // 8
        table[GOT_AT + target] = m
        table[GOT_ROW + m] = target
    for d in range(5):
        table[KEPT_COL + d] = maps[side, d * 16 + here_col] // 16
    table[GOT_COL] = maps[other, got_place * 16 + here_col] // 16
    for j in range(4):
        d = j + (j >= got_place).astype(jnp.int32)
        table[GOT_COL + 1 + j] = maps[other, d * 16 + here_col] // 16
    table[ROW] = here_row
    table[COL] = here_col
    table[SIDE] = side
    turned = pivots[...].T
    wanted = jnp.concatenate(
        [jnp.where(here_col < 4, turned[:, 4 + k : 5 + k], turned[:, k : k + 1]) for k in range(4)],
        axis=0,
    )
    block, offset = wanted >> 7, wanted & 127
    mine = jnp.where((block & 7) == here_row, (block >> 3) * BLK + offset, -1)
    sent = jnp.full_like(mine, -1)
    for m in range(10):
        hit = (block == maps[side, m * 8 + (here_row ^ 4)]) & (found > 0)
        sent = jnp.where(hit, m * BLK + offset, sent)
    reads[0].wait()
    for copy in writes:
        copy.start()
    first[...] = sending[:, :, columns(place)]
    reads[1].wait()
    reads[2].wait()

    @pl.when(found > 0)
    def _():
        for m in range(10):
            at = pl.multiple_of(maps[side, m * 8 + here_row] // 8 * BLK, BLK)
            panel[pl.ds(at, BLK), :] += kept[m]

    def rows_of(index, values, base):
        lane = lax.broadcasted_iota(jnp.int32, (PANEL, values.shape[0]), 1) + base
        chosen = jnp.where(lane == index, 1.0, 0.0).astype(BF16)
        both = jnp.concatenate(split(values), axis=1)
        return jnp.dot(chosen, both, preferred_element_type=F32)

    terms = jnp.zeros((PANEL, 2 * BLK), F32)
    for k in range(8):
        terms += rows_of(mine, panel[k * 256 : (k + 1) * 256, :], k * 256)
    for k in range(5):
        values = first[2 * k : 2 * k + 2].reshape(256, BLK)
        terms += rows_of(sent, values, k * 256)
    total[...] = terms[:, :BLK] + terms[:, BLK:]
    own[...] = total[pl.ds(pl.multiple_of(core * 256, 256), 256), :]
    away[...] = total[pl.ds(pl.multiple_of((1 - core) * 256, 256), 256), :]
    for copy in writes:
        copy.wait()


def prepare(maps, pivots, front, pieces):
    column = jax.ShapeDtypeStruct((10, BLK, BLK), F32)
    half = jax.ShapeDtypeStruct((5, BLK, BLK), F32)
    return pl.pallas_call(
        prepare_kernel,
        out_shape=[
            column,
            column,
            half,
            half,
            column,
            column,
            jax.ShapeDtypeStruct((2048, BLK), F32),
            jax.ShapeDtypeStruct((256, BLK), F32),
            jax.ShapeDtypeStruct((256, BLK), F32),
            jax.ShapeDtypeStruct((64,), jnp.int32),
        ],
        in_specs=[SMEM, VMEM, HBM, HBM],
        out_specs=[VMEM, HBM, HBM, HBM, HBM, HBM, VMEM, VMEM, VMEM, SMEM],
        scratch_shapes=[
            pltpu.VMEM((10, BLK, 640), F32),
            pltpu.VMEM((10, BLK, BLK), F32),
            pltpu.VMEM((PANEL, BLK), F32),
            pltpu.SemaphoreType.DMA((8,)),
        ],
        compiler_params=params(24),
        cost_estimate=cost(0, 9 * MIB),
        name="prepare",
    )(in_hbm(maps), in_hbm(pivots.reshape(8, BLK)), in_hbm(front), in_hbm(pieces))


def pivot_kernel(mine_half, maps, pivots, front, children, *refs):
    rows, marks, front_list, spread, inverse, child_list, sem, child_sem = refs[-8:]
    rows[...] = jnp.zeros_like(rows)
    marks[...] = refs[0][...] if mine_half else jnp.zeros_like(marks)
    here_row, here_col = lax.axis_index("row"), lax.axis_index("col")
    side, quarter, core = here_row // 4, here_row % 4, here_row % 2
    half = core if mine_half else 1 - core
    spread[...] = jnp.zeros_like(spread)

    def clear(b, carry):
        inverse[b] = -1
        return carry

    lax.fori_loop(0, 128, clear, 0, unroll=16)
    for k in range(20):
        inverse[maps[side, 4 * k + quarter]] = k

    def visit(p, counts):
        pivot = pivots[half * PANEL + p]
        block, offset = pivot >> 7, pivot & 127
        child_block = inverse[block]
        mine = (block & 7) == here_row
        shared = ((block & 3) == quarter) & (child_block >= 0)
        front_list[counts[0]] = (((block >> 3) * BLK + offset) << 9) | p
        child_list[counts[1]] = ((child_block * BLK + offset) << 9) | p
        return counts[0] + mine.astype(jnp.int32), counts[1] + shared.astype(jnp.int32)

    counts = lax.fori_loop(0, PANEL, visit, (jnp.int32(0), jnp.int32(0)), unroll=8)
    front_list[PANEL] = counts[0]
    mark = jnp.full((1, BLK), half + 1, jnp.int32).astype(F32)

    def take_front(n, carry):
        at, p = front_list[n] >> 9, front_list[n] & 511
        pltpu.make_async_copy(front.at[pl.ds(at, 1), :], rows.at[pl.ds(p, 1), :], sem).start()
        marks[pl.ds(at, 1), :] = mark
        return carry

    def take_child(n, carry):
        at, p = child_list[n] >> 9, child_list[n] & 511
        pltpu.make_async_copy(
            children.at[pl.ds(at, 1), :], spread.at[pl.ds(p, 1), :], child_sem
        ).start()
        return carry

    def wait(source, target, semaphore, count):
        def some(size):
            def body(_, carry):
                pltpu.make_async_copy(
                    source.at[pl.ds(0, size), :], target.at[pl.ds(0, size), :], semaphore
                ).wait()
                return carry

            return body

        lax.fori_loop(0, count // 16, some(16), 0)
        lax.fori_loop(0, count % 16, some(1), 0)

    lax.fori_loop(0, counts[0], take_front, 0)
    lax.fori_loop(0, counts[1], take_child, 0)
    wait(front, rows, sem, counts[0])
    wait(children, spread, child_sem, counts[1])
    for d in range(5):
        to = pl.ds(pl.multiple_of(maps[side, d * 16 + here_col] // 16 * BLK, BLK), BLK)
        rows[:, to] += spread[:, d * BLK : (d + 1) * BLK]


def pivot_terms(maps, pivots, front, children, *before):
    mine_half = len(before) > 0
    return pl.pallas_call(
        functools.partial(pivot_kernel, mine_half),
        out_shape=[
            jax.ShapeDtypeStruct((PANEL, 1024), F32),
            jax.ShapeDtypeStruct((2048, BLK), F32),
            jax.ShapeDtypeStruct((PANEL + 1,), jnp.int32),
        ],
        in_specs=[SMEM, SMEM, HBM, HBM] + [VMEM] * len(before),
        out_specs=[VMEM, VMEM, SMEM],
        scratch_shapes=[
            pltpu.VMEM((PANEL, 640), F32),
            pltpu.SMEM((128,), jnp.int32),
            pltpu.SMEM((PANEL + 1,), jnp.int32),
            pltpu.SemaphoreType.DMA(()),
            pltpu.SemaphoreType.DMA(()),
        ],
        compiler_params=params(12),
        cost_estimate=cost(0, 24 * MIB),
        name="pivot_terms_mine" if mine_half else "pivot_terms_other",
    )(in_hbm(maps), in_hbm(pivots), in_hbm(front), in_hbm(children), *before)


def panel_kernel(table, panel, got, top, bottom):
    top[...] = panel[:1024, :]
    bottom[...] = panel[1024:, :]

    @pl.when(table[GOT_COL] == 0)
    def _():
        for kk in range(16):
            m = table[GOT_AT + kk]
            half = top if kk < 8 else bottom
            at = kk % 8 * BLK

            @pl.when(m >= 0)
            def _(half=half, at=at, m=m):
                half[at : at + BLK, :] += got[m]


def whole_panel(table, panel, got):
    shape = jax.ShapeDtypeStruct((1024, BLK), F32)
    return pl.pallas_call(
        panel_kernel,
        out_shape=[shape, shape],
        in_specs=[SMEM, VMEM, VMEM],
        out_specs=[VMEM, VMEM],
        compiler_params=params(12),
        cost_estimate=cost(0, 3 * MIB),
        name="whole_panel",
    )(table, panel, got)


def flips(delta):
    return (delta & 1) ^ (delta >> 1), delta >> 1


def corner_kernel(table, own, swapped, inverses, factor_h, factor_l, cross):
    here_row, here_col = table[ROW], table[COL]
    core, x, y = here_row % 2, here_col % 4, here_col // 4
    mine = (y ^ (y >> 1)) & 1

    def corner(panel, half):
        blocks = []
        for xx in range(4):
            one, three = flips(xx ^ x)
            pair = mine ^ panel
            slot = jnp.where(half == 0, pair | (one << 1) | (three << 2), one | (three << 1) | (pair << 2))
            blocks.append(jnp.where(core == half, own[slot], swapped[slot]))
        return jnp.concatenate(blocks, axis=1)

    for p in range(2):
        factor_h[p], factor_l[p] = split(inverses[p])
    for half in range(2):
        rows = slice(half * 256, (half + 1) * 256)
        factor_h[2, rows, :], factor_l[2, rows, :] = split(corner(1, half))
        cross[rows, :] = dot3(split(corner(0, half)), (factor_h[0], factor_l[0]))


def corners(table, own, swapped, inverses):
    return pl.pallas_call(
        corner_kernel,
        out_shape=[
            jax.ShapeDtypeStruct((3, PANEL, PANEL), BF16),
            jax.ShapeDtypeStruct((3, PANEL, PANEL), BF16),
            jax.ShapeDtypeStruct((PANEL, PANEL), F32),
        ],
        in_specs=[SMEM, VMEM, VMEM, VMEM],
        out_specs=[VMEM] * 3,
        compiler_params=params(20),
        cost_estimate=cost(6 * PANEL**3, 8 * MIB),
        name="corners",
    )(table, own, swapped, inverses)


def factor_kernel(table, own, swapped, factor_h, factor_l, cross, high, low, patch):
    here_row, col = table[ROW], table[COL]
    core, slot = here_row % 2, col % 4
    inside = lax.broadcasted_iota(jnp.int32, (PANEL, 1024), 1) < BLK

    def mine(x):
        out = x[:, :BLK]
        for s in range(1, 4):
            out = jnp.where(slot == s, x[:, s * BLK : (s + 1) * BLK], out)
        return out

    def begin_with(block, x):
        return jnp.concatenate([block, x[:, BLK:]], axis=1)

    def factor(n):
        return factor_h[n], factor_l[n]

    def factor_columns(n):
        return mine(factor_h[n].astype(F32)) + mine(factor_l[n].astype(F32))

    first = jnp.where(core == 0, own[...], swapped[...])
    first = jnp.where(inside & (col < 4), 0.0, first)
    second = jnp.where(core == 0, swapped[...], own[...])
    second = second - dot3(split(cross[...]), split(first))
    patch[...] = begin_with(jnp.where(col < 4, mine(cross[...]), second[:, :BLK]), second)
    second = jnp.where(inside & (col < 8), 0.0, second)
    right = dot3(factor(1), split(second))
    in_second = (col >= 4) & (col < 8)
    right = begin_with(jnp.where(in_second, factor_columns(1), right[:, :BLK]), right)
    terms = split(right)
    high[PANEL:], low[PANEL:] = terms
    first = jnp.where(inside & (col < 8), 0.0, first)
    left = dot3(factor(0), split(first - dot3(factor(2), terms)))
    left = begin_with(jnp.where(col < 4, factor_columns(0), left[:, :BLK]), left)
    high[:PANEL], low[:PANEL] = split(left)


def right_factor(table, own, swapped, factors, cross):
    shape = jax.ShapeDtypeStruct((1024, 1024), BF16)
    return pl.pallas_call(
        factor_kernel,
        out_shape=[shape, shape, jax.ShapeDtypeStruct((PANEL, 1024), F32)],
        in_specs=[SMEM] + [VMEM] * 5,
        out_specs=[VMEM] * 3,
        compiler_params=params(34),
        cost_estimate=cost(4 * 6 * PANEL * PANEL * 1024, 14 * MIB),
        name="right_factor",
    )(table, own, swapped, *factors, cross)


def block_at(base, half, t, s):
    return jnp.maximum(s[base + half * 8 + t], 0)


def extend_kernel(columns, table, front, *refs):
    out, refs = refs[-1], refs[:-1]
    kept, *got = (refs[2 * k : 2 * k + 2] for k in range(1 + columns))
    step = pl.program_id(0)
    out[...] = front[...]
    for half in range(2):

        @pl.when(table[KEPT_AT + half * 8 + step] >= 0)
        def _(half=half):
            for d in range(5):
                to = pl.ds(pl.multiple_of(table[KEPT_COL + d] * BLK, BLK), BLK)
                out[half, :, to] += kept[half][0, 0, :, d * BLK : (d + 1) * BLK]

        @pl.when(table[GOT_AT + half * 8 + step] >= 0)
        def _(half=half):
            for j in range(columns):
                to = pl.ds(pl.multiple_of(table[GOT_COL + j] * BLK, BLK), BLK)
                out[half, :, to] += got[j][half][0]


def extend(table, front, pieces, got):
    def kept_at(half):
        return lambda t, s: (block_at(KEPT_AT, half, t, s), s[SIDE], 0, 0)

    def got_at(half):
        return lambda t, s: (block_at(GOT_AT, half, t, s), 0, 0)

    tile = pl.BlockSpec((2, BLK, 1024), lambda t, s: (0, t, 0))
    kept_specs = [pl.BlockSpec((1, 1, BLK, 640), kept_at(half)) for half in range(2)]
    got_specs = [pl.BlockSpec((1, BLK, BLK), got_at(half)) for half in range(2)]
    return pl.pallas_call(
        functools.partial(extend_kernel, len(got)),
        out_shape=pltpu.HBM((2, 1024, 1024), F32),
        grid_spec=pltpu.PrefetchScalarGridSpec(
            num_scalar_prefetch=1,
            grid=(8,),
            in_specs=[tile, *kept_specs, *got_specs * len(got)],
            out_specs=tile,
        ),
        compiler_params=params(20),
        cost_estimate=cost(0, 22 * MIB),
        name="extend",
    )(table, in_hbm(front.reshape(2, 1024, 1024)), *[in_hbm(pieces)] * 2, *[g for g in got for _ in range(2)])


ORDERS = ((1, 3, 4, 12), (3, 1, 12, 4)), ((4, 12, 1, 3), (12, 4, 3, 1))


def update_kernel(table, front, *refs):
    blocks = refs[:4], refs[4:8]
    right_h, right_l, marks, out, panels = refs[8:]
    step = pl.program_id(0)
    col, core = table[COL], table[ROW] % 2

    def assemble(which):
        held, came, held_far, came_far = blocks[which]
        for c in range(16):
            one_x, three_x = flips((c ^ col) & 3)
            one_y, three_y = flips((c ^ col) >> 2)
            bits = {1: one_x, 3: three_x, 4: one_y, 12: three_y}
            even, odd = (ORDERS[q][which] for q in range(2))
            flip = [jnp.where(core == 0, bits[e], bits[o]) for e, o in zip(even, odd)]
            slot = flip[0] | (flip[1] << 1)
            later, far = flip[2] == 1, flip[3] == 1
            near_block = jnp.where(later, came[slot], held[slot])
            far_block = jnp.where(later, came_far[slot], held_far[slot])
            block = jnp.where(far, far_block, near_block)
            y, x = c // 4, c % 4
            rows = slice(0, 256) if y < 2 else slice(256, PANEL)
            first = min(y, 3 - y) * PANEL + x * BLK
            columns = slice(first, first + BLK)
            panels[0, rows, columns], panels[1, rows, columns] = split(block)

    for which in range(2):
        pl.when(step // 2 == which)(functools.partial(assemble, which))

    change = dot3((panels[0], panels[1]), (right_h[...], right_l[...])).reshape(2, 256, 1024)
    active = marks[...] == 0
    for j in range(8):
        columns = slice(j * BLK, (j + 1) * BLK)
        before, part = front[:, :, columns], change[:, :, columns]
        after = before - part
        if j == 0:
            after = jnp.where(col < 8, part, after)
        out[:, :, columns] = jnp.where(active, after, before)


def update(table, front, blocks, right, marks):
    def whole(x):
        return pl.BlockSpec(x.shape, lambda t, s: (0,) * x.ndim, pipeline_mode=pl.Buffered(1))

    first = pl.BlockSpec((4, 256, BLK), lambda t, s: (0, jnp.minimum(t, 1), 0))
    second = pl.BlockSpec((4, 256, BLK), lambda t, s: (0, jnp.maximum(t - 2, 0), 0))
    tile = pl.BlockSpec((2, 256, 1024), lambda t, s: (0, t, 0))
    return pl.pallas_call(
        update_kernel,
        out_shape=pltpu.HBM((2, 1024, 1024), F32),
        grid_spec=pltpu.PrefetchScalarGridSpec(
            num_scalar_prefetch=1,
            grid=(4,),
            in_specs=[
                tile,
                *[first] * 4,
                *[second] * 4,
                *[whole(x) for x in right],
                pl.BlockSpec((2, 256, BLK), lambda t, s: (0, t, 0)),
            ],
            out_specs=tile,
            scratch_shapes=[pltpu.VMEM((2, PANEL, 1024), BF16)],
        ),
        compiler_params=params(34),
        cost_estimate=cost(6 * 2048 * 1024 * 1024, 32 * MIB),
        name="update",
    )(table, in_hbm(front), *blocks[0], *blocks[1], *right, marks.reshape(2, 1024, BLK))


def finish_kernel(
    table, list_other, list_mine, front, got_b, got_c, got_d, got_e, patch,
    out, held, read_sem, write_sem, sem,
):
    del front
    core = table[ROW] % 2
    copies = []
    for n, (column, first, got) in enumerate(
        [(2, 0, got_b), (2, 5, got_c), (3, 0, got_d), (4, 0, got_e)]
    ):
        columns = pl.ds(pl.multiple_of(table[GOT_COL + column] * BLK, BLK), BLK)
        for m in range(got.shape[0]):
            rows = pl.ds(pl.multiple_of(table[GOT_ROW + first + m] * BLK, BLK), BLK)
            there, here = out.at[rows, columns], held.at[n, m]
            read = pltpu.make_async_copy(there, here, read_sem.at[n, m])
            write = pltpu.make_async_copy(here, there, write_sem.at[n, m])
            copies.append((read, write, n, m, got))
    for read, *_ in copies:
        read.start()
    for read, write, n, m, got in copies:
        read.wait()
        held[n, m] += got[m]
        write.start()
    for _, write, *_ in copies:
        write.wait()

    def entry(n):
        return jnp.where(core == 0, list_other[n], list_mine[n])

    def place(n, carry):
        at, p = entry(n) >> 9, entry(n) & 511
        pltpu.make_async_copy(patch.at[pl.ds(p, 1), :], out.at[pl.ds(at, 1), :], sem).start()
        return carry

    def wait(_, carry):
        pltpu.make_async_copy(patch.at[pl.ds(0, 1), :], out.at[pl.ds(0, 1), :], sem).wait()
        return carry

    lax.fori_loop(0, entry(PANEL), place, 0)
    lax.fori_loop(0, entry(PANEL), wait, 0)


def finish(table, lists, front, got, patch):
    return pl.pallas_call(
        finish_kernel,
        out_shape=jax.ShapeDtypeStruct((2048, 1024), F32),
        in_specs=[SMEM, SMEM, SMEM, HBM] + [VMEM] * 5,
        out_specs=HBM,
        scratch_shapes=[
            pltpu.VMEM((4, 10, BLK, BLK), F32),
            pltpu.SemaphoreType.DMA((4, 10)),
            pltpu.SemaphoreType.DMA((4, 10)),
            pltpu.SemaphoreType.DMA(()),
        ],
        input_output_aliases={3: 0},
        compiler_params=params(12),
        cost_estimate=cost(0, 8 * MIB),
        name="finish",
    )(table, *lists, front, *got, patch)


def swap(block, axis, partner):
    count = lax.axis_size(axis)
    return lax.ppermute(block, axis, [(i, partner(i)) for i in range(count)])


def fold(block, near):
    came = lax.ppermute(block[1], "col", [(c, c ^ 12) for c in range(8)])
    return jnp.where(near, block[0], came)


def local(front, children, child_maps, pivots, diag_inverses):
    here_row, here_col = lax.axis_index("row"), lax.axis_index("col")
    chip = here_row >> 1
    together = lax.optimization_barrier
    pieces = children.reshape(10, 2, BLK, 640)

    def by_row(block, mask):
        return swap(block, "row", lambda i: i ^ mask)

    def by_col(block, mask):
        return swap(block, "col", lambda i: i ^ mask)

    bits = (chip ^ (chip >> 1)) & 1, chip >> 1
    rings = [[(r, r ^ ((2, 6), (6, 2))[r % 2][k]) for r in range(8)] for k in range(2)]
    low = [jnp.where(here_row & 1 == 0, bits[k], bits[1 - k]) == 0 for k in range(2)]
    pivots, near, low = together((pivots, here_col < 8, low))

    def halve(part, step):
        size = part.shape[0] // 2
        leave = jnp.where(low[step], part[size:], part[:size])
        stay = jnp.where(low[step], part[:size], part[size:])
        return stay + lax.ppermute(leave, "row", rings[step])

    def double(part, step):
        came = lax.ppermute(part, "row", rings[step])
        first, second = jnp.where(low[step], part, came), jnp.where(low[step], came, part)
        return jnp.concatenate([first, second], axis=0)

    def gather_step(block, which, step):
        route = [
            (r * 16 + c, r * 16 + (c ^ ORDERS[r % 2][which][step]))
            for r in range(8)
            for c in range(16)
        ]
        return lax.ppermute(block, ("row", "col"), route)

    first, rest_a, rest_b, rest_c, rest_d, rest_e, panel, corner, away, table = prepare(
        child_maps, pivots, front, pieces
    )
    got0 = by_row(first, 4)
    corner = corner + by_row(away, 1)
    for k in range(2):
        corner = corner + lax.ppermute(corner, "row", rings[k])
    away_rows, marks, list_other = pivot_terms(child_maps, pivots, front, children)
    got0, away_rows, rest_a, marks, corner = together((got0, away_rows, rest_a, marks, corner))

    top, bottom = whole_panel(table, panel, got0)
    mine = fold((top, bottom), near)
    corner = fold((corner, corner), near)[None]
    got_a = by_row(rest_a, 4)
    own_rows, marks, list_mine = pivot_terms(child_maps, pivots, front, children, marks)
    total = own_rows + by_row(away_rows, 1)
    mine, corner, total, got_a, rest_b = together((mine, corner, total, got_a, rest_b))

    def corner_step(block, step):
        masks = ((4, 1, 3), (1, 3, 4))
        route = [
            (r * 16 + c, r * 16 + (c ^ masks[r % 2][step])) for r in range(8) for c in range(16)
        ]
        return jnp.concatenate([block, lax.ppermute(block, ("row", "col"), route)], axis=0)

    held = [mine[None, :PANEL], mine[None, PANEL:]]
    for k in range(2):
        came = [gather_step(held[w], w, k) for w in range(2)]
        held = [jnp.concatenate([h, c], axis=0) for h, c in zip(held, came)]
        corner = corner_step(corner, k)
        total = halve(total, k)
        if k == 0:
            held, corner, total, rest_b = together((held, corner, total, rest_b))
            got_b = by_row(rest_b, 4)
        else:
            held, corner, total, got_b, rest_c = together((held, corner, total, got_b, rest_c))
    came = [gather_step(held[w], w, 2) for w in range(2)]
    corner = corner_step(corner, 2)
    total = double(total, 1)
    got_c = by_row(rest_c, 4)
    came, corner, total, got_c = together((came, corner, total, got_c))
    held_far = [gather_step(held[w], w, 3) for w in range(2)]
    *factors, cross = corners(table, corner, by_row(corner, 1), diag_inverses)
    total = double(total, 0)
    front = extend(table, front, pieces, (got0, got_a))
    came, held_far, total, rest_d, factors, cross, front = together(
        (came, held_far, total, rest_d, factors, cross, front)
    )
    came_far = [gather_step(came[w], w, 3) for w in range(2)]
    got_d = by_row(rest_d, 4)
    *right, patch = right_factor(table, total, by_row(total, 1), factors, cross)
    came_far, got_d, rest_e, right, patch = together((came_far, got_d, rest_e, right, patch))
    got_e = by_row(rest_e, 4)
    blocks = [(held[w], came[w], held_far[w], came_far[w]) for w in range(2)]
    front = update(table, front, blocks, right, marks).reshape(2048, 1024)
    return finish(table, (list_other, list_mine), front, (got_b, got_c, got_d, got_e), patch)


def solution(mesh):
    return jax.shard_map(
        local,
        mesh=mesh,
        in_specs=(P("row", "col"), P("row", "col"), P(), P(), P()),
        out_specs=P("row", "col"),
        check_vma=False,
    )
```

```python
import functools

import jax
import jax.numpy as jnp
from jax import lax
from jax.experimental import pallas as pl
from jax.experimental.pallas import tpu as pltpu
from jax.sharding import PartitionSpec as P

BLK = 128
PANEL = 512
MIB = 1 << 20
F32 = jnp.float32
BF16 = jnp.bfloat16
SMEM = pl.BlockSpec(memory_space=pltpu.SMEM)
VMEM = pl.BlockSpec(memory_space=pltpu.VMEM)
HBM = pl.BlockSpec(memory_space=pltpu.HBM)
KEPT_AT = 0
GOT_AT = 16
KEPT_COL = 32
GOT_COL = 40
ROW, COL, SIDE = 48, 49, 50
GOT_ROW = 52


def split(x):
    high = x.astype(BF16)
    return high, (x - high.astype(F32)).astype(BF16)


def dot3(a, b):
    rows = a[0].shape[0]
    both = jnp.dot(jnp.concatenate(a, axis=0), b[0], preferred_element_type=F32)
    return both[:rows] + (both[rows:] + jnp.dot(a[0], b[1], preferred_element_type=F32))


def params(mib):
    return pltpu.CompilerParams(vmem_limit_bytes=mib * MIB)


def in_hbm(x):
    return pltpu.with_memory_space_constraint(x, pltpu.HBM)


def cost(flops, moved):
    return pl.CostEstimate(flops=flops, bytes_accessed=moved, transcendentals=0)


def first_block(maps, child, here_col):
    place, found = jnp.int32(0), jnp.int32(0)
    for d in range(5):
        hit = (maps[child, d * 16 + here_col] // 16 == 0).astype(jnp.int32)
        place, found = place + d * hit, found + hit
    return place, found


def cut_kernel(maps, pieces, first, sem):
    other = 1 - lax.axis_index("row") // 4
    place, _ = first_block(maps, 1 - other, lax.axis_index("col"))
    columns = pl.ds(pl.multiple_of(place * BLK, BLK), BLK)
    copy = pltpu.make_async_copy(pieces.at[:, other, :, columns], first, sem)
    copy.start()
    copy.wait()


def cut(maps, pieces):
    return pl.pallas_call(
        cut_kernel,
        out_shape=jax.ShapeDtypeStruct((10, BLK, BLK), F32),
        in_specs=[SMEM, HBM],
        out_specs=VMEM,
        scratch_shapes=[pltpu.SemaphoreType.DMA(())],
        compiler_params=params(4),
        cost_estimate=cost(0, MIB),
        name="cut",
    )(in_hbm(maps), in_hbm(pieces))


def prepare_kernel(
    maps, pivots, front, pieces, first, *refs,
):
    *rests, panel, own, away, table, sending, kept, total, sem = refs
    here_row, here_col = lax.axis_index("row"), lax.axis_index("col")
    side, core = here_row // 4, here_row % 2
    other = 1 - side
    place, found = first_block(maps, side, here_col)
    got_place, _ = first_block(maps, other, here_col)

    def columns(d):
        return pl.ds(pl.multiple_of(d * BLK, BLK), BLK)

    reads = [
        pltpu.make_async_copy(pieces.at[:, other], sending, sem.at[0]),
        pltpu.make_async_copy(pieces.at[:, side, :, columns(place)], kept, sem.at[1]),
        pltpu.make_async_copy(front.at[:, pl.ds(0, BLK)], panel, sem.at[2]),
    ]
    writes = []
    places = (0, 0), (1, 0), (1, 5), (2, 0), (2, 5), (3, 0)
    for n, ((j, start), target) in enumerate(zip(places, rests)):
        d = j + (j >= place).astype(jnp.int32)
        source = sending.at[pl.ds(start, target.shape[0]), :, columns(d)]
        writes.append(pltpu.make_async_copy(source, target, sem.at[3 + n]))
    for copy in reads:
        copy.start()
    for kk in range(16):
        table[KEPT_AT + kk] = -1
        table[GOT_AT + kk] = -1
    for m in range(10):
        table[KEPT_AT + maps[side, m * 8 + here_row] // 8] = m
        target = maps[other, m * 8 + here_row] // 8
        table[GOT_AT + target] = m
        table[GOT_ROW + m] = target
    for d in range(5):
        table[KEPT_COL + d] = maps[side, d * 16 + here_col] // 16
    table[GOT_COL] = maps[other, got_place * 16 + here_col] // 16
    for j in range(4):
        d = j + (j >= got_place).astype(jnp.int32)
        table[GOT_COL + 1 + j] = maps[other, d * 16 + here_col] // 16
    table[ROW] = here_row
    table[COL] = here_col
    table[SIDE] = side
    turned = pivots[...].T
    wanted = jnp.concatenate(
        [jnp.where(here_col < 4, turned[:, 4 + k : 5 + k], turned[:, k : k + 1]) for k in range(4)],
        axis=0,
    )
    block, offset = wanted >> 7, wanted & 127
    mine = jnp.where((block & 7) == here_row, (block >> 3) * BLK + offset, -1)
    sent = jnp.full_like(mine, -1)
    for m in range(10):
        hit = (block == maps[side, m * 8 + (here_row ^ 4)]) & (found > 0)
        sent = jnp.where(hit, m * BLK + offset, sent)
    reads[0].wait()
    for copy in writes:
        copy.start()
    reads[1].wait()
    reads[2].wait()

    @pl.when(found > 0)
    def _():
        for m in range(10):
            at = pl.multiple_of(maps[side, m * 8 + here_row] // 8 * BLK, BLK)
            panel[pl.ds(at, BLK), :] += kept[m]

    def rows_of(index, values, base):
        lane = lax.broadcasted_iota(jnp.int32, (PANEL, values.shape[0]), 1) + base
        chosen = jnp.where(lane == index, 1.0, 0.0).astype(BF16)
        both = jnp.concatenate(split(values), axis=1)
        return jnp.dot(chosen, both, preferred_element_type=F32)

    terms = jnp.zeros((PANEL, 2 * BLK), F32)
    for k in range(8):
        terms += rows_of(mine, panel[k * 256 : (k + 1) * 256, :], k * 256)
    for k in range(5):
        values = first[2 * k : 2 * k + 2].reshape(256, BLK)
        terms += rows_of(sent, values, k * 256)
    total[...] = terms[:, :BLK] + terms[:, BLK:]
    own[...] = total[pl.ds(pl.multiple_of(core * 256, 256), 256), :]
    away[...] = total[pl.ds(pl.multiple_of((1 - core) * 256, 256), 256), :]
    for copy in writes:
        copy.wait()


def prepare(maps, pivots, front, pieces, first):
    column = jax.ShapeDtypeStruct((10, BLK, BLK), F32)
    half = jax.ShapeDtypeStruct((5, BLK, BLK), F32)
    return pl.pallas_call(
        prepare_kernel,
        out_shape=[
            column,
            half,
            half,
            half,
            half,
            column,
            jax.ShapeDtypeStruct((2048, BLK), F32),
            jax.ShapeDtypeStruct((256, BLK), F32),
            jax.ShapeDtypeStruct((256, BLK), F32),
            jax.ShapeDtypeStruct((64,), jnp.int32),
        ],
        in_specs=[SMEM, VMEM, HBM, HBM, VMEM],
        out_specs=[HBM] * 6 + [VMEM, VMEM, VMEM, SMEM],
        scratch_shapes=[
            pltpu.VMEM((10, BLK, 640), F32),
            pltpu.VMEM((10, BLK, BLK), F32),
            pltpu.VMEM((PANEL, BLK), F32),
            pltpu.SemaphoreType.DMA((9,)),
        ],
        compiler_params=params(24),
        cost_estimate=cost(0, 9 * MIB),
        name="prepare",
    )(in_hbm(maps), in_hbm(pivots.reshape(8, BLK)), in_hbm(front), in_hbm(pieces), first)


def pivot_kernel(mine_half, maps, pivots, front, children, *refs):
    rows, marks, front_list, spread, inverse, child_list, sem, child_sem = refs[-8:]
    rows[...] = jnp.zeros_like(rows)
    marks[...] = refs[0][...] if mine_half else jnp.zeros_like(marks)
    here_row, here_col = lax.axis_index("row"), lax.axis_index("col")
    side, quarter, core = here_row // 4, here_row % 4, here_row % 2
    half = core if mine_half else 1 - core
    spread[...] = jnp.zeros_like(spread)

    def clear(b, carry):
        inverse[b] = -1
        return carry

    lax.fori_loop(0, 128, clear, 0, unroll=16)
    for k in range(20):
        inverse[maps[side, 4 * k + quarter]] = k

    def visit(p, counts):
        pivot = pivots[half * PANEL + p]
        block, offset = pivot >> 7, pivot & 127
        child_block = inverse[block]
        mine = (block & 7) == here_row
        shared = ((block & 3) == quarter) & (child_block >= 0)
        front_list[counts[0]] = (((block >> 3) * BLK + offset) << 9) | p
        child_list[counts[1]] = ((child_block * BLK + offset) << 9) | p
        return counts[0] + mine.astype(jnp.int32), counts[1] + shared.astype(jnp.int32)

    counts = lax.fori_loop(0, PANEL, visit, (jnp.int32(0), jnp.int32(0)), unroll=8)
    front_list[PANEL] = counts[0]
    mark = jnp.full((1, BLK), half + 1, jnp.int32).astype(F32)

    def take_front(n, carry):
        at, p = front_list[n] >> 9, front_list[n] & 511
        pltpu.make_async_copy(front.at[pl.ds(at, 1), :], rows.at[pl.ds(p, 1), :], sem).start()
        marks[pl.ds(at, 1), :] = mark
        return carry

    def take_child(n, carry):
        at, p = child_list[n] >> 9, child_list[n] & 511
        pltpu.make_async_copy(
            children.at[pl.ds(at, 1), :], spread.at[pl.ds(p, 1), :], child_sem
        ).start()
        return carry

    def wait(source, target, semaphore, count):
        def some(size):
            def body(_, carry):
                pltpu.make_async_copy(
                    source.at[pl.ds(0, size), :], target.at[pl.ds(0, size), :], semaphore
                ).wait()
                return carry

            return body

        lax.fori_loop(0, count // 16, some(16), 0)
        lax.fori_loop(0, count % 16, some(1), 0)

    lax.fori_loop(0, counts[0], take_front, 0)
    lax.fori_loop(0, counts[1], take_child, 0)
    wait(front, rows, sem, counts[0])
    wait(children, spread, child_sem, counts[1])
    for d in range(5):
        to = pl.ds(pl.multiple_of(maps[side, d * 16 + here_col] // 16 * BLK, BLK), BLK)
        rows[:, to] += spread[:, d * BLK : (d + 1) * BLK]


def pivot_terms(maps, pivots, front, children, *before):
    mine_half = len(before) > 0
    return pl.pallas_call(
        functools.partial(pivot_kernel, mine_half),
        out_shape=[
            jax.ShapeDtypeStruct((PANEL, 1024), F32),
            jax.ShapeDtypeStruct((2048, BLK), F32),
            jax.ShapeDtypeStruct((PANEL + 1,), jnp.int32),
        ],
        in_specs=[SMEM, SMEM, HBM, HBM] + [VMEM] * len(before),
        out_specs=[VMEM, VMEM, SMEM],
        scratch_shapes=[
            pltpu.VMEM((PANEL, 640), F32),
            pltpu.SMEM((128,), jnp.int32),
            pltpu.SMEM((PANEL + 1,), jnp.int32),
            pltpu.SemaphoreType.DMA(()),
            pltpu.SemaphoreType.DMA(()),
        ],
        compiler_params=params(12),
        cost_estimate=cost(0, 24 * MIB),
        name="pivot_terms_mine" if mine_half else "pivot_terms_other",
    )(in_hbm(maps), in_hbm(pivots), in_hbm(front), in_hbm(children), *before)


def panel_kernel(table, panel, got, top, bottom):
    top[...] = panel[:1024, :]
    bottom[...] = panel[1024:, :]

    @pl.when(table[GOT_COL] == 0)
    def _():
        for kk in range(16):
            m = table[GOT_AT + kk]
            half = top if kk < 8 else bottom
            at = kk % 8 * BLK

            @pl.when(m >= 0)
            def _(half=half, at=at, m=m):
                half[at : at + BLK, :] += got[m]


def whole_panel(table, panel, got):
    shape = jax.ShapeDtypeStruct((1024, BLK), F32)
    return pl.pallas_call(
        panel_kernel,
        out_shape=[shape, shape],
        in_specs=[SMEM, VMEM, VMEM],
        out_specs=[VMEM, VMEM],
        compiler_params=params(12),
        cost_estimate=cost(0, 3 * MIB),
        name="whole_panel",
    )(table, panel, got)


def flips(delta):
    return (delta & 1) ^ (delta >> 1), delta >> 1


def corner_kernel(table, own, swapped, inverses, factor_h, factor_l, cross):
    here_row, here_col = table[ROW], table[COL]
    core, x, y = here_row % 2, here_col % 4, here_col // 4
    mine = (y ^ (y >> 1)) & 1

    def corner(panel, half):
        blocks = []
        for xx in range(4):
            one, three = flips(xx ^ x)
            pair = mine ^ panel
            slot = jnp.where(half == 0, pair | (one << 1) | (three << 2), one | (three << 1) | (pair << 2))
            blocks.append(jnp.where(core == half, own[slot], swapped[slot]))
        return jnp.concatenate(blocks, axis=1)

    for p in range(2):
        factor_h[p], factor_l[p] = split(inverses[p])
    for half in range(2):
        rows = slice(half * 256, (half + 1) * 256)
        factor_h[2, rows, :], factor_l[2, rows, :] = split(corner(1, half))
        cross[rows, :] = dot3(split(corner(0, half)), (factor_h[0], factor_l[0]))


def corners(table, own, swapped, inverses):
    return pl.pallas_call(
        corner_kernel,
        out_shape=[
            jax.ShapeDtypeStruct((3, PANEL, PANEL), BF16),
            jax.ShapeDtypeStruct((3, PANEL, PANEL), BF16),
            jax.ShapeDtypeStruct((PANEL, PANEL), F32),
        ],
        in_specs=[SMEM, VMEM, VMEM, VMEM],
        out_specs=[VMEM] * 3,
        compiler_params=params(20),
        cost_estimate=cost(6 * PANEL**3, 8 * MIB),
        name="corners",
    )(table, own, swapped, inverses)


def factor_kernel(table, own, swapped, factor_h, factor_l, cross, high, low, patch):
    here_row, col = table[ROW], table[COL]
    core, slot = here_row % 2, col % 4
    inside = lax.broadcasted_iota(jnp.int32, (PANEL, 1024), 1) < BLK

    def mine(x):
        out = x[:, :BLK]
        for s in range(1, 4):
            out = jnp.where(slot == s, x[:, s * BLK : (s + 1) * BLK], out)
        return out

    def begin_with(block, x):
        return jnp.concatenate([block, x[:, BLK:]], axis=1)

    def factor(n):
        return factor_h[n], factor_l[n]

    def factor_columns(n):
        return mine(factor_h[n].astype(F32)) + mine(factor_l[n].astype(F32))

    first = jnp.where(core == 0, own[...], swapped[...])
    first = jnp.where(inside & (col < 4), 0.0, first)
    second = jnp.where(core == 0, swapped[...], own[...])
    second = second - dot3(split(cross[...]), split(first))
    patch[...] = begin_with(jnp.where(col < 4, mine(cross[...]), second[:, :BLK]), second)
    second = jnp.where(inside & (col < 8), 0.0, second)
    right = dot3(factor(1), split(second))
    in_second = (col >= 4) & (col < 8)
    right = begin_with(jnp.where(in_second, factor_columns(1), right[:, :BLK]), right)
    terms = split(right)
    high[PANEL:], low[PANEL:] = terms
    first = jnp.where(inside & (col < 8), 0.0, first)
    left = dot3(factor(0), split(first - dot3(factor(2), terms)))
    left = begin_with(jnp.where(col < 4, factor_columns(0), left[:, :BLK]), left)
    high[:PANEL], low[:PANEL] = split(left)


def right_factor(table, own, swapped, factors, cross):
    shape = jax.ShapeDtypeStruct((1024, 1024), BF16)
    return pl.pallas_call(
        factor_kernel,
        out_shape=[shape, shape, jax.ShapeDtypeStruct((PANEL, 1024), F32)],
        in_specs=[SMEM] + [VMEM] * 5,
        out_specs=[VMEM] * 3,
        compiler_params=params(34),
        cost_estimate=cost(4 * 6 * PANEL * PANEL * 1024, 14 * MIB),
        name="right_factor",
    )(table, own, swapped, *factors, cross)


def block_at(base, half, t, s):
    return jnp.maximum(s[base + half * 8 + t], 0)


def extend_kernel(columns, table, front, *refs):
    out, refs = refs[-1], refs[:-1]
    kept, *got = (refs[2 * k : 2 * k + 2] for k in range(1 + columns))
    step = pl.program_id(0)
    out[...] = front[...]
    for half in range(2):

        @pl.when(table[KEPT_AT + half * 8 + step] >= 0)
        def _(half=half):
            for d in range(5):
                to = pl.ds(pl.multiple_of(table[KEPT_COL + d] * BLK, BLK), BLK)
                out[half, :, to] += kept[half][0, 0, :, d * BLK : (d + 1) * BLK]

        @pl.when(table[GOT_AT + half * 8 + step] >= 0)
        def _(half=half):
            for j in range(columns):
                to = pl.ds(pl.multiple_of(table[GOT_COL + j] * BLK, BLK), BLK)
                out[half, :, to] += got[j][half][0]


def extend(table, front, pieces, got):
    def kept_at(half):
        return lambda t, s: (block_at(KEPT_AT, half, t, s), s[SIDE], 0, 0)

    def got_at(half):
        return lambda t, s: (block_at(GOT_AT, half, t, s), 0, 0)

    tile = pl.BlockSpec((2, BLK, 1024), lambda t, s: (0, t, 0))
    kept_specs = [pl.BlockSpec((1, 1, BLK, 640), kept_at(half)) for half in range(2)]
    got_specs = [pl.BlockSpec((1, BLK, BLK), got_at(half)) for half in range(2)]
    return pl.pallas_call(
        functools.partial(extend_kernel, len(got)),
        out_shape=pltpu.HBM((2, 1024, 1024), F32),
        grid_spec=pltpu.PrefetchScalarGridSpec(
            num_scalar_prefetch=1,
            grid=(8,),
            in_specs=[tile, *kept_specs, *got_specs * len(got)],
            out_specs=tile,
        ),
        compiler_params=params(20),
        cost_estimate=cost(0, MIB),
        name="extend",
    )(table, in_hbm(front.reshape(2, 1024, 1024)), *[in_hbm(pieces)] * 2, *[g for g in got for _ in range(2)])


ORDERS = ((1, 3, 4, 12), (3, 1, 12, 4)), ((4, 12, 1, 3), (12, 4, 3, 1))


def update_kernel(table, front, *refs):
    blocks = refs[:4], refs[4:8]
    right_h, right_l, marks, got_b, got_c, got_d, out, panels = refs[8:]
    step = pl.program_id(0)
    span = pl.ds(pl.multiple_of(step % 2 * 256, 256), 256)
    col, core = table[COL], table[ROW] % 2

    def assemble(which):
        held, came, held_far, came_far = blocks[which]
        for c in range(16):
            one_x, three_x = flips((c ^ col) & 3)
            one_y, three_y = flips((c ^ col) >> 2)
            bits = {1: one_x, 3: three_x, 4: one_y, 12: three_y}
            even, odd = (ORDERS[q][which] for q in range(2))
            flip = [jnp.where(core == 0, bits[e], bits[o]) for e, o in zip(even, odd)]
            slot = flip[0] | (flip[1] << 1)
            later, far = flip[2] == 1, flip[3] == 1
            near_block = jnp.where(later, came[slot, span, :], held[slot, span, :])
            far_block = jnp.where(later, came_far[slot, span, :], held_far[slot, span, :])
            block = jnp.where(far, far_block, near_block)
            y, x = c // 4, c % 4
            rows = slice(0, 256) if y < 2 else slice(256, PANEL)
            first = min(y, 3 - y) * PANEL + x * BLK
            columns = slice(first, first + BLK)
            panels[0, rows, columns], panels[1, rows, columns] = split(block)

    for which in range(2):
        pl.when(step // 2 == which)(functools.partial(assemble, which))

    change = dot3((panels[0], panels[1]), (right_h[...], right_l[...])).reshape(2, 256, 1024)
    active = marks[...] == 0
    for j in range(8):
        columns = slice(j * BLK, (j + 1) * BLK)
        before, part = front[:, :, columns], change[:, :, columns]
        after = before - part
        if j == 0:
            after = jnp.where(col < 8, part, after)
        out[:, :, columns] = jnp.where(active, after, before)

    def columns_of(j):
        return pl.ds(pl.multiple_of(table[GOT_COL + j] * BLK, BLK), BLK)

    for part in range(4):
        half, rest = part // 2, part % 2
        rows = slice(rest * BLK, (rest + 1) * BLK)
        m = table[GOT_AT + half * 8 + 2 * step + rest]

        @pl.when((m >= 0) & (m < 5))
        def _(half=half, rows=rows, m=m):
            out[half, rows, columns_of(2)] += got_b[m]
            out[half, rows, columns_of(3)] += got_d[m]

        @pl.when(m >= 5)
        def _(half=half, rows=rows, m=m):
            out[half, rows, columns_of(2)] += got_c[m - 5]


def update(table, front, blocks, right, marks, got):
    tile = pl.BlockSpec((2, 256, 1024), lambda t, s: (0, t, 0))
    return pl.pallas_call(
        update_kernel,
        out_shape=pltpu.HBM((2, 1024, 1024), F32),
        grid_spec=pltpu.PrefetchScalarGridSpec(
            num_scalar_prefetch=1,
            grid=(4,),
            in_specs=[
                tile,
                *[VMEM] * 10,
                pl.BlockSpec((2, 256, BLK), lambda t, s: (0, t, 0)),
                *[VMEM] * 3,
            ],
            out_specs=tile,
            scratch_shapes=[pltpu.VMEM((2, PANEL, 1024), BF16)],
        ),
        compiler_params=params(34),
        cost_estimate=cost(6 * 2048 * 1024 * 1024, 32 * MIB),
        name="update",
    )(table, in_hbm(front), *blocks[0], *blocks[1], *right, marks.reshape(2, 1024, BLK), *got)


def finish_kernel(
    table, list_other, list_mine, front, got_e, got_f, patch,
    out, held, read_sem, write_sem, sem,
):
    del front
    core = table[ROW] % 2
    copies = []
    for n, (column, first, got) in enumerate([(3, 5, got_e), (4, 0, got_f)]):
        columns = pl.ds(pl.multiple_of(table[GOT_COL + column] * BLK, BLK), BLK)
        for m in range(got.shape[0]):
            rows = pl.ds(pl.multiple_of(table[GOT_ROW + first + m] * BLK, BLK), BLK)
            there, here = out.at[rows, columns], held.at[n, m]
            read = pltpu.make_async_copy(there, here, read_sem.at[n, m])
            write = pltpu.make_async_copy(here, there, write_sem.at[n, m])
            copies.append((read, write, n, m, got))
    for read, *_ in copies:
        read.start()
    for read, write, n, m, got in copies:
        read.wait()
        held[n, m] += got[m]
        write.start()
    for _, write, *_ in copies:
        write.wait()

    def entry(n):
        return jnp.where(core == 0, list_other[n], list_mine[n])

    def place(n, carry):
        at, p = entry(n) >> 9, entry(n) & 511
        pltpu.make_async_copy(patch.at[pl.ds(p, 1), :], out.at[pl.ds(at, 1), :], sem).start()
        return carry

    def wait(_, carry):
        pltpu.make_async_copy(patch.at[pl.ds(0, 1), :], out.at[pl.ds(0, 1), :], sem).wait()
        return carry

    lax.fori_loop(0, entry(PANEL), place, 0)
    lax.fori_loop(0, entry(PANEL), wait, 0)


def finish(table, lists, front, got, patch):
    return pl.pallas_call(
        finish_kernel,
        out_shape=jax.ShapeDtypeStruct((2048, 1024), F32),
        in_specs=[SMEM, SMEM, SMEM, HBM] + [VMEM] * 3,
        out_specs=HBM,
        scratch_shapes=[
            pltpu.VMEM((2, 10, BLK, BLK), F32),
            pltpu.SemaphoreType.DMA((2, 10)),
            pltpu.SemaphoreType.DMA((2, 10)),
            pltpu.SemaphoreType.DMA(()),
        ],
        input_output_aliases={3: 0},
        compiler_params=params(12),
        cost_estimate=cost(0, 8 * MIB),
        name="finish",
    )(table, *lists, front, *got, patch)


def swap(block, axis, partner):
    count = lax.axis_size(axis)
    return lax.ppermute(block, axis, [(i, partner(i)) for i in range(count)])


def fold(block, near):
    came = lax.ppermute(block[1], "col", [(c, c ^ 12) for c in range(8)])
    return jnp.where(near, block[0], came)


def local(front, children, child_maps, pivots, diag_inverses):
    here_row, here_col = lax.axis_index("row"), lax.axis_index("col")
    chip = here_row >> 1
    together = lax.optimization_barrier
    pieces = children.reshape(10, 2, BLK, 640)

    def by_row(block, mask):
        return swap(block, "row", lambda i: i ^ mask)

    def by_col(block, mask):
        return swap(block, "col", lambda i: i ^ mask)

    bits = (chip ^ (chip >> 1)) & 1, chip >> 1
    rings = [[(r, r ^ ((2, 6), (6, 2))[r % 2][k]) for r in range(8)] for k in range(2)]
    low = [jnp.where(here_row & 1 == 0, bits[k], bits[1 - k]) == 0 for k in range(2)]
    pivots, near, low = together((pivots, here_col < 8, low))

    def halve(part, step):
        size = part.shape[0] // 2
        leave = jnp.where(low[step], part[size:], part[:size])
        stay = jnp.where(low[step], part[:size], part[size:])
        return stay + lax.ppermute(leave, "row", rings[step])

    def double(part, step):
        came = lax.ppermute(part, "row", rings[step])
        first, second = jnp.where(low[step], part, came), jnp.where(low[step], came, part)
        return jnp.concatenate([first, second], axis=0)

    def gather_step(block, which, step):
        route = [
            (r * 16 + c, r * 16 + (c ^ ORDERS[r % 2][which][step]))
            for r in range(8)
            for c in range(16)
        ]
        return lax.ppermute(block, ("row", "col"), route)

    first = cut(child_maps, pieces)
    got0 = by_row(first, 4)
    *rest, panel, corner, away, table = prepare(child_maps, pivots, front, pieces, first)
    rest_a, rest_b, rest_c, rest_d, rest_e, rest_f = rest
    corner = corner + by_row(away, 1)
    corner = corner + (by_row(corner, 2) + (by_row(corner, 6) + by_row(corner, 4)))
    away_rows, marks, list_other = pivot_terms(child_maps, pivots, front, children)
    got0, away_rows, rest_a, marks, corner = together((got0, away_rows, rest_a, marks, corner))

    top, bottom = whole_panel(table, panel, got0)
    mine = fold((top, bottom), near)
    corner = fold((corner, corner), near)[None]
    got_a = by_row(rest_a, 4)
    own_rows, marks, list_mine = pivot_terms(child_maps, pivots, front, children, marks)
    total = own_rows + by_row(away_rows, 1)
    mine, corner, total, got_a, rest_b = together((mine, corner, total, got_a, rest_b))

    def corner_step(block, step):
        masks = ((4, 1, 3), (1, 3, 4))
        route = [
            (r * 16 + c, r * 16 + (c ^ masks[r % 2][step])) for r in range(8) for c in range(16)
        ]
        return jnp.concatenate([block, lax.ppermute(block, ("row", "col"), route)], axis=0)

    held = [mine[None, :PANEL], mine[None, PANEL:]]
    for k in range(2):
        came = [gather_step(held[w], w, k) for w in range(2)]
        held = [jnp.concatenate([h, c], axis=0) for h, c in zip(held, came)]
        corner = corner_step(corner, k)
        total = halve(total, k)
        if k == 0:
            front = extend(table, front, pieces, (got0, got_a))
        held, corner, total, rest_b, front = together((held, corner, total, rest_b, front))
    came = [gather_step(held[w], w, 2) for w in range(2)]
    corner = corner_step(corner, 2)
    total = double(total, 1)
    got_b = by_row(rest_b, 4)
    came, corner, total, got_b, rest_c = together((came, corner, total, got_b, rest_c))
    held_far = [gather_step(held[w], w, 3) for w in range(2)]
    *factors, cross = corners(table, corner, by_row(corner, 1), diag_inverses)
    total = double(total, 0)
    got_c = by_row(rest_c, 4)
    came, held_far, total, got_c, rest_d, factors, cross = together(
        (came, held_far, total, got_c, rest_d, factors, cross)
    )
    came_far = [gather_step(came[w], w, 3) for w in range(2)]
    got_d = by_row(rest_d, 4)
    *right, patch = right_factor(table, total, by_row(total, 1), factors, cross)
    came_far, got_d, rest_e, rest_f, right, patch = together(
        (came_far, got_d, rest_e, rest_f, right, patch)
    )
    got_e, got_f = by_row(rest_e, 4), by_row(rest_f, 4)
    blocks = [(held[w], came[w], held_far[w], came_far[w]) for w in range(2)]
    front = update(table, front, blocks, right, marks, (got_b, got_c, got_d))
    front = front.reshape(2048, 1024)
    return finish(table, (list_other, list_mine), front, (got_e, got_f), patch)


def solution(mesh):
    return jax.shard_map(
        local,
        mesh=mesh,
        in_specs=(P("row", "col"), P("row", "col"), P(), P(), P()),
        out_specs=P("row", "col"),
        check_vma=False,
    )
```

```python
import functools

import jax
import jax.numpy as jnp
from jax import lax
from jax.experimental import pallas as pl
from jax.experimental.pallas import tpu as pltpu
from jax.sharding import PartitionSpec as P

BLK = 128
PANEL = 512
MIB = 1 << 20
F32 = jnp.float32
BF16 = jnp.bfloat16
SMEM = pl.BlockSpec(memory_space=pltpu.SMEM)
VMEM = pl.BlockSpec(memory_space=pltpu.VMEM)
HBM = pl.BlockSpec(memory_space=pltpu.HBM)
KEPT_AT = 0
GOT_AT = 16
KEPT_COL = 32
GOT_COL = 40
ROW, COL, SIDE = 48, 49, 50
GOT_ROW = 52


def split(x):
    high = x.astype(BF16)
    return high, (x - high.astype(F32)).astype(BF16)


def dot3(a, b):
    rows = a[0].shape[0]
    both = jnp.dot(jnp.concatenate(a, axis=0), b[0], preferred_element_type=F32)
    return both[:rows] + (both[rows:] + jnp.dot(a[0], b[1], preferred_element_type=F32))


def params(mib):
    return pltpu.CompilerParams(vmem_limit_bytes=mib * MIB)


def in_hbm(x):
    return pltpu.with_memory_space_constraint(x, pltpu.HBM)


def cost(flops, moved):
    return pl.CostEstimate(flops=flops, bytes_accessed=moved, transcendentals=0)


def first_block(maps, child, here_col):
    place, found = jnp.int32(0), jnp.int32(0)
    for d in range(5):
        hit = (maps[child, d * 16 + here_col] // 16 == 0).astype(jnp.int32)
        place, found = place + d * hit, found + hit
    return place, found


def cut_kernel(maps, pieces, first, sem):
    other = 1 - lax.axis_index("row") // 4
    place, _ = first_block(maps, 1 - other, lax.axis_index("col"))
    columns = pl.ds(pl.multiple_of(place * BLK, BLK), BLK)
    copy = pltpu.make_async_copy(pieces.at[:, other, :, columns], first, sem)
    copy.start()
    copy.wait()


def cut(maps, pieces):
    return pl.pallas_call(
        cut_kernel,
        out_shape=jax.ShapeDtypeStruct((10, BLK, BLK), F32),
        in_specs=[SMEM, HBM],
        out_specs=VMEM,
        scratch_shapes=[pltpu.SemaphoreType.DMA(())],
        compiler_params=params(4),
        cost_estimate=cost(0, MIB),
        name="cut",
    )(in_hbm(maps), in_hbm(pieces))


def prepare_kernel(
    maps, pivots, front, pieces, first, *refs,
):
    *rests, panel, own, away, table, sending, kept, total, sem = refs
    here_row, here_col = lax.axis_index("row"), lax.axis_index("col")
    side, core = here_row // 4, here_row % 2
    other = 1 - side
    place, found = first_block(maps, side, here_col)
    got_place, _ = first_block(maps, other, here_col)

    def columns(d):
        return pl.ds(pl.multiple_of(d * BLK, BLK), BLK)

    reads = [
        pltpu.make_async_copy(pieces.at[:, other], sending, sem.at[0]),
        pltpu.make_async_copy(pieces.at[:, side, :, columns(place)], kept, sem.at[1]),
        pltpu.make_async_copy(front.at[:, pl.ds(0, BLK)], panel, sem.at[2]),
    ]
    writes = []
    rest_a, rest_b, rest_c = rests
    parts = (
        (0, 0, rest_a),
        (1, 0, rest_b),
        (1, 5, rest_c.at[pl.ds(0, 5)]),
        (2, 0, rest_c.at[pl.ds(5, 10)]),
        (3, 0, rest_c.at[pl.ds(15, 10)]),
    )
    for n, (j, start, target) in enumerate(parts):
        d = j + (j >= place).astype(jnp.int32)
        source = sending.at[pl.ds(start, target.shape[0]), :, columns(d)]
        writes.append(pltpu.make_async_copy(source, target, sem.at[3 + n]))
    for copy in reads:
        copy.start()
    for kk in range(16):
        table[KEPT_AT + kk] = -1
        table[GOT_AT + kk] = -1
    for m in range(10):
        table[KEPT_AT + maps[side, m * 8 + here_row] // 8] = m
        target = maps[other, m * 8 + here_row] // 8
        table[GOT_AT + target] = m
        table[GOT_ROW + m] = target
    for d in range(5):
        table[KEPT_COL + d] = maps[side, d * 16 + here_col] // 16
    table[GOT_COL] = maps[other, got_place * 16 + here_col] // 16
    for j in range(4):
        d = j + (j >= got_place).astype(jnp.int32)
        table[GOT_COL + 1 + j] = maps[other, d * 16 + here_col] // 16
    table[ROW] = here_row
    table[COL] = here_col
    table[SIDE] = side
    turned = pivots[...].T
    wanted = jnp.concatenate(
        [jnp.where(here_col < 4, turned[:, 4 + k : 5 + k], turned[:, k : k + 1]) for k in range(4)],
        axis=0,
    )
    block, offset = wanted >> 7, wanted & 127
    mine = jnp.where((block & 7) == here_row, (block >> 3) * BLK + offset, -1)
    sent = jnp.full_like(mine, -1)
    for m in range(10):
        hit = (block == maps[side, m * 8 + (here_row ^ 4)]) & (found > 0)
        sent = jnp.where(hit, m * BLK + offset, sent)
    reads[0].wait()
    for copy in writes:
        copy.start()
    reads[1].wait()
    reads[2].wait()

    @pl.when(found > 0)
    def _():
        for m in range(10):
            at = pl.multiple_of(maps[side, m * 8 + here_row] // 8 * BLK, BLK)
            panel[pl.ds(at, BLK), :] += kept[m]

    def rows_of(index, values, base):
        lane = lax.broadcasted_iota(jnp.int32, (PANEL, values.shape[0]), 1) + base
        chosen = jnp.where(lane == index, 1.0, 0.0).astype(BF16)
        both = jnp.concatenate(split(values), axis=1)
        return jnp.dot(chosen, both, preferred_element_type=F32)

    terms = jnp.zeros((PANEL, 2 * BLK), F32)
    for k in range(8):
        terms += rows_of(mine, panel[k * 256 : (k + 1) * 256, :], k * 256)
    for k in range(5):
        values = first[2 * k : 2 * k + 2].reshape(256, BLK)
        terms += rows_of(sent, values, k * 256)
    total[...] = terms[:, :BLK] + terms[:, BLK:]
    own[...] = total[pl.ds(pl.multiple_of(core * 256, 256), 256), :]
    away[...] = total[pl.ds(pl.multiple_of((1 - core) * 256, 256), 256), :]
    for copy in writes:
        copy.wait()


def prepare(maps, pivots, front, pieces, first):
    column = jax.ShapeDtypeStruct((10, BLK, BLK), F32)
    return pl.pallas_call(
        prepare_kernel,
        out_shape=[
            column,
            jax.ShapeDtypeStruct((5, BLK, BLK), F32),
            jax.ShapeDtypeStruct((25, BLK, BLK), F32),
            jax.ShapeDtypeStruct((2048, BLK), F32),
            jax.ShapeDtypeStruct((256, BLK), F32),
            jax.ShapeDtypeStruct((256, BLK), F32),
            jax.ShapeDtypeStruct((64,), jnp.int32),
        ],
        in_specs=[SMEM, VMEM, HBM, HBM, VMEM],
        out_specs=[HBM] * 3 + [VMEM, VMEM, VMEM, SMEM],
        scratch_shapes=[
            pltpu.VMEM((10, BLK, 640), F32),
            pltpu.VMEM((10, BLK, BLK), F32),
            pltpu.VMEM((PANEL, BLK), F32),
            pltpu.SemaphoreType.DMA((8,)),
        ],
        compiler_params=params(24),
        cost_estimate=cost(0, 9 * MIB),
        name="prepare",
    )(in_hbm(maps), in_hbm(pivots.reshape(8, BLK)), in_hbm(front), in_hbm(pieces), first)


def pivot_kernel(mine_half, maps, pivots, front, children, *refs):
    rows, marks, front_list, spread, inverse, child_list, sem, child_sem = refs[-8:]
    rows[...] = jnp.zeros_like(rows)
    marks[...] = refs[0][...] if mine_half else jnp.zeros_like(marks)
    here_row, here_col = lax.axis_index("row"), lax.axis_index("col")
    side, quarter, core = here_row // 4, here_row % 4, here_row % 2
    half = core if mine_half else 1 - core
    spread[...] = jnp.zeros_like(spread)

    def clear(b, carry):
        inverse[b] = -1
        return carry

    lax.fori_loop(0, 128, clear, 0, unroll=16)
    for k in range(20):
        inverse[maps[side, 4 * k + quarter]] = k

    def visit(p, counts):
        pivot = pivots[half * PANEL + p]
        block, offset = pivot >> 7, pivot & 127
        child_block = inverse[block]
        mine = (block & 7) == here_row
        shared = ((block & 3) == quarter) & (child_block >= 0)
        front_list[counts[0]] = (((block >> 3) * BLK + offset) << 9) | p
        child_list[counts[1]] = ((child_block * BLK + offset) << 9) | p
        return counts[0] + mine.astype(jnp.int32), counts[1] + shared.astype(jnp.int32)

    counts = lax.fori_loop(0, PANEL, visit, (jnp.int32(0), jnp.int32(0)), unroll=8)
    front_list[PANEL] = counts[0]
    mark = jnp.full((1, BLK), half + 1, jnp.int32).astype(F32)

    def take_front(n, carry):
        at, p = front_list[n] >> 9, front_list[n] & 511
        pltpu.make_async_copy(front.at[pl.ds(at, 1), :], rows.at[pl.ds(p, 1), :], sem).start()
        marks[pl.ds(at, 1), :] = mark
        return carry

    def take_child(n, carry):
        at, p = child_list[n] >> 9, child_list[n] & 511
        pltpu.make_async_copy(
            children.at[pl.ds(at, 1), :], spread.at[pl.ds(p, 1), :], child_sem
        ).start()
        return carry

    def wait(source, target, semaphore, count):
        def some(size):
            def body(_, carry):
                pltpu.make_async_copy(
                    source.at[pl.ds(0, size), :], target.at[pl.ds(0, size), :], semaphore
                ).wait()
                return carry

            return body

        lax.fori_loop(0, count // 16, some(16), 0)
        lax.fori_loop(0, count % 16, some(1), 0)

    lax.fori_loop(0, counts[0], take_front, 0)
    lax.fori_loop(0, counts[1], take_child, 0)
    wait(front, rows, sem, counts[0])
    wait(children, spread, child_sem, counts[1])
    for d in range(5):
        to = pl.ds(pl.multiple_of(maps[side, d * 16 + here_col] // 16 * BLK, BLK), BLK)
        rows[:, to] += spread[:, d * BLK : (d + 1) * BLK]


def pivot_terms(maps, pivots, front, children, *before):
    mine_half = len(before) > 0
    return pl.pallas_call(
        functools.partial(pivot_kernel, mine_half),
        out_shape=[
            jax.ShapeDtypeStruct((PANEL, 1024), F32),
            jax.ShapeDtypeStruct((2048, BLK), F32),
            jax.ShapeDtypeStruct((PANEL + 1,), jnp.int32),
        ],
        in_specs=[SMEM, SMEM, HBM, HBM] + [VMEM] * len(before),
        out_specs=[VMEM, VMEM, SMEM],
        scratch_shapes=[
            pltpu.VMEM((PANEL, 640), F32),
            pltpu.SMEM((128,), jnp.int32),
            pltpu.SMEM((PANEL + 1,), jnp.int32),
            pltpu.SemaphoreType.DMA(()),
            pltpu.SemaphoreType.DMA(()),
        ],
        compiler_params=params(12),
        cost_estimate=cost(0, 24 * MIB),
        name="pivot_terms_mine" if mine_half else "pivot_terms_other",
    )(in_hbm(maps), in_hbm(pivots), in_hbm(front), in_hbm(children), *before)


def panel_kernel(table, panel, got, top, bottom):
    top[...] = panel[:1024, :]
    bottom[...] = panel[1024:, :]

    @pl.when(table[GOT_COL] == 0)
    def _():
        for kk in range(16):
            m = table[GOT_AT + kk]
            half = top if kk < 8 else bottom
            at = kk % 8 * BLK

            @pl.when(m >= 0)
            def _(half=half, at=at, m=m):
                half[at : at + BLK, :] += got[m]


def whole_panel(table, panel, got):
    shape = jax.ShapeDtypeStruct((1024, BLK), F32)
    return pl.pallas_call(
        panel_kernel,
        out_shape=[shape, shape],
        in_specs=[SMEM, VMEM, VMEM],
        out_specs=[VMEM, VMEM],
        compiler_params=params(12),
        cost_estimate=cost(0, 3 * MIB),
        name="whole_panel",
    )(table, panel, got)


def flips(delta):
    return (delta & 1) ^ (delta >> 1), delta >> 1


def corner_kernel(table, own, swapped, inverses, factor_h, factor_l, cross):
    here_row, here_col = table[ROW], table[COL]
    core, x, y = here_row % 2, here_col % 4, here_col // 4
    mine = (y ^ (y >> 1)) & 1

    def corner(panel, half):
        blocks = []
        for xx in range(4):
            one, three = flips(xx ^ x)
            pair = mine ^ panel
            slot = jnp.where(half == 0, pair | (one << 1) | (three << 2), one | (three << 1) | (pair << 2))
            blocks.append(jnp.where(core == half, own[slot], swapped[slot]))
        return jnp.concatenate(blocks, axis=1)

    for p in range(2):
        factor_h[p], factor_l[p] = split(inverses[p])
    for half in range(2):
        rows = slice(half * 256, (half + 1) * 256)
        factor_h[2, rows, :], factor_l[2, rows, :] = split(corner(1, half))
        cross[rows, :] = dot3(split(corner(0, half)), (factor_h[0], factor_l[0]))


def corners(table, own, swapped, inverses):
    return pl.pallas_call(
        corner_kernel,
        out_shape=[
            jax.ShapeDtypeStruct((3, PANEL, PANEL), BF16),
            jax.ShapeDtypeStruct((3, PANEL, PANEL), BF16),
            jax.ShapeDtypeStruct((PANEL, PANEL), F32),
        ],
        in_specs=[SMEM, VMEM, VMEM, VMEM],
        out_specs=[VMEM] * 3,
        compiler_params=params(20),
        cost_estimate=cost(6 * PANEL**3, 8 * MIB),
        name="corners",
    )(table, own, swapped, inverses)


def factor_kernel(table, own, swapped, factor_h, factor_l, cross, high, low, patch):
    here_row, col = table[ROW], table[COL]
    core, slot = here_row % 2, col % 4
    inside = lax.broadcasted_iota(jnp.int32, (PANEL, 1024), 1) < BLK

    def mine(x):
        out = x[:, :BLK]
        for s in range(1, 4):
            out = jnp.where(slot == s, x[:, s * BLK : (s + 1) * BLK], out)
        return out

    def begin_with(block, x):
        return jnp.concatenate([block, x[:, BLK:]], axis=1)

    def factor(n):
        return factor_h[n], factor_l[n]

    def factor_columns(n):
        return mine(factor_h[n].astype(F32)) + mine(factor_l[n].astype(F32))

    first = jnp.where(core == 0, own[...], swapped[...])
    first = jnp.where(inside & (col < 4), 0.0, first)
    second = jnp.where(core == 0, swapped[...], own[...])
    second = second - dot3(split(cross[...]), split(first))
    patch[...] = begin_with(jnp.where(col < 4, mine(cross[...]), second[:, :BLK]), second)
    second = jnp.where(inside & (col < 8), 0.0, second)
    right = dot3(factor(1), split(second))
    in_second = (col >= 4) & (col < 8)
    right = begin_with(jnp.where(in_second, factor_columns(1), right[:, :BLK]), right)
    terms = split(right)
    high[PANEL:], low[PANEL:] = terms
    first = jnp.where(inside & (col < 8), 0.0, first)
    left = dot3(factor(0), split(first - dot3(factor(2), terms)))
    left = begin_with(jnp.where(col < 4, factor_columns(0), left[:, :BLK]), left)
    high[:PANEL], low[:PANEL] = split(left)


def right_factor(table, own, swapped, factors, cross):
    shape = jax.ShapeDtypeStruct((1024, 1024), BF16)
    return pl.pallas_call(
        factor_kernel,
        out_shape=[shape, shape, jax.ShapeDtypeStruct((PANEL, 1024), F32)],
        in_specs=[SMEM] + [VMEM] * 5,
        out_specs=[VMEM] * 3,
        compiler_params=params(24),
        cost_estimate=cost(4 * 6 * PANEL * PANEL * 1024, 14 * MIB),
        name="right_factor",
    )(table, own, swapped, *factors, cross)


def block_at(base, half, t, s):
    return jnp.maximum(s[base + half * 8 + t], 0)


def extend_kernel(columns, table, front, *refs):
    out, refs = refs[-1], refs[:-1]
    kept, *got = (refs[2 * k : 2 * k + 2] for k in range(1 + columns))
    step = pl.program_id(0)
    out[...] = front[...]
    for half in range(2):

        @pl.when(table[KEPT_AT + half * 8 + step] >= 0)
        def _(half=half):
            for d in range(5):
                to = pl.ds(pl.multiple_of(table[KEPT_COL + d] * BLK, BLK), BLK)
                out[half, :, to] += kept[half][0, 0, :, d * BLK : (d + 1) * BLK]

        @pl.when(table[GOT_AT + half * 8 + step] >= 0)
        def _(half=half):
            for j in range(columns):
                to = pl.ds(pl.multiple_of(table[GOT_COL + j] * BLK, BLK), BLK)
                out[half, :, to] += got[j][half][0]


def extend(table, front, pieces, got):
    def kept_at(half):
        return lambda t, s: (block_at(KEPT_AT, half, t, s), s[SIDE], 0, 0)

    def got_at(half):
        return lambda t, s: (block_at(GOT_AT, half, t, s), 0, 0)

    tile = pl.BlockSpec((2, BLK, 1024), lambda t, s: (0, t, 0))
    kept_specs = [pl.BlockSpec((1, 1, BLK, 640), kept_at(half)) for half in range(2)]
    got_specs = [pl.BlockSpec((1, BLK, BLK), got_at(half)) for half in range(2)]
    return pl.pallas_call(
        functools.partial(extend_kernel, len(got)),
        out_shape=pltpu.HBM((2, 1024, 1024), F32),
        grid_spec=pltpu.PrefetchScalarGridSpec(
            num_scalar_prefetch=1,
            grid=(8,),
            in_specs=[tile, *kept_specs, *got_specs * len(got)],
            out_specs=tile,
        ),
        compiler_params=params(20),
        cost_estimate=cost(0, MIB),
        name="extend",
    )(table, in_hbm(front.reshape(2, 1024, 1024)), *[in_hbm(pieces)] * 2, *[g for g in got for _ in range(2)])


ORDERS = ((1, 3, 4, 12), (3, 1, 12, 4)), ((4, 12, 1, 3), (12, 4, 3, 1))


def update_kernel(table, front, *refs):
    blocks = refs[:4], refs[4:8]
    right_h, right_l, marks, got_b, out, panels = refs[8:]
    step = pl.program_id(0)
    span = pl.ds(pl.multiple_of(step % 2 * 256, 256), 256)
    col, core = table[COL], table[ROW] % 2

    def assemble(which):
        held, came, held_far, came_far = blocks[which]
        for c in range(16):
            one_x, three_x = flips((c ^ col) & 3)
            one_y, three_y = flips((c ^ col) >> 2)
            bits = {1: one_x, 3: three_x, 4: one_y, 12: three_y}
            even, odd = (ORDERS[q][which] for q in range(2))
            flip = [jnp.where(core == 0, bits[e], bits[o]) for e, o in zip(even, odd)]
            slot = flip[0] | (flip[1] << 1)
            later, far = flip[2] == 1, flip[3] == 1
            near_block = jnp.where(later, came[slot, span, :], held[slot, span, :])
            far_block = jnp.where(later, came_far[slot, span, :], held_far[slot, span, :])
            block = jnp.where(far, far_block, near_block)
            y, x = c // 4, c % 4
            rows = slice(0, 256) if y < 2 else slice(256, PANEL)
            first = min(y, 3 - y) * PANEL + x * BLK
            columns = slice(first, first + BLK)
            panels[0, rows, columns], panels[1, rows, columns] = split(block)

    for which in range(2):
        pl.when(step // 2 == which)(functools.partial(assemble, which))

    active = marks[...] == 0
    for piece in range(4):
        wide = slice(piece * 256, (piece + 1) * 256)
        change = dot3((panels[0], panels[1]), (right_h[:, wide], right_l[:, wide]))
        change = change.reshape(2, 256, 256)
        for j in range(2):
            columns = slice(piece * 256 + j * BLK, piece * 256 + (j + 1) * BLK)
            before, part = front[:, :, columns], change[:, :, j * BLK : (j + 1) * BLK]
            after = before - part
            if piece == 0 and j == 0:
                after = jnp.where(col < 8, part, after)
            out[:, :, columns] = jnp.where(active, after, before)

    columns_b = pl.ds(pl.multiple_of(table[GOT_COL + 2] * BLK, BLK), BLK)
    for part in range(4):
        half, rest = part // 2, part % 2
        rows = slice(rest * BLK, (rest + 1) * BLK)
        m = table[GOT_AT + half * 8 + 2 * step + rest]

        @pl.when((m >= 0) & (m < 5))
        def _(half=half, rows=rows, m=m):
            out[half, rows, columns_b] += got_b[m]


def update(table, front, blocks, right, marks, got_b):
    tile = pl.BlockSpec((2, 256, 1024), lambda t, s: (0, t, 0))
    return pl.pallas_call(
        update_kernel,
        out_shape=pltpu.HBM((2, 1024, 1024), F32),
        grid_spec=pltpu.PrefetchScalarGridSpec(
            num_scalar_prefetch=1,
            grid=(4,),
            in_specs=[
                tile,
                *[VMEM] * 10,
                pl.BlockSpec((2, 256, BLK), lambda t, s: (0, t, 0)),
                VMEM,
            ],
            out_specs=tile,
            scratch_shapes=[pltpu.VMEM((2, PANEL, 1024), BF16)],
        ),
        compiler_params=params(24),
        cost_estimate=cost(6 * 2048 * 1024 * 1024, 32 * MIB),
        name="update",
    )(table, in_hbm(front), *blocks[0], *blocks[1], *right, marks.reshape(2, 1024, BLK), got_b)


def finish_kernel(
    table, list_other, list_mine, front, got, patch,
    out, held, read_sem, write_sem, sem,
):
    del front
    core = table[ROW] % 2
    copies = []
    places = [(2, m) for m in range(5, 10)] + [(j, m) for j in (3, 4) for m in range(10)]
    for n, (column, m) in enumerate(places):
        columns = pl.ds(pl.multiple_of(table[GOT_COL + column] * BLK, BLK), BLK)
        rows = pl.ds(pl.multiple_of(table[GOT_ROW + m] * BLK, BLK), BLK)
        there, here = out.at[rows, columns], held.at[n]
        read = pltpu.make_async_copy(there, here, read_sem.at[n])
        write = pltpu.make_async_copy(here, there, write_sem.at[n])
        copies.append((read, write))
    for read, _ in copies:
        read.start()
    for n, (read, write) in enumerate(copies):
        read.wait()
        held[n] += got[n]
        write.start()
    for _, write in copies:
        write.wait()

    def entry(n):
        return jnp.where(core == 0, list_other[n], list_mine[n])

    def place(n, carry):
        at, p = entry(n) >> 9, entry(n) & 511
        pltpu.make_async_copy(patch.at[pl.ds(p, 1), :], out.at[pl.ds(at, 1), :], sem).start()
        return carry

    def wait(_, carry):
        pltpu.make_async_copy(patch.at[pl.ds(0, 1), :], out.at[pl.ds(0, 1), :], sem).wait()
        return carry

    lax.fori_loop(0, entry(PANEL), place, 0)
    lax.fori_loop(0, entry(PANEL), wait, 0)


def finish(table, lists, front, got, patch):
    return pl.pallas_call(
        finish_kernel,
        out_shape=jax.ShapeDtypeStruct((2048, 1024), F32),
        in_specs=[SMEM, SMEM, SMEM, HBM] + [VMEM] * 2,
        out_specs=HBM,
        scratch_shapes=[
            pltpu.VMEM((25, BLK, BLK), F32),
            pltpu.SemaphoreType.DMA((25,)),
            pltpu.SemaphoreType.DMA((25,)),
            pltpu.SemaphoreType.DMA(()),
        ],
        input_output_aliases={3: 0},
        compiler_params=params(12),
        cost_estimate=cost(0, 8 * MIB),
        name="finish",
    )(table, *lists, front, got, patch)


def swap(block, axis, partner):
    count = lax.axis_size(axis)
    return lax.ppermute(block, axis, [(i, partner(i)) for i in range(count)])


def fold(block, near):
    came = lax.ppermute(block[1], "col", [(c, c ^ 12) for c in range(8)])
    return jnp.where(near, block[0], came)


def local(front, children, child_maps, pivots, diag_inverses):
    here_row, here_col = lax.axis_index("row"), lax.axis_index("col")
    chip = here_row >> 1
    together = lax.optimization_barrier
    pieces = children.reshape(10, 2, BLK, 640)

    def by_row(block, mask):
        return swap(block, "row", lambda i: i ^ mask)

    def by_col(block, mask):
        return swap(block, "col", lambda i: i ^ mask)

    bits = (chip ^ (chip >> 1)) & 1, chip >> 1
    rings = [[(r, r ^ ((2, 6), (6, 2))[r % 2][k]) for r in range(8)] for k in range(2)]
    low = [jnp.where(here_row & 1 == 0, bits[k], bits[1 - k]) == 0 for k in range(2)]
    pivots, near, low = together((pivots, here_col < 8, low))

    def halve(part, step):
        size = part.shape[0] // 2
        leave = jnp.where(low[step], part[size:], part[:size])
        stay = jnp.where(low[step], part[:size], part[size:])
        return stay + lax.ppermute(leave, "row", rings[step])

    def double(part, step):
        came = lax.ppermute(part, "row", rings[step])
        first, second = jnp.where(low[step], part, came), jnp.where(low[step], came, part)
        return jnp.concatenate([first, second], axis=0)

    def gather_step(block, which, step):
        route = [
            (r * 16 + c, r * 16 + (c ^ ORDERS[r % 2][which][step]))
            for r in range(8)
            for c in range(16)
        ]
        return lax.ppermute(block, ("row", "col"), route)

    first = cut(child_maps, pieces)
    got0 = by_row(first, 4)
    *rest, panel, corner, away, table = prepare(child_maps, pivots, front, pieces, first)
    rest_a, rest_b, rest_c = rest
    corner = corner + by_row(away, 1)
    corner = corner + (by_row(corner, 2) + (by_row(corner, 6) + by_row(corner, 4)))
    away_rows, marks, list_other = pivot_terms(child_maps, pivots, front, children)
    got0, away_rows, rest_a, marks, corner = together((got0, away_rows, rest_a, marks, corner))

    top, bottom = whole_panel(table, panel, got0)
    mine = fold((top, bottom), near)
    corner = fold((corner, corner), near)[None]
    got_a = by_row(rest_a, 4)
    own_rows, marks, list_mine = pivot_terms(child_maps, pivots, front, children, marks)
    total = own_rows + by_row(away_rows, 1)
    mine, corner, total, got_a, rest_b = together((mine, corner, total, got_a, rest_b))

    def corner_step(block, step):
        masks = ((4, 1, 3), (1, 3, 4))
        route = [
            (r * 16 + c, r * 16 + (c ^ masks[r % 2][step])) for r in range(8) for c in range(16)
        ]
        return jnp.concatenate([block, lax.ppermute(block, ("row", "col"), route)], axis=0)

    held = [mine[None, :PANEL], mine[None, PANEL:]]
    for k in range(2):
        came = [gather_step(held[w], w, k) for w in range(2)]
        held = [jnp.concatenate([h, c], axis=0) for h, c in zip(held, came)]
        corner = corner_step(corner, k)
        total = halve(total, k)
        if k == 0:
            front = extend(table, front, pieces, (got0, got_a))
        held, corner, total, front = together((held, corner, total, front))
    came = [gather_step(held[w], w, 2) for w in range(2)]
    corner = corner_step(corner, 2)
    total, rest_b = together((double(total, 1), rest_b))
    got_b = by_row(rest_b, 4)
    came, corner, total, got_b = together((came, corner, total, got_b))
    held_far = [gather_step(held[w], w, 3) for w in range(2)]
    *factors, cross = corners(table, corner, by_row(corner, 1), diag_inverses)
    total = double(total, 0)
    came, held_far, total, rest_c, factors, cross = together(
        (came, held_far, total, rest_c, factors, cross)
    )
    came_far = [gather_step(came[w], w, 3) for w in range(2)]
    got_c = by_row(rest_c, 4)
    *right, patch = right_factor(table, total, by_row(total, 1), factors, cross)
    came_far, right, patch = together((came_far, right, patch))
    blocks = [(held[w], came[w], held_far[w], came_far[w]) for w in range(2)]
    front = update(table, front, blocks, right, marks, got_b).reshape(2048, 1024)
    return finish(table, (list_other, list_mine), front, got_c, patch)


def solution(mesh):
    return jax.shard_map(
        local,
        mesh=mesh,
        in_specs=(P("row", "col"), P("row", "col"), P(), P(), P()),
        out_specs=P("row", "col"),
        check_vma=False,
    )
```

```python
import functools

import jax
import jax.numpy as jnp
from jax import lax
from jax.experimental import pallas as pl
from jax.experimental.pallas import tpu as pltpu
from jax.sharding import PartitionSpec as P

BLK = 128
PANEL = 512
MIB = 1 << 20
F32 = jnp.float32
BF16 = jnp.bfloat16
SMEM = pl.BlockSpec(memory_space=pltpu.SMEM)
VMEM = pl.BlockSpec(memory_space=pltpu.VMEM)
HBM = pl.BlockSpec(memory_space=pltpu.HBM)
KEPT_AT = 0
GOT_AT = 16
KEPT_COL = 32
GOT_COL = 40
ROW, COL, SIDE = 48, 49, 50
GOT_ROW = 52


def split(x):
    high = x.astype(BF16)
    return high, (x - high.astype(F32)).astype(BF16)


def dot3(a, b):
    rows = a[0].shape[0]
    both = jnp.dot(jnp.concatenate(a, axis=0), b[0], preferred_element_type=F32)
    return both[:rows] + (both[rows:] + jnp.dot(a[0], b[1], preferred_element_type=F32))


def params(mib):
    return pltpu.CompilerParams(vmem_limit_bytes=mib * MIB)


def in_hbm(x):
    return pltpu.with_memory_space_constraint(x, pltpu.HBM)


def cost(flops, moved):
    return pl.CostEstimate(flops=flops, bytes_accessed=moved, transcendentals=0)


def first_block(maps, child, here_col):
    place, found = jnp.int32(0), jnp.int32(0)
    for d in range(5):
        hit = (maps[child, d * 16 + here_col] // 16 == 0).astype(jnp.int32)
        place, found = place + d * hit, found + hit
    return place, found


def cut_kernel(maps, pieces, first, sem):
    other = 1 - lax.axis_index("row") // 4
    place, _ = first_block(maps, 1 - other, lax.axis_index("col"))
    columns = pl.ds(pl.multiple_of(place * BLK, BLK), BLK)
    copy = pltpu.make_async_copy(pieces.at[:, other, :, columns], first, sem)
    copy.start()
    copy.wait()


def cut(maps, pieces):
    return pl.pallas_call(
        cut_kernel,
        out_shape=jax.ShapeDtypeStruct((10, BLK, BLK), F32),
        in_specs=[SMEM, HBM],
        out_specs=VMEM,
        scratch_shapes=[pltpu.SemaphoreType.DMA(())],
        compiler_params=params(4),
        cost_estimate=cost(0, MIB),
        name="cut",
    )(in_hbm(maps), in_hbm(pieces))


def prepare_kernel(
    maps, pivots, front, pieces, first, *refs,
):
    *rests, panel, own, away, table, sending, kept, total, sem = refs
    here_row, here_col = lax.axis_index("row"), lax.axis_index("col")
    side, core = here_row // 4, here_row % 2
    other = 1 - side
    place, found = first_block(maps, side, here_col)
    got_place, _ = first_block(maps, other, here_col)

    def columns(d):
        return pl.ds(pl.multiple_of(d * BLK, BLK), BLK)

    reads = [
        pltpu.make_async_copy(pieces.at[:, other], sending, sem.at[0]),
        pltpu.make_async_copy(pieces.at[:, side, :, columns(place)], kept, sem.at[1]),
        pltpu.make_async_copy(front.at[:, pl.ds(0, BLK)], panel, sem.at[2]),
    ]
    writes = []
    rest_a, rest_b = rests
    parts = (
        (0, 0, rest_a),
        (0, 5, rest_b.at[pl.ds(0, 5)]),
        (1, 0, rest_b.at[pl.ds(5, 10)]),
        (2, 0, rest_b.at[pl.ds(15, 10)]),
        (3, 0, rest_b.at[pl.ds(25, 10)]),
    )
    for n, (j, start, target) in enumerate(parts):
        d = j + (j >= place).astype(jnp.int32)
        source = sending.at[pl.ds(start, target.shape[0]), :, columns(d)]
        writes.append(pltpu.make_async_copy(source, target, sem.at[3 + n]))
    for copy in reads:
        copy.start()
    for kk in range(16):
        table[KEPT_AT + kk] = -1
        table[GOT_AT + kk] = -1
    for m in range(10):
        table[KEPT_AT + maps[side, m * 8 + here_row] // 8] = m
        target = maps[other, m * 8 + here_row] // 8
        table[GOT_AT + target] = m
        table[GOT_ROW + m] = target
    for d in range(5):
        table[KEPT_COL + d] = maps[side, d * 16 + here_col] // 16
    table[GOT_COL] = maps[other, got_place * 16 + here_col] // 16
    for j in range(4):
        d = j + (j >= got_place).astype(jnp.int32)
        table[GOT_COL + 1 + j] = maps[other, d * 16 + here_col] // 16
    table[ROW] = here_row
    table[COL] = here_col
    table[SIDE] = side
    turned = pivots[...].T
    wanted = jnp.concatenate(
        [jnp.where(here_col < 4, turned[:, 4 + k : 5 + k], turned[:, k : k + 1]) for k in range(4)],
        axis=0,
    )
    block, offset = wanted >> 7, wanted & 127
    mine = jnp.where((block & 7) == here_row, (block >> 3) * BLK + offset, -1)
    sent = jnp.full_like(mine, -1)
    for m in range(10):
        hit = (block == maps[side, m * 8 + (here_row ^ 4)]) & (found > 0)
        sent = jnp.where(hit, m * BLK + offset, sent)
    reads[0].wait()
    for copy in writes:
        copy.start()
    reads[1].wait()
    reads[2].wait()

    @pl.when(found > 0)
    def _():
        for m in range(10):
            at = pl.multiple_of(maps[side, m * 8 + here_row] // 8 * BLK, BLK)
            panel[pl.ds(at, BLK), :] += kept[m]

    def rows_of(index, values, base):
        lane = lax.broadcasted_iota(jnp.int32, (PANEL, values.shape[0]), 1) + base
        chosen = jnp.where(lane == index, 1.0, 0.0).astype(BF16)
        both = jnp.concatenate(split(values), axis=1)
        return jnp.dot(chosen, both, preferred_element_type=F32)

    terms = jnp.zeros((PANEL, 2 * BLK), F32)
    for k in range(8):
        terms += rows_of(mine, panel[k * 256 : (k + 1) * 256, :], k * 256)
    for k in range(5):
        values = first[2 * k : 2 * k + 2].reshape(256, BLK)
        terms += rows_of(sent, values, k * 256)
    total[...] = terms[:, :BLK] + terms[:, BLK:]
    own[...] = total[pl.ds(pl.multiple_of(core * 256, 256), 256), :]
    away[...] = total[pl.ds(pl.multiple_of((1 - core) * 256, 256), 256), :]
    for copy in writes:
        copy.wait()


def prepare(maps, pivots, front, pieces, first):
    return pl.pallas_call(
        prepare_kernel,
        out_shape=[
            jax.ShapeDtypeStruct((5, BLK, BLK), F32),
            jax.ShapeDtypeStruct((35, BLK, BLK), F32),
            jax.ShapeDtypeStruct((2048, BLK), F32),
            jax.ShapeDtypeStruct((256, BLK), F32),
            jax.ShapeDtypeStruct((256, BLK), F32),
            jax.ShapeDtypeStruct((64,), jnp.int32),
        ],
        in_specs=[SMEM, VMEM, HBM, HBM, VMEM],
        out_specs=[HBM] * 2 + [VMEM, VMEM, VMEM, SMEM],
        scratch_shapes=[
            pltpu.VMEM((10, BLK, 640), F32),
            pltpu.VMEM((10, BLK, BLK), F32),
            pltpu.VMEM((PANEL, BLK), F32),
            pltpu.SemaphoreType.DMA((8,)),
        ],
        compiler_params=params(24),
        cost_estimate=cost(0, 9 * MIB),
        name="prepare",
    )(in_hbm(maps), in_hbm(pivots.reshape(8, BLK)), in_hbm(front), in_hbm(pieces), first)


def pivot_kernel(mine_half, maps, pivots, front, children, *refs):
    rows, marks, front_list, spread, inverse, child_list, sem, child_sem = refs[-8:]
    rows[...] = jnp.zeros_like(rows)
    marks[...] = refs[0][...] if mine_half else jnp.zeros_like(marks)
    here_row, here_col = lax.axis_index("row"), lax.axis_index("col")
    side, quarter, core = here_row // 4, here_row % 4, here_row % 2
    half = core if mine_half else 1 - core
    spread[...] = jnp.zeros_like(spread)

    def clear(b, carry):
        inverse[b] = -1
        return carry

    lax.fori_loop(0, 128, clear, 0, unroll=16)
    for k in range(20):
        inverse[maps[side, 4 * k + quarter]] = k

    def visit(p, counts):
        pivot = pivots[half * PANEL + p]
        block, offset = pivot >> 7, pivot & 127
        child_block = inverse[block]
        mine = (block & 7) == here_row
        shared = ((block & 3) == quarter) & (child_block >= 0)
        front_list[counts[0]] = (((block >> 3) * BLK + offset) << 9) | p
        child_list[counts[1]] = ((child_block * BLK + offset) << 9) | p
        return counts[0] + mine.astype(jnp.int32), counts[1] + shared.astype(jnp.int32)

    counts = lax.fori_loop(0, PANEL, visit, (jnp.int32(0), jnp.int32(0)), unroll=8)
    front_list[PANEL] = counts[0]
    mark = jnp.full((1, BLK), half + 1, jnp.int32).astype(F32)

    def take_front(n, carry):
        at, p = front_list[n] >> 9, front_list[n] & 511
        pltpu.make_async_copy(front.at[pl.ds(at, 1), :], rows.at[pl.ds(p, 1), :], sem).start()
        marks[pl.ds(at, 1), :] = mark
        return carry

    def take_child(n, carry):
        at, p = child_list[n] >> 9, child_list[n] & 511
        pltpu.make_async_copy(
            children.at[pl.ds(at, 1), :], spread.at[pl.ds(p, 1), :], child_sem
        ).start()
        return carry

    def wait(source, target, semaphore, count):
        def some(size):
            def body(_, carry):
                pltpu.make_async_copy(
                    source.at[pl.ds(0, size), :], target.at[pl.ds(0, size), :], semaphore
                ).wait()
                return carry

            return body

        lax.fori_loop(0, count // 16, some(16), 0)
        lax.fori_loop(0, count % 16, some(1), 0)

    lax.fori_loop(0, counts[0], take_front, 0)
    lax.fori_loop(0, counts[1], take_child, 0)
    wait(front, rows, sem, counts[0])
    wait(children, spread, child_sem, counts[1])
    for d in range(5):
        to = pl.ds(pl.multiple_of(maps[side, d * 16 + here_col] // 16 * BLK, BLK), BLK)
        rows[:, to] += spread[:, d * BLK : (d + 1) * BLK]


def pivot_terms(maps, pivots, front, children, *before):
    mine_half = len(before) > 0
    return pl.pallas_call(
        functools.partial(pivot_kernel, mine_half),
        out_shape=[
            jax.ShapeDtypeStruct((PANEL, 1024), F32),
            jax.ShapeDtypeStruct((2048, BLK), F32),
            jax.ShapeDtypeStruct((PANEL + 1,), jnp.int32),
        ],
        in_specs=[SMEM, SMEM, HBM, HBM] + [VMEM] * len(before),
        out_specs=[VMEM, VMEM, SMEM],
        scratch_shapes=[
            pltpu.VMEM((PANEL, 640), F32),
            pltpu.SMEM((128,), jnp.int32),
            pltpu.SMEM((PANEL + 1,), jnp.int32),
            pltpu.SemaphoreType.DMA(()),
            pltpu.SemaphoreType.DMA(()),
        ],
        compiler_params=params(12),
        cost_estimate=cost(0, 24 * MIB),
        name="pivot_terms_mine" if mine_half else "pivot_terms_other",
    )(in_hbm(maps), in_hbm(pivots), in_hbm(front), in_hbm(children), *before)


def panel_kernel(table, panel, got, top, bottom):
    top[...] = panel[:1024, :]
    bottom[...] = panel[1024:, :]

    @pl.when(table[GOT_COL] == 0)
    def _():
        for kk in range(16):
            m = table[GOT_AT + kk]
            half = top if kk < 8 else bottom
            at = kk % 8 * BLK

            @pl.when(m >= 0)
            def _(half=half, at=at, m=m):
                half[at : at + BLK, :] += got[m]


def whole_panel(table, panel, got):
    shape = jax.ShapeDtypeStruct((1024, BLK), F32)
    return pl.pallas_call(
        panel_kernel,
        out_shape=[shape, shape],
        in_specs=[SMEM, VMEM, VMEM],
        out_specs=[VMEM, VMEM],
        compiler_params=params(12),
        cost_estimate=cost(0, 3 * MIB),
        name="whole_panel",
    )(table, panel, got)


def flips(delta):
    return (delta & 1) ^ (delta >> 1), delta >> 1


def corner_kernel(table, own, swapped, inverses, factor_h, factor_l, cross):
    here_row, here_col = table[ROW], table[COL]
    core, x, y = here_row % 2, here_col % 4, here_col // 4
    mine = (y ^ (y >> 1)) & 1

    def corner(panel, half):
        blocks = []
        for xx in range(4):
            one, three = flips(xx ^ x)
            pair = mine ^ panel
            slot = jnp.where(half == 0, pair | (one << 1) | (three << 2), one | (three << 1) | (pair << 2))
            blocks.append(jnp.where(core == half, own[slot], swapped[slot]))
        return jnp.concatenate(blocks, axis=1)

    for p in range(2):
        factor_h[p], factor_l[p] = split(inverses[p])
    for half in range(2):
        rows = slice(half * 256, (half + 1) * 256)
        factor_h[2, rows, :], factor_l[2, rows, :] = split(corner(1, half))
        cross[rows, :] = dot3(split(corner(0, half)), (factor_h[0], factor_l[0]))


def corners(table, own, swapped, inverses):
    return pl.pallas_call(
        corner_kernel,
        out_shape=[
            jax.ShapeDtypeStruct((3, PANEL, PANEL), BF16),
            jax.ShapeDtypeStruct((3, PANEL, PANEL), BF16),
            jax.ShapeDtypeStruct((PANEL, PANEL), F32),
        ],
        in_specs=[SMEM, VMEM, VMEM, VMEM],
        out_specs=[VMEM] * 3,
        compiler_params=params(20),
        cost_estimate=cost(6 * PANEL**3, 8 * MIB),
        name="corners",
    )(table, own, swapped, inverses)


def factor_kernel(table, own, swapped, factor_h, factor_l, cross, high, low, patch):
    here_row, col = table[ROW], table[COL]
    core, slot = here_row % 2, col % 4
    inside = lax.broadcasted_iota(jnp.int32, (PANEL, 1024), 1) < BLK

    def mine(x):
        out = x[:, :BLK]
        for s in range(1, 4):
            out = jnp.where(slot == s, x[:, s * BLK : (s + 1) * BLK], out)
        return out

    def begin_with(block, x):
        return jnp.concatenate([block, x[:, BLK:]], axis=1)

    def factor(n):
        return factor_h[n], factor_l[n]

    def factor_columns(n):
        return mine(factor_h[n].astype(F32)) + mine(factor_l[n].astype(F32))

    first = jnp.where(core == 0, own[...], swapped[...])
    first = jnp.where(inside & (col < 4), 0.0, first)
    second = jnp.where(core == 0, swapped[...], own[...])
    second = second - dot3(split(cross[...]), split(first))
    patch[...] = begin_with(jnp.where(col < 4, mine(cross[...]), second[:, :BLK]), second)
    second = jnp.where(inside & (col < 8), 0.0, second)
    right = dot3(factor(1), split(second))
    in_second = (col >= 4) & (col < 8)
    right = begin_with(jnp.where(in_second, factor_columns(1), right[:, :BLK]), right)
    terms = split(right)
    high[PANEL:], low[PANEL:] = terms
    first = jnp.where(inside & (col < 8), 0.0, first)
    left = dot3(factor(0), split(first - dot3(factor(2), terms)))
    left = begin_with(jnp.where(col < 4, factor_columns(0), left[:, :BLK]), left)
    high[:PANEL], low[:PANEL] = split(left)


def right_factor(table, own, swapped, factors, cross):
    shape = jax.ShapeDtypeStruct((1024, 1024), BF16)
    return pl.pallas_call(
        factor_kernel,
        out_shape=[shape, shape, jax.ShapeDtypeStruct((PANEL, 1024), F32)],
        in_specs=[SMEM] + [VMEM] * 5,
        out_specs=[VMEM] * 3,
        compiler_params=params(24),
        cost_estimate=cost(4 * 6 * PANEL * PANEL * 1024, 14 * MIB),
        name="right_factor",
    )(table, own, swapped, *factors, cross)


def block_at(base, half, t, s):
    return jnp.maximum(s[base + half * 8 + t], 0)


def extend_kernel(counts, table, front, *refs):
    out, refs = refs[-1], refs[:-1]
    kept, *got = (refs[2 * k : 2 * k + 2] for k in range(1 + len(counts)))
    step = pl.program_id(0)
    out[...] = front[...]
    for half in range(2):

        @pl.when(table[KEPT_AT + half * 8 + step] >= 0)
        def _(half=half):
            for d in range(5):
                to = pl.ds(pl.multiple_of(table[KEPT_COL + d] * BLK, BLK), BLK)
                out[half, :, to] += kept[half][0, 0, :, d * BLK : (d + 1) * BLK]

        m = table[GOT_AT + half * 8 + step]
        for j, count in enumerate(counts):

            @pl.when((m >= 0) & (m < count))
            def _(half=half, j=j):
                to = pl.ds(pl.multiple_of(table[GOT_COL + j] * BLK, BLK), BLK)
                out[half, :, to] += got[j][half][0]


def extend(table, front, pieces, got):
    def kept_at(half):
        return lambda t, s: (block_at(KEPT_AT, half, t, s), s[SIDE], 0, 0)

    def got_at(half, count):
        return lambda t, s: (jnp.minimum(block_at(GOT_AT, half, t, s), count - 1), 0, 0)

    tile = pl.BlockSpec((2, BLK, 1024), lambda t, s: (0, t, 0))
    kept_specs = [pl.BlockSpec((1, 1, BLK, 640), kept_at(half)) for half in range(2)]
    got_specs = [
        pl.BlockSpec((1, BLK, BLK), got_at(half, g.shape[0])) for g in got for half in range(2)
    ]
    return pl.pallas_call(
        functools.partial(extend_kernel, [g.shape[0] for g in got]),
        out_shape=pltpu.HBM((2, 1024, 1024), F32),
        grid_spec=pltpu.PrefetchScalarGridSpec(
            num_scalar_prefetch=1,
            grid=(8,),
            in_specs=[tile, *kept_specs, *got_specs],
            out_specs=tile,
        ),
        compiler_params=params(20),
        cost_estimate=cost(0, MIB),
        name="extend",
    )(table, in_hbm(front.reshape(2, 1024, 1024)), *[in_hbm(pieces)] * 2, *[g for g in got for _ in range(2)])


ORDERS = ((1, 3, 4, 12), (3, 1, 12, 4)), ((4, 12, 1, 3), (12, 4, 3, 1))


def update_kernel(table, front, *refs):
    blocks = refs[:4], refs[4:8]
    right_h, right_l, marks, out, panels = refs[8:]
    step = pl.program_id(0)
    span = pl.ds(pl.multiple_of(step % 2 * 256, 256), 256)
    col, core = table[COL], table[ROW] % 2

    def assemble(which):
        held, came, held_far, came_far = blocks[which]
        for c in range(16):
            one_x, three_x = flips((c ^ col) & 3)
            one_y, three_y = flips((c ^ col) >> 2)
            bits = {1: one_x, 3: three_x, 4: one_y, 12: three_y}
            even, odd = (ORDERS[q][which] for q in range(2))
            flip = [jnp.where(core == 0, bits[e], bits[o]) for e, o in zip(even, odd)]
            slot = flip[0] | (flip[1] << 1)
            later, far = flip[2] == 1, flip[3] == 1
            near_block = jnp.where(later, came[slot, span, :], held[slot, span, :])
            far_block = jnp.where(later, came_far[slot, span, :], held_far[slot, span, :])
            block = jnp.where(far, far_block, near_block)
            y, x = c // 4, c % 4
            rows = slice(0, 256) if y < 2 else slice(256, PANEL)
            first = min(y, 3 - y) * PANEL + x * BLK
            columns = slice(first, first + BLK)
            panels[0, rows, columns], panels[1, rows, columns] = split(block)

    for which in range(2):
        pl.when(step // 2 == which)(functools.partial(assemble, which))

    active = marks[...] == 0
    for piece in range(4):
        wide = slice(piece * 256, (piece + 1) * 256)
        change = dot3((panels[0], panels[1]), (right_h[:, wide], right_l[:, wide]))
        change = change.reshape(2, 256, 256)
        for j in range(2):
            columns = slice(piece * 256 + j * BLK, piece * 256 + (j + 1) * BLK)
            before, part = front[:, :, columns], change[:, :, j * BLK : (j + 1) * BLK]
            after = before - part
            if piece == 0 and j == 0:
                after = jnp.where(col < 8, part, after)
            out[:, :, columns] = jnp.where(active, after, before)


def update(table, front, blocks, right, marks):
    tile = pl.BlockSpec((2, 256, 1024), lambda t, s: (0, t, 0))
    return pl.pallas_call(
        update_kernel,
        out_shape=pltpu.HBM((2, 1024, 1024), F32),
        grid_spec=pltpu.PrefetchScalarGridSpec(
            num_scalar_prefetch=1,
            grid=(4,),
            in_specs=[
                tile,
                *[VMEM] * 10,
                pl.BlockSpec((2, 256, BLK), lambda t, s: (0, t, 0)),
            ],
            out_specs=tile,
            scratch_shapes=[pltpu.VMEM((2, PANEL, 1024), BF16)],
        ),
        compiler_params=params(24),
        cost_estimate=cost(6 * 2048 * 1024 * 1024, 32 * MIB),
        name="update",
    )(table, in_hbm(front), *blocks[0], *blocks[1], *right, marks.reshape(2, 1024, BLK))


def finish_kernel(
    table, list_other, list_mine, front, got, patch,
    out, held, read_sem, write_sem, sem,
):
    del front
    core = table[ROW] % 2
    copies = []
    places = [(1, m) for m in range(5, 10)] + [(j, m) for j in (2, 3, 4) for m in range(10)]
    for n, (column, m) in enumerate(places):
        columns = pl.ds(pl.multiple_of(table[GOT_COL + column] * BLK, BLK), BLK)
        rows = pl.ds(pl.multiple_of(table[GOT_ROW + m] * BLK, BLK), BLK)
        there, here = out.at[rows, columns], held.at[n]
        read = pltpu.make_async_copy(there, here, read_sem.at[n])
        write = pltpu.make_async_copy(here, there, write_sem.at[n])
        copies.append((read, write))
    for read, _ in copies:
        read.start()
    for n, (read, write) in enumerate(copies):
        read.wait()
        held[n] += got[n]
        write.start()
    for _, write in copies:
        write.wait()

    def entry(n):
        return jnp.where(core == 0, list_other[n], list_mine[n])

    def place(n, carry):
        at, p = entry(n) >> 9, entry(n) & 511
        pltpu.make_async_copy(patch.at[pl.ds(p, 1), :], out.at[pl.ds(at, 1), :], sem).start()
        return carry

    def wait(_, carry):
        pltpu.make_async_copy(patch.at[pl.ds(0, 1), :], out.at[pl.ds(0, 1), :], sem).wait()
        return carry

    lax.fori_loop(0, entry(PANEL), place, 0)
    lax.fori_loop(0, entry(PANEL), wait, 0)


def finish(table, lists, front, got, patch):
    return pl.pallas_call(
        finish_kernel,
        out_shape=jax.ShapeDtypeStruct((2048, 1024), F32),
        in_specs=[SMEM, SMEM, SMEM, HBM] + [VMEM] * 2,
        out_specs=HBM,
        scratch_shapes=[
            pltpu.VMEM((35, BLK, BLK), F32),
            pltpu.SemaphoreType.DMA((35,)),
            pltpu.SemaphoreType.DMA((35,)),
            pltpu.SemaphoreType.DMA(()),
        ],
        input_output_aliases={3: 0},
        compiler_params=params(12),
        cost_estimate=cost(0, 8 * MIB),
        name="finish",
    )(table, *lists, front, got, patch)


def swap(block, axis, partner):
    count = lax.axis_size(axis)
    return lax.ppermute(block, axis, [(i, partner(i)) for i in range(count)])


def fold(block, near):
    came = lax.ppermute(block[1], "col", [(c, c ^ 12) for c in range(8)])
    return jnp.where(near, block[0], came)


def local(front, children, child_maps, pivots, diag_inverses):
    here_row, here_col = lax.axis_index("row"), lax.axis_index("col")
    chip = here_row >> 1
    together = lax.optimization_barrier
    pieces = children.reshape(10, 2, BLK, 640)

    def by_row(block, mask):
        return swap(block, "row", lambda i: i ^ mask)

    def by_col(block, mask):
        return swap(block, "col", lambda i: i ^ mask)

    bits = (chip ^ (chip >> 1)) & 1, chip >> 1
    rings = [[(r, r ^ ((2, 6), (6, 2))[r % 2][k]) for r in range(8)] for k in range(2)]
    low = [jnp.where(here_row & 1 == 0, bits[k], bits[1 - k]) == 0 for k in range(2)]
    pivots, near, low = together((pivots, here_col < 8, low))

    def halve(part, step):
        size = part.shape[0] // 2
        leave = jnp.where(low[step], part[size:], part[:size])
        stay = jnp.where(low[step], part[:size], part[size:])
        return stay + lax.ppermute(leave, "row", rings[step])

    def double(part, step):
        came = lax.ppermute(part, "row", rings[step])
        first, second = jnp.where(low[step], part, came), jnp.where(low[step], came, part)
        return jnp.concatenate([first, second], axis=0)

    def gather_step(block, which, step):
        route = [
            (r * 16 + c, r * 16 + (c ^ ORDERS[r % 2][which][step]))
            for r in range(8)
            for c in range(16)
        ]
        return lax.ppermute(block, ("row", "col"), route)

    first = cut(child_maps, pieces)
    got0 = by_row(first, 4)
    *rest, panel, corner, away, table = prepare(child_maps, pivots, front, pieces, first)
    rest_a, rest_b = rest
    corner = corner + by_row(away, 1)
    corner = corner + (by_row(corner, 2) + (by_row(corner, 6) + by_row(corner, 4)))
    away_rows, marks, list_other = pivot_terms(child_maps, pivots, front, children)
    got0, away_rows, rest_a, marks, corner = together((got0, away_rows, rest_a, marks, corner))

    top, bottom = whole_panel(table, panel, got0)
    mine = fold((top, bottom), near)
    corner = fold((corner, corner), near)[None]
    got_a = by_row(rest_a, 4)
    own_rows, marks, list_mine = pivot_terms(child_maps, pivots, front, children, marks)
    total = own_rows + by_row(away_rows, 1)
    mine, corner, total, got_a, rest_b = together((mine, corner, total, got_a, rest_b))

    def corner_step(block, step):
        masks = ((4, 1, 3), (1, 3, 4))
        route = [
            (r * 16 + c, r * 16 + (c ^ masks[r % 2][step])) for r in range(8) for c in range(16)
        ]
        return jnp.concatenate([block, lax.ppermute(block, ("row", "col"), route)], axis=0)

    held = [mine[None, :PANEL], mine[None, PANEL:]]
    for k in range(2):
        came = [gather_step(held[w], w, k) for w in range(2)]
        held = [jnp.concatenate([h, c], axis=0) for h, c in zip(held, came)]
        corner = corner_step(corner, k)
        total = halve(total, k)
        if k == 1:
            total = double(total, 1)
        if k == 0:
            front = extend(table, front, pieces, (got0, got_a))
        held, corner, total, front = together((held, corner, total, front))
    came = [gather_step(held[w], w, 2) for w in range(2)]
    corner = corner_step(corner, 2)
    total = double(total, 0)
    came, corner, total, rest_b = together((came, corner, total, rest_b))
    got_b = by_row(rest_b, 4)
    held_far = [gather_step(held[w], w, 3) for w in range(2)]
    came_far = [gather_step(came[w], w, 3) for w in range(2)]
    *factors, cross = corners(table, corner, by_row(corner, 1), diag_inverses)
    *right, patch = right_factor(table, total, by_row(total, 1), factors, cross)
    held_far, came_far, right, patch = together((held_far, came_far, right, patch))
    blocks = [(held[w], came[w], held_far[w], came_far[w]) for w in range(2)]
    front = update(table, front, blocks, right, marks).reshape(2048, 1024)
    return finish(table, (list_other, list_mine), front, got_b, patch)


def solution(mesh):
    return jax.shard_map(
        local,
        mesh=mesh,
        in_specs=(P("row", "col"), P("row", "col"), P(), P(), P()),
        out_specs=P("row", "col"),
        check_vma=False,
    )
```

```python
import functools

import jax
import jax.numpy as jnp
from jax import lax
from jax.experimental import pallas as pl
from jax.experimental.pallas import tpu as pltpu
from jax.sharding import PartitionSpec as P

BLK = 128
PANEL = 512
MIB = 1 << 20
F32 = jnp.float32
BF16 = jnp.bfloat16
SMEM = pl.BlockSpec(memory_space=pltpu.SMEM)
VMEM = pl.BlockSpec(memory_space=pltpu.VMEM)
HBM = pl.BlockSpec(memory_space=pltpu.HBM)
KEPT_AT = 0
GOT_AT = 16
KEPT_COL = 32
GOT_COL = 40
ROW, COL, SIDE = 48, 49, 50
GOT_ROW = 52


def split(x):
    high = x.astype(BF16)
    return high, (x - high.astype(F32)).astype(BF16)


def dot3(a, b):
    rows = a[0].shape[0]
    both = jnp.dot(jnp.concatenate(a, axis=0), b[0], preferred_element_type=F32)
    return both[:rows] + (both[rows:] + jnp.dot(a[0], b[1], preferred_element_type=F32))


def params(mib):
    return pltpu.CompilerParams(vmem_limit_bytes=mib * MIB)


def in_hbm(x):
    return pltpu.with_memory_space_constraint(x, pltpu.HBM)


def cost(flops, moved):
    return pl.CostEstimate(flops=flops, bytes_accessed=moved, transcendentals=0)


def first_block(maps, child, here_col):
    place, found = jnp.int32(0), jnp.int32(0)
    for d in range(5):
        hit = (maps[child, d * 16 + here_col] // 16 == 0).astype(jnp.int32)
        place, found = place + d * hit, found + hit
    return place, found


def cut_kernel(maps, pieces, first, sem):
    other = 1 - lax.axis_index("row") // 4
    place, _ = first_block(maps, 1 - other, lax.axis_index("col"))
    columns = pl.ds(pl.multiple_of(place * BLK, BLK), BLK)
    copy = pltpu.make_async_copy(pieces.at[:, other, :, columns], first, sem)
    copy.start()
    copy.wait()


def cut(maps, pieces):
    return pl.pallas_call(
        cut_kernel,
        out_shape=jax.ShapeDtypeStruct((10, BLK, BLK), F32),
        in_specs=[SMEM, HBM],
        out_specs=VMEM,
        scratch_shapes=[pltpu.SemaphoreType.DMA(())],
        compiler_params=params(4),
        cost_estimate=cost(0, MIB),
        name="cut",
    )(in_hbm(maps), in_hbm(pieces))


def prepare_kernel(
    maps, pivots, front, pieces, first, *refs,
):
    *rests, panel, own, away, table, sending, kept, total, sem = refs
    here_row, here_col = lax.axis_index("row"), lax.axis_index("col")
    side, core = here_row // 4, here_row % 2
    other = 1 - side
    place, found = first_block(maps, side, here_col)
    got_place, _ = first_block(maps, other, here_col)

    def columns(d):
        return pl.ds(pl.multiple_of(d * BLK, BLK), BLK)

    reads = [
        pltpu.make_async_copy(pieces.at[:, other], sending, sem.at[0]),
        pltpu.make_async_copy(pieces.at[:, side, :, columns(place)], kept, sem.at[1]),
        pltpu.make_async_copy(front.at[:, pl.ds(0, BLK)], panel, sem.at[2]),
    ]
    writes = []
    rest_a, rest_b = rests
    parts = (
        (0, 0, rest_a),
        (1, 0, rest_b.at[pl.ds(0, 10)]),
        (2, 0, rest_b.at[pl.ds(10, 10)]),
        (3, 0, rest_b.at[pl.ds(20, 10)]),
    )
    for n, (j, start, target) in enumerate(parts):
        d = j + (j >= place).astype(jnp.int32)
        source = sending.at[pl.ds(start, target.shape[0]), :, columns(d)]
        writes.append(pltpu.make_async_copy(source, target, sem.at[3 + n]))
    for copy in reads:
        copy.start()
    for kk in range(16):
        table[KEPT_AT + kk] = -1
        table[GOT_AT + kk] = -1
    for m in range(10):
        table[KEPT_AT + maps[side, m * 8 + here_row] // 8] = m
        target = maps[other, m * 8 + here_row] // 8
        table[GOT_AT + target] = m
        table[GOT_ROW + m] = target
    for d in range(5):
        table[KEPT_COL + d] = maps[side, d * 16 + here_col] // 16
    table[GOT_COL] = maps[other, got_place * 16 + here_col] // 16
    for j in range(4):
        d = j + (j >= got_place).astype(jnp.int32)
        table[GOT_COL + 1 + j] = maps[other, d * 16 + here_col] // 16
    table[ROW] = here_row
    table[COL] = here_col
    table[SIDE] = side
    turned = pivots[...].T
    wanted = jnp.concatenate(
        [jnp.where(here_col < 4, turned[:, 4 + k : 5 + k], turned[:, k : k + 1]) for k in range(4)],
        axis=0,
    )
    block, offset = wanted >> 7, wanted & 127
    mine = jnp.where((block & 7) == here_row, (block >> 3) * BLK + offset, -1)
    sent = jnp.full_like(mine, -1)
    for m in range(10):
        hit = (block == maps[side, m * 8 + (here_row ^ 4)]) & (found > 0)
        sent = jnp.where(hit, m * BLK + offset, sent)
    reads[0].wait()
    for copy in writes:
        copy.start()
    reads[1].wait()
    reads[2].wait()

    @pl.when(found > 0)
    def _():
        for m in range(10):
            at = pl.multiple_of(maps[side, m * 8 + here_row] // 8 * BLK, BLK)
            panel[pl.ds(at, BLK), :] += kept[m]

    def rows_of(index, values, base):
        lane = lax.broadcasted_iota(jnp.int32, (PANEL, values.shape[0]), 1) + base
        chosen = jnp.where(lane == index, 1.0, 0.0).astype(BF16)
        both = jnp.concatenate(split(values), axis=1)
        return jnp.dot(chosen, both, preferred_element_type=F32)

    terms = jnp.zeros((PANEL, 2 * BLK), F32)
    for k in range(8):
        terms += rows_of(mine, panel[k * 256 : (k + 1) * 256, :], k * 256)
    for k in range(5):
        values = first[2 * k : 2 * k + 2].reshape(256, BLK)
        terms += rows_of(sent, values, k * 256)
    total[...] = terms[:, :BLK] + terms[:, BLK:]
    own[...] = total[pl.ds(pl.multiple_of(core * 256, 256), 256), :]
    away[...] = total[pl.ds(pl.multiple_of((1 - core) * 256, 256), 256), :]
    for copy in writes:
        copy.wait()


def prepare(maps, pivots, front, pieces, first):
    return pl.pallas_call(
        prepare_kernel,
        out_shape=[
            jax.ShapeDtypeStruct((10, BLK, BLK), F32),
            jax.ShapeDtypeStruct((30, BLK, BLK), F32),
            jax.ShapeDtypeStruct((2048, BLK), F32),
            jax.ShapeDtypeStruct((256, BLK), F32),
            jax.ShapeDtypeStruct((256, BLK), F32),
            jax.ShapeDtypeStruct((64,), jnp.int32),
        ],
        in_specs=[SMEM, VMEM, HBM, HBM, VMEM],
        out_specs=[HBM] * 2 + [VMEM, VMEM, VMEM, SMEM],
        scratch_shapes=[
            pltpu.VMEM((10, BLK, 640), F32),
            pltpu.VMEM((10, BLK, BLK), F32),
            pltpu.VMEM((PANEL, BLK), F32),
            pltpu.SemaphoreType.DMA((7,)),
        ],
        compiler_params=params(24),
        cost_estimate=cost(0, 9 * MIB),
        name="prepare",
    )(in_hbm(maps), in_hbm(pivots.reshape(8, BLK)), in_hbm(front), in_hbm(pieces), first)


def pivot_kernel(mine_half, maps, pivots, front, children, *refs):
    rows, marks, front_list, spread, inverse, child_list, sem, child_sem = refs[-8:]
    rows[...] = jnp.zeros_like(rows)
    marks[...] = refs[0][...] if mine_half else jnp.zeros_like(marks)
    here_row, here_col = lax.axis_index("row"), lax.axis_index("col")
    side, quarter, core = here_row // 4, here_row % 4, here_row % 2
    half = core if mine_half else 1 - core
    spread[...] = jnp.zeros_like(spread)

    def clear(b, carry):
        inverse[b] = -1
        return carry

    lax.fori_loop(0, 128, clear, 0, unroll=16)
    for k in range(20):
        inverse[maps[side, 4 * k + quarter]] = k

    def visit(p, counts):
        pivot = pivots[half * PANEL + p]
        block, offset = pivot >> 7, pivot & 127
        child_block = inverse[block]
        mine = (block & 7) == here_row
        shared = ((block & 3) == quarter) & (child_block >= 0)
        front_list[counts[0]] = (((block >> 3) * BLK + offset) << 9) | p
        child_list[counts[1]] = ((child_block * BLK + offset) << 9) | p
        return counts[0] + mine.astype(jnp.int32), counts[1] + shared.astype(jnp.int32)

    counts = lax.fori_loop(0, PANEL, visit, (jnp.int32(0), jnp.int32(0)), unroll=8)
    front_list[PANEL] = counts[0]
    mark = jnp.full((1, BLK), half + 1, jnp.int32).astype(F32)

    def take_front(n, carry):
        at, p = front_list[n] >> 9, front_list[n] & 511
        pltpu.make_async_copy(front.at[pl.ds(at, 1), :], rows.at[pl.ds(p, 1), :], sem).start()
        marks[pl.ds(at, 1), :] = mark
        return carry

    def take_child(n, carry):
        at, p = child_list[n] >> 9, child_list[n] & 511
        pltpu.make_async_copy(
            children.at[pl.ds(at, 1), :], spread.at[pl.ds(p, 1), :], child_sem
        ).start()
        return carry

    def wait(source, target, semaphore, count):
        def some(size):
            def body(_, carry):
                pltpu.make_async_copy(
                    source.at[pl.ds(0, size), :], target.at[pl.ds(0, size), :], semaphore
                ).wait()
                return carry

            return body

        lax.fori_loop(0, count // 16, some(16), 0)
        lax.fori_loop(0, count % 16, some(1), 0)

    lax.fori_loop(0, counts[0], take_front, 0)
    lax.fori_loop(0, counts[1], take_child, 0)
    wait(front, rows, sem, counts[0])
    wait(children, spread, child_sem, counts[1])
    for d in range(5):
        to = pl.ds(pl.multiple_of(maps[side, d * 16 + here_col] // 16 * BLK, BLK), BLK)
        rows[:, to] += spread[:, d * BLK : (d + 1) * BLK]


def pivot_terms(maps, pivots, front, children, *before):
    mine_half = len(before) > 0
    return pl.pallas_call(
        functools.partial(pivot_kernel, mine_half),
        out_shape=[
            jax.ShapeDtypeStruct((PANEL, 1024), F32),
            jax.ShapeDtypeStruct((2048, BLK), F32),
            jax.ShapeDtypeStruct((PANEL + 1,), jnp.int32),
        ],
        in_specs=[SMEM, SMEM, HBM, HBM] + [VMEM] * len(before),
        out_specs=[VMEM, VMEM, SMEM],
        scratch_shapes=[
            pltpu.VMEM((PANEL, 640), F32),
            pltpu.SMEM((128,), jnp.int32),
            pltpu.SMEM((PANEL + 1,), jnp.int32),
            pltpu.SemaphoreType.DMA(()),
            pltpu.SemaphoreType.DMA(()),
        ],
        compiler_params=params(12),
        cost_estimate=cost(0, 24 * MIB),
        name="pivot_terms_mine" if mine_half else "pivot_terms_other",
    )(in_hbm(maps), in_hbm(pivots), in_hbm(front), in_hbm(children), *before)


def panel_kernel(table, panel, got, top, bottom):
    top[...] = panel[:1024, :]
    bottom[...] = panel[1024:, :]

    @pl.when(table[GOT_COL] == 0)
    def _():
        for kk in range(16):
            m = table[GOT_AT + kk]
            half = top if kk < 8 else bottom
            at = kk % 8 * BLK

            @pl.when(m >= 0)
            def _(half=half, at=at, m=m):
                half[at : at + BLK, :] += got[m]


def whole_panel(table, panel, got):
    shape = jax.ShapeDtypeStruct((1024, BLK), F32)
    return pl.pallas_call(
        panel_kernel,
        out_shape=[shape, shape],
        in_specs=[SMEM, VMEM, VMEM],
        out_specs=[VMEM, VMEM],
        compiler_params=params(12),
        cost_estimate=cost(0, 3 * MIB),
        name="whole_panel",
    )(table, panel, got)


def flips(delta):
    return (delta & 1) ^ (delta >> 1), delta >> 1


def corner_kernel(table, own, swapped, inverses, factor_h, factor_l, cross):
    here_row, here_col = table[ROW], table[COL]
    core, x, y = here_row % 2, here_col % 4, here_col // 4
    mine = (y ^ (y >> 1)) & 1

    def corner(panel, half):
        blocks = []
        for xx in range(4):
            one, three = flips(xx ^ x)
            pair = mine ^ panel
            slot = jnp.where(half == 0, pair | (one << 1) | (three << 2), one | (three << 1) | (pair << 2))
            blocks.append(jnp.where(core == half, own[slot], swapped[slot]))
        return jnp.concatenate(blocks, axis=1)

    for p in range(2):
        factor_h[p], factor_l[p] = split(inverses[p])
    for half in range(2):
        rows = slice(half * 256, (half + 1) * 256)
        factor_h[2, rows, :], factor_l[2, rows, :] = split(corner(1, half))
        cross[rows, :] = dot3(split(corner(0, half)), (factor_h[0], factor_l[0]))


def corners(table, own, swapped, inverses):
    return pl.pallas_call(
        corner_kernel,
        out_shape=[
            jax.ShapeDtypeStruct((3, PANEL, PANEL), BF16),
            jax.ShapeDtypeStruct((3, PANEL, PANEL), BF16),
            jax.ShapeDtypeStruct((PANEL, PANEL), F32),
        ],
        in_specs=[SMEM, VMEM, VMEM, VMEM],
        out_specs=[VMEM] * 3,
        compiler_params=params(20),
        cost_estimate=cost(6 * PANEL**3, 8 * MIB),
        name="corners",
    )(table, own, swapped, inverses)


def factor_kernel(table, own, swapped, factor_h, factor_l, cross, high, low, patch):
    here_row, col = table[ROW], table[COL]
    core, slot = here_row % 2, col % 4
    inside = lax.broadcasted_iota(jnp.int32, (PANEL, 1024), 1) < BLK

    def mine(x):
        out = x[:, :BLK]
        for s in range(1, 4):
            out = jnp.where(slot == s, x[:, s * BLK : (s + 1) * BLK], out)
        return out

    def begin_with(block, x):
        return jnp.concatenate([block, x[:, BLK:]], axis=1)

    def factor(n):
        return factor_h[n], factor_l[n]

    def factor_columns(n):
        return mine(factor_h[n].astype(F32)) + mine(factor_l[n].astype(F32))

    first = jnp.where(core == 0, own[...], swapped[...])
    first = jnp.where(inside & (col < 4), 0.0, first)
    second = jnp.where(core == 0, swapped[...], own[...])
    second = second - dot3(split(cross[...]), split(first))
    patch[...] = begin_with(jnp.where(col < 4, mine(cross[...]), second[:, :BLK]), second)
    second = jnp.where(inside & (col < 8), 0.0, second)
    right = dot3(factor(1), split(second))
    in_second = (col >= 4) & (col < 8)
    right = begin_with(jnp.where(in_second, factor_columns(1), right[:, :BLK]), right)
    terms = split(right)
    high[PANEL:], low[PANEL:] = terms
    first = jnp.where(inside & (col < 8), 0.0, first)
    left = dot3(factor(0), split(first - dot3(factor(2), terms)))
    left = begin_with(jnp.where(col < 4, factor_columns(0), left[:, :BLK]), left)
    high[:PANEL], low[:PANEL] = split(left)


def right_factor(table, own, swapped, factors, cross):
    shape = jax.ShapeDtypeStruct((1024, 1024), BF16)
    return pl.pallas_call(
        factor_kernel,
        out_shape=[shape, shape, jax.ShapeDtypeStruct((PANEL, 1024), F32)],
        in_specs=[SMEM] + [VMEM] * 5,
        out_specs=[VMEM] * 3,
        compiler_params=params(24),
        cost_estimate=cost(4 * 6 * PANEL * PANEL * 1024, 14 * MIB),
        name="right_factor",
    )(table, own, swapped, *factors, cross)


def block_at(base, half, t, s):
    return jnp.maximum(s[base + half * 8 + t], 0)


def extend_kernel(counts, table, front, *refs):
    out, refs = refs[-1], refs[:-1]
    kept, *got = (refs[2 * k : 2 * k + 2] for k in range(1 + len(counts)))
    step = pl.program_id(0)
    out[...] = front[...]
    for half in range(2):

        @pl.when(table[KEPT_AT + half * 8 + step] >= 0)
        def _(half=half):
            for d in range(5):
                to = pl.ds(pl.multiple_of(table[KEPT_COL + d] * BLK, BLK), BLK)
                out[half, :, to] += kept[half][0, 0, :, d * BLK : (d + 1) * BLK]

        m = table[GOT_AT + half * 8 + step]
        for j, count in enumerate(counts):

            @pl.when((m >= 0) & (m < count))
            def _(half=half, j=j):
                to = pl.ds(pl.multiple_of(table[GOT_COL + j] * BLK, BLK), BLK)
                out[half, :, to] += got[j][half][0]


def extend(table, front, pieces, got):
    def kept_at(half):
        return lambda t, s: (block_at(KEPT_AT, half, t, s), s[SIDE], 0, 0)

    def got_at(half, count):
        return lambda t, s: (jnp.minimum(block_at(GOT_AT, half, t, s), count - 1), 0, 0)

    tile = pl.BlockSpec((2, BLK, 1024), lambda t, s: (0, t, 0))
    kept_specs = [pl.BlockSpec((1, 1, BLK, 640), kept_at(half)) for half in range(2)]
    got_specs = [
        pl.BlockSpec((1, BLK, BLK), got_at(half, g.shape[0])) for g in got for half in range(2)
    ]
    return pl.pallas_call(
        functools.partial(extend_kernel, [g.shape[0] for g in got]),
        out_shape=pltpu.HBM((2, 1024, 1024), F32),
        grid_spec=pltpu.PrefetchScalarGridSpec(
            num_scalar_prefetch=1,
            grid=(8,),
            in_specs=[tile, *kept_specs, *got_specs],
            out_specs=tile,
        ),
        compiler_params=params(20),
        cost_estimate=cost(0, MIB),
        name="extend",
    )(table, in_hbm(front.reshape(2, 1024, 1024)), *[in_hbm(pieces)] * 2, *[g for g in got for _ in range(2)])


ORDERS = ((1, 3, 4, 12), (3, 1, 12, 4)), ((4, 12, 1, 3), (12, 4, 3, 1))


def update_kernel(table, front, *refs):
    blocks = refs[:4], refs[4:8]
    right_h, right_l, marks, out, panels = refs[8:]
    step = pl.program_id(0)
    span = pl.ds(pl.multiple_of(step % 2 * 256, 256), 256)
    col, core = table[COL], table[ROW] % 2

    def assemble(which):
        held, came, held_far, came_far = blocks[which]
        for c in range(16):
            one_x, three_x = flips((c ^ col) & 3)
            one_y, three_y = flips((c ^ col) >> 2)
            bits = {1: one_x, 3: three_x, 4: one_y, 12: three_y}
            even, odd = (ORDERS[q][which] for q in range(2))
            flip = [jnp.where(core == 0, bits[e], bits[o]) for e, o in zip(even, odd)]
            slot = flip[0] | (flip[1] << 1)
            later, far = flip[2] == 1, flip[3] == 1
            near_block = jnp.where(later, came[slot, span, :], held[slot, span, :])
            far_block = jnp.where(later, came_far[slot, span, :], held_far[slot, span, :])
            block = jnp.where(far, far_block, near_block)
            y, x = c // 4, c % 4
            rows = slice(0, 256) if y < 2 else slice(256, PANEL)
            first = min(y, 3 - y) * PANEL + x * BLK
            columns = slice(first, first + BLK)
            panels[0, rows, columns], panels[1, rows, columns] = split(block)

    for which in range(2):
        pl.when(step // 2 == which)(functools.partial(assemble, which))

    active = marks[...] == 0
    for piece in range(4):
        wide = slice(piece * 256, (piece + 1) * 256)
        change = dot3((panels[0], panels[1]), (right_h[:, wide], right_l[:, wide]))
        change = change.reshape(2, 256, 256)
        for j in range(2):
            columns = slice(piece * 256 + j * BLK, piece * 256 + (j + 1) * BLK)
            before, part = front[:, :, columns], change[:, :, j * BLK : (j + 1) * BLK]
            after = before - part
            if piece == 0 and j == 0:
                after = jnp.where(col < 8, part, after)
            out[:, :, columns] = jnp.where(active, after, before)


def update(table, front, blocks, right, marks):
    tile = pl.BlockSpec((2, 256, 1024), lambda t, s: (0, t, 0))
    return pl.pallas_call(
        update_kernel,
        out_shape=pltpu.HBM((2, 1024, 1024), F32),
        grid_spec=pltpu.PrefetchScalarGridSpec(
            num_scalar_prefetch=1,
            grid=(4,),
            in_specs=[
                tile,
                *[VMEM] * 10,
                pl.BlockSpec((2, 256, BLK), lambda t, s: (0, t, 0)),
            ],
            out_specs=tile,
            scratch_shapes=[pltpu.VMEM((2, PANEL, 1024), BF16)],
        ),
        compiler_params=params(24),
        cost_estimate=cost(6 * 2048 * 1024 * 1024, 32 * MIB),
        name="update",
    )(table, in_hbm(front), *blocks[0], *blocks[1], *right, marks.reshape(2, 1024, BLK))


def finish_kernel(
    table, list_other, list_mine, front, got, patch,
    out, held, read_sem, write_sem, sem,
):
    del front
    core = table[ROW] % 2
    copies = []
    places = [(j, m) for j in (2, 3, 4) for m in range(10)]
    for n, (column, m) in enumerate(places):
        columns = pl.ds(pl.multiple_of(table[GOT_COL + column] * BLK, BLK), BLK)
        rows = pl.ds(pl.multiple_of(table[GOT_ROW + m] * BLK, BLK), BLK)
        there, here = out.at[rows, columns], held.at[n]
        read = pltpu.make_async_copy(there, here, read_sem.at[n])
        write = pltpu.make_async_copy(here, there, write_sem.at[n])
        copies.append((read, write))
    for read, _ in copies:
        read.start()
    for n, (read, write) in enumerate(copies):
        read.wait()
        held[n] += got[n]
        write.start()
    for _, write in copies:
        write.wait()

    def entry(n):
        return jnp.where(core == 0, list_other[n], list_mine[n])

    def place(n, carry):
        at, p = entry(n) >> 9, entry(n) & 511
        pltpu.make_async_copy(patch.at[pl.ds(p, 1), :], out.at[pl.ds(at, 1), :], sem).start()
        return carry

    def wait(_, carry):
        pltpu.make_async_copy(patch.at[pl.ds(0, 1), :], out.at[pl.ds(0, 1), :], sem).wait()
        return carry

    lax.fori_loop(0, entry(PANEL), place, 0)
    lax.fori_loop(0, entry(PANEL), wait, 0)


def finish(table, lists, front, got, patch):
    return pl.pallas_call(
        finish_kernel,
        out_shape=jax.ShapeDtypeStruct((2048, 1024), F32),
        in_specs=[SMEM, SMEM, SMEM, HBM] + [VMEM] * 2,
        out_specs=HBM,
        scratch_shapes=[
            pltpu.VMEM((30, BLK, BLK), F32),
            pltpu.SemaphoreType.DMA((30,)),
            pltpu.SemaphoreType.DMA((30,)),
            pltpu.SemaphoreType.DMA(()),
        ],
        input_output_aliases={3: 0},
        compiler_params=params(12),
        cost_estimate=cost(0, 8 * MIB),
        name="finish",
    )(table, *lists, front, got, patch)


def swap(block, axis, partner):
    count = lax.axis_size(axis)
    return lax.ppermute(block, axis, [(i, partner(i)) for i in range(count)])


def fold(block, near):
    came = lax.ppermute(block[1], "col", [(c, c ^ 12) for c in range(8)])
    return jnp.where(near, block[0], came)


def local(front, children, child_maps, pivots, diag_inverses):
    here_row, here_col = lax.axis_index("row"), lax.axis_index("col")
    chip = here_row >> 1
    together = lax.optimization_barrier
    pieces = children.reshape(10, 2, BLK, 640)

    def by_row(block, mask):
        return swap(block, "row", lambda i: i ^ mask)

    def by_col(block, mask):
        return swap(block, "col", lambda i: i ^ mask)

    bits = (chip ^ (chip >> 1)) & 1, chip >> 1
    rings = [[(r, r ^ ((2, 6), (6, 2))[r % 2][k]) for r in range(8)] for k in range(2)]
    low = [jnp.where(here_row & 1 == 0, bits[k], bits[1 - k]) == 0 for k in range(2)]
    pivots, near, low = together((pivots, here_col < 8, low))

    def halve(part, step):
        size = part.shape[0] // 2
        leave = jnp.where(low[step], part[size:], part[:size])
        stay = jnp.where(low[step], part[:size], part[size:])
        return stay + lax.ppermute(leave, "row", rings[step])

    def double(part, step):
        came = lax.ppermute(part, "row", rings[step])
        first, second = jnp.where(low[step], part, came), jnp.where(low[step], came, part)
        return jnp.concatenate([first, second], axis=0)

    def gather_step(block, which, step):
        route = [
            (r * 16 + c, r * 16 + (c ^ ORDERS[r % 2][which][step]))
            for r in range(8)
            for c in range(16)
        ]
        return lax.ppermute(block, ("row", "col"), route)

    first = cut(child_maps, pieces)
    got0 = by_row(first, 4)
    *rest, panel, corner, away, table = prepare(child_maps, pivots, front, pieces, first)
    rest_a, rest_b = rest
    corner = corner + by_row(away, 1)
    corner = corner + (by_row(corner, 2) + (by_row(corner, 6) + by_row(corner, 4)))
    away_rows, marks, list_other = pivot_terms(child_maps, pivots, front, children)
    got0, away_rows, rest_a, marks, corner = together((got0, away_rows, rest_a, marks, corner))

    top, bottom = whole_panel(table, panel, got0)
    mine = fold((top, bottom), near)
    corner = fold((corner, corner), near)[None]
    got_a = by_row(rest_a, 4)
    own_rows, marks, list_mine = pivot_terms(child_maps, pivots, front, children, marks)
    total = own_rows + by_row(away_rows, 1)
    mine, corner, total, got_a, rest_b = together((mine, corner, total, got_a, rest_b))

    def corner_step(block, step):
        masks = ((4, 1, 3), (1, 3, 4))
        route = [
            (r * 16 + c, r * 16 + (c ^ masks[r % 2][step])) for r in range(8) for c in range(16)
        ]
        return jnp.concatenate([block, lax.ppermute(block, ("row", "col"), route)], axis=0)

    held = [mine[None, :PANEL], mine[None, PANEL:]]
    for k in range(2):
        came = [gather_step(held[w], w, k) for w in range(2)]
        held = [jnp.concatenate([h, c], axis=0) for h, c in zip(held, came)]
        corner = corner_step(corner, k)
    total = halve(total, 0)
    held, corner, total = together((held, corner, total))
    came = [gather_step(held[w], w, 2) for w in range(2)]
    corner = corner_step(corner, 2)
    total = double(halve(total, 1), 1)
    came, corner, total, front = together((came, corner, total, front))
    held_far = [gather_step(held[w], w, 3) for w in range(2)]
    front = extend(table, front, pieces, (got0, got_a))
    *factors, cross = corners(table, corner, by_row(corner, 1), diag_inverses)
    came, held_far, total, rest_b, factors, cross, front = together(
        (came, held_far, double(total, 0), rest_b, factors, cross, front)
    )
    came_far = [gather_step(came[w], w, 3) for w in range(2)]
    got_b = by_row(rest_b, 4)
    *right, patch = right_factor(table, total, by_row(total, 1), factors, cross)
    came_far, right, patch = together((came_far, right, patch))
    blocks = [(held[w], came[w], held_far[w], came_far[w]) for w in range(2)]
    front = update(table, front, blocks, right, marks).reshape(2048, 1024)
    return finish(table, (list_other, list_mine), front, got_b, patch)


def solution(mesh):
    return jax.shard_map(
        local,
        mesh=mesh,
        in_specs=(P("row", "col"), P("row", "col"), P(), P(), P()),
        out_specs=P("row", "col"),
        check_vma=False,
    )
```

```python
import functools

import jax
import jax.numpy as jnp
from jax import lax
from jax.experimental import pallas as pl
from jax.experimental.pallas import tpu as pltpu
from jax.sharding import PartitionSpec as P

BLK = 128
PANEL = 512
MIB = 1 << 20
F32 = jnp.float32
BF16 = jnp.bfloat16
SMEM = pl.BlockSpec(memory_space=pltpu.SMEM)
VMEM = pl.BlockSpec(memory_space=pltpu.VMEM)
HBM = pl.BlockSpec(memory_space=pltpu.HBM)
KEPT_AT = 0
GOT_AT = 16
KEPT_COL = 32
GOT_COL = 40
ROW, COL, SIDE = 48, 49, 50
GOT_ROW = 52


def split(x):
    high = x.astype(BF16)
    return high, (x - high.astype(F32)).astype(BF16)


def dot3(a, b):
    rows = a[0].shape[0]
    both = jnp.dot(jnp.concatenate(a, axis=0), b[0], preferred_element_type=F32)
    return both[:rows] + (both[rows:] + jnp.dot(a[0], b[1], preferred_element_type=F32))


def params(mib):
    return pltpu.CompilerParams(vmem_limit_bytes=mib * MIB)


def in_hbm(x):
    return pltpu.with_memory_space_constraint(x, pltpu.HBM)


def cost(flops, moved):
    return pl.CostEstimate(flops=flops, bytes_accessed=moved, transcendentals=0)


def first_block(maps, child, here_col):
    place, found = jnp.int32(0), jnp.int32(0)
    for d in range(5):
        hit = (maps[child, d * 16 + here_col] // 16 == 0).astype(jnp.int32)
        place, found = place + d * hit, found + hit
    return place, found


def cut_kernel(maps, pieces, first, sem):
    other = 1 - lax.axis_index("row") // 4
    place, _ = first_block(maps, 1 - other, lax.axis_index("col"))
    columns = pl.ds(pl.multiple_of(place * BLK, BLK), BLK)
    copy = pltpu.make_async_copy(pieces.at[:, other, :, columns], first, sem)
    copy.start()
    copy.wait()


def cut(maps, pieces):
    return pl.pallas_call(
        cut_kernel,
        out_shape=jax.ShapeDtypeStruct((10, BLK, BLK), F32),
        in_specs=[SMEM, HBM],
        out_specs=VMEM,
        scratch_shapes=[pltpu.SemaphoreType.DMA(())],
        compiler_params=params(4),
        cost_estimate=cost(0, MIB),
        name="cut",
    )(in_hbm(maps), in_hbm(pieces))


def prepare_kernel(
    maps, pivots, front, pieces, first, *refs,
):
    *rests, panel, own, away, table, sending, kept, total, sem = refs
    here_row, here_col = lax.axis_index("row"), lax.axis_index("col")
    side, core = here_row // 4, here_row % 2
    other = 1 - side
    place, found = first_block(maps, side, here_col)
    got_place, _ = first_block(maps, other, here_col)

    def columns(d):
        return pl.ds(pl.multiple_of(d * BLK, BLK), BLK)

    reads = [
        pltpu.make_async_copy(pieces.at[:, other], sending, sem.at[0]),
        pltpu.make_async_copy(pieces.at[:, side, :, columns(place)], kept, sem.at[1]),
        pltpu.make_async_copy(front.at[:, pl.ds(0, BLK)], panel, sem.at[2]),
    ]
    writes = []
    rest_a, rest_b, rest_c, rest_d = rests
    parts = (
        (0, 0, rest_a),
        (1, 0, rest_b),
        (1, 5, rest_c),
        (2, 0, rest_d.at[pl.ds(0, 10)]),
        (3, 0, rest_d.at[pl.ds(10, 10)]),
    )
    for n, (j, start, target) in enumerate(parts):
        d = j + (j >= place).astype(jnp.int32)
        source = sending.at[pl.ds(start, target.shape[0]), :, columns(d)]
        writes.append(pltpu.make_async_copy(source, target, sem.at[3 + n]))
    for copy in reads:
        copy.start()
    for kk in range(16):
        table[KEPT_AT + kk] = -1
        table[GOT_AT + kk] = -1
    for m in range(10):
        table[KEPT_AT + maps[side, m * 8 + here_row] // 8] = m
        target = maps[other, m * 8 + here_row] // 8
        table[GOT_AT + target] = m
        table[GOT_ROW + m] = target
    for d in range(5):
        table[KEPT_COL + d] = maps[side, d * 16 + here_col] // 16
    table[GOT_COL] = maps[other, got_place * 16 + here_col] // 16
    for j in range(4):
        d = j + (j >= got_place).astype(jnp.int32)
        table[GOT_COL + 1 + j] = maps[other, d * 16 + here_col] // 16
    table[ROW] = here_row
    table[COL] = here_col
    table[SIDE] = side
    turned = pivots[...].T
    wanted = jnp.concatenate(
        [jnp.where(here_col < 4, turned[:, 4 + k : 5 + k], turned[:, k : k + 1]) for k in range(4)],
        axis=0,
    )
    block, offset = wanted >> 7, wanted & 127
    mine = jnp.where((block & 7) == here_row, (block >> 3) * BLK + offset, -1)
    sent = jnp.full_like(mine, -1)
    for m in range(10):
        hit = (block == maps[side, m * 8 + (here_row ^ 4)]) & (found > 0)
        sent = jnp.where(hit, m * BLK + offset, sent)
    reads[0].wait()
    for copy in writes:
        copy.start()
    reads[1].wait()
    reads[2].wait()

    @pl.when(found > 0)
    def _():
        for m in range(10):
            at = pl.multiple_of(maps[side, m * 8 + here_row] // 8 * BLK, BLK)
            panel[pl.ds(at, BLK), :] += kept[m]

    def rows_of(index, values, base):
        lane = lax.broadcasted_iota(jnp.int32, (PANEL, values.shape[0]), 1) + base
        chosen = jnp.where(lane == index, 1.0, 0.0).astype(BF16)
        both = jnp.concatenate(split(values), axis=1)
        return jnp.dot(chosen, both, preferred_element_type=F32)

    terms = jnp.zeros((PANEL, 2 * BLK), F32)
    for k in range(8):
        terms += rows_of(mine, panel[k * 256 : (k + 1) * 256, :], k * 256)
    for k in range(5):
        values = first[2 * k : 2 * k + 2].reshape(256, BLK)
        terms += rows_of(sent, values, k * 256)
    total[...] = terms[:, :BLK] + terms[:, BLK:]
    own[...] = total[pl.ds(pl.multiple_of(core * 256, 256), 256), :]
    away[...] = total[pl.ds(pl.multiple_of((1 - core) * 256, 256), 256), :]
    for copy in writes:
        copy.wait()


def prepare(maps, pivots, front, pieces, first):
    return pl.pallas_call(
        prepare_kernel,
        out_shape=[
            jax.ShapeDtypeStruct((10, BLK, BLK), F32),
            jax.ShapeDtypeStruct((5, BLK, BLK), F32),
            jax.ShapeDtypeStruct((5, BLK, BLK), F32),
            jax.ShapeDtypeStruct((20, BLK, BLK), F32),
            jax.ShapeDtypeStruct((2048, BLK), F32),
            jax.ShapeDtypeStruct((256, BLK), F32),
            jax.ShapeDtypeStruct((256, BLK), F32),
            jax.ShapeDtypeStruct((64,), jnp.int32),
        ],
        in_specs=[SMEM, VMEM, HBM, HBM, VMEM],
        out_specs=[HBM] * 4 + [VMEM, VMEM, VMEM, SMEM],
        scratch_shapes=[
            pltpu.VMEM((10, BLK, 640), F32),
            pltpu.VMEM((10, BLK, BLK), F32),
            pltpu.VMEM((PANEL, BLK), F32),
            pltpu.SemaphoreType.DMA((8,)),
        ],
        compiler_params=params(24),
        cost_estimate=cost(0, 9 * MIB),
        name="prepare",
    )(in_hbm(maps), in_hbm(pivots.reshape(8, BLK)), in_hbm(front), in_hbm(pieces), first)


def pivot_kernel(mine_half, maps, pivots, front, children, *refs):
    rows, marks, front_list, spread, inverse, child_list, sem, child_sem = refs[-8:]
    rows[...] = jnp.zeros_like(rows)
    marks[...] = refs[0][...] if mine_half else jnp.zeros_like(marks)
    here_row, here_col = lax.axis_index("row"), lax.axis_index("col")
    side, quarter, core = here_row // 4, here_row % 4, here_row % 2
    half = core if mine_half else 1 - core
    spread[...] = jnp.zeros_like(spread)

    def clear(b, carry):
        inverse[b] = -1
        return carry

    lax.fori_loop(0, 128, clear, 0, unroll=16)
    for k in range(20):
        inverse[maps[side, 4 * k + quarter]] = k

    def visit(p, counts):
        pivot = pivots[half * PANEL + p]
        block, offset = pivot >> 7, pivot & 127
        child_block = inverse[block]
        mine = (block & 7) == here_row
        shared = ((block & 3) == quarter) & (child_block >= 0)
        front_list[counts[0]] = (((block >> 3) * BLK + offset) << 9) | p
        child_list[counts[1]] = ((child_block * BLK + offset) << 9) | p
        return counts[0] + mine.astype(jnp.int32), counts[1] + shared.astype(jnp.int32)

    counts = lax.fori_loop(0, PANEL, visit, (jnp.int32(0), jnp.int32(0)), unroll=8)
    front_list[PANEL] = counts[0]
    mark = jnp.full((1, BLK), half + 1, jnp.int32).astype(F32)

    def take_front(n, carry):
        at, p = front_list[n] >> 9, front_list[n] & 511
        pltpu.make_async_copy(front.at[pl.ds(at, 1), :], rows.at[pl.ds(p, 1), :], sem).start()
        marks[pl.ds(at, 1), :] = mark
        return carry

    def take_child(n, carry):
        at, p = child_list[n] >> 9, child_list[n] & 511
        pltpu.make_async_copy(
            children.at[pl.ds(at, 1), :], spread.at[pl.ds(p, 1), :], child_sem
        ).start()
        return carry

    def wait(source, target, semaphore, count):
        def some(size):
            def body(_, carry):
                pltpu.make_async_copy(
                    source.at[pl.ds(0, size), :], target.at[pl.ds(0, size), :], semaphore
                ).wait()
                return carry

            return body

        lax.fori_loop(0, count // 16, some(16), 0)
        lax.fori_loop(0, count % 16, some(1), 0)

    lax.fori_loop(0, counts[0], take_front, 0)
    lax.fori_loop(0, counts[1], take_child, 0)
    wait(front, rows, sem, counts[0])
    wait(children, spread, child_sem, counts[1])
    for d in range(5):
        to = pl.ds(pl.multiple_of(maps[side, d * 16 + here_col] // 16 * BLK, BLK), BLK)
        rows[:, to] += spread[:, d * BLK : (d + 1) * BLK]


def pivot_terms(maps, pivots, front, children, *before):
    mine_half = len(before) > 0
    return pl.pallas_call(
        functools.partial(pivot_kernel, mine_half),
        out_shape=[
            jax.ShapeDtypeStruct((PANEL, 1024), F32),
            jax.ShapeDtypeStruct((2048, BLK), F32),
            jax.ShapeDtypeStruct((PANEL + 1,), jnp.int32),
        ],
        in_specs=[SMEM, SMEM, HBM, HBM] + [VMEM] * len(before),
        out_specs=[VMEM, VMEM, SMEM],
        scratch_shapes=[
            pltpu.VMEM((PANEL, 640), F32),
            pltpu.SMEM((128,), jnp.int32),
            pltpu.SMEM((PANEL + 1,), jnp.int32),
            pltpu.SemaphoreType.DMA(()),
            pltpu.SemaphoreType.DMA(()),
        ],
        compiler_params=params(12),
        cost_estimate=cost(0, 24 * MIB),
        name="pivot_terms_mine" if mine_half else "pivot_terms_other",
    )(in_hbm(maps), in_hbm(pivots), in_hbm(front), in_hbm(children), *before)


def panel_kernel(table, panel, got, top, bottom):
    top[...] = panel[:1024, :]
    bottom[...] = panel[1024:, :]

    @pl.when(table[GOT_COL] == 0)
    def _():
        for kk in range(16):
            m = table[GOT_AT + kk]
            half = top if kk < 8 else bottom
            at = kk % 8 * BLK

            @pl.when(m >= 0)
            def _(half=half, at=at, m=m):
                half[at : at + BLK, :] += got[m]


def whole_panel(table, panel, got):
    shape = jax.ShapeDtypeStruct((1024, BLK), F32)
    return pl.pallas_call(
        panel_kernel,
        out_shape=[shape, shape],
        in_specs=[SMEM, VMEM, VMEM],
        out_specs=[VMEM, VMEM],
        compiler_params=params(12),
        cost_estimate=cost(0, 3 * MIB),
        name="whole_panel",
    )(table, panel, got)


def flips(delta):
    return (delta & 1) ^ (delta >> 1), delta >> 1


def corner_kernel(table, own, swapped, inverses, factor_h, factor_l, cross):
    here_row, here_col = table[ROW], table[COL]
    core, x, y = here_row % 2, here_col % 4, here_col // 4
    mine = (y ^ (y >> 1)) & 1

    def corner(panel, half):
        blocks = []
        for xx in range(4):
            one, three = flips(xx ^ x)
            pair = mine ^ panel
            slot = jnp.where(half == 0, pair | (one << 1) | (three << 2), one | (three << 1) | (pair << 2))
            blocks.append(jnp.where(core == half, own[slot], swapped[slot]))
        return jnp.concatenate(blocks, axis=1)

    for p in range(2):
        factor_h[p], factor_l[p] = split(inverses[p])
    for half in range(2):
        rows = slice(half * 256, (half + 1) * 256)
        factor_h[2, rows, :], factor_l[2, rows, :] = split(corner(1, half))
        cross[rows, :] = dot3(split(corner(0, half)), (factor_h[0], factor_l[0]))


def corners(table, own, swapped, inverses):
    return pl.pallas_call(
        corner_kernel,
        out_shape=[
            jax.ShapeDtypeStruct((3, PANEL, PANEL), BF16),
            jax.ShapeDtypeStruct((3, PANEL, PANEL), BF16),
            jax.ShapeDtypeStruct((PANEL, PANEL), F32),
        ],
        in_specs=[SMEM, VMEM, VMEM, VMEM],
        out_specs=[VMEM] * 3,
        compiler_params=params(20),
        cost_estimate=cost(6 * PANEL**3, 8 * MIB),
        name="corners",
    )(table, own, swapped, inverses)


def factor_kernel(table, own, swapped, factor_h, factor_l, cross, high, low, patch):
    here_row, col = table[ROW], table[COL]
    core, slot = here_row % 2, col % 4
    inside = lax.broadcasted_iota(jnp.int32, (PANEL, 1024), 1) < BLK

    def mine(x):
        out = x[:, :BLK]
        for s in range(1, 4):
            out = jnp.where(slot == s, x[:, s * BLK : (s + 1) * BLK], out)
        return out

    def begin_with(block, x):
        return jnp.concatenate([block, x[:, BLK:]], axis=1)

    def factor(n):
        return factor_h[n], factor_l[n]

    def factor_columns(n):
        return mine(factor_h[n].astype(F32)) + mine(factor_l[n].astype(F32))

    first = jnp.where(core == 0, own[...], swapped[...])
    first = jnp.where(inside & (col < 4), 0.0, first)
    second = jnp.where(core == 0, swapped[...], own[...])
    second = second - dot3(split(cross[...]), split(first))
    patch[...] = begin_with(jnp.where(col < 4, mine(cross[...]), second[:, :BLK]), second)
    second = jnp.where(inside & (col < 8), 0.0, second)
    right = dot3(factor(1), split(second))
    in_second = (col >= 4) & (col < 8)
    right = begin_with(jnp.where(in_second, factor_columns(1), right[:, :BLK]), right)
    terms = split(right)
    high[PANEL:], low[PANEL:] = terms
    first = jnp.where(inside & (col < 8), 0.0, first)
    left = dot3(factor(0), split(first - dot3(factor(2), terms)))
    left = begin_with(jnp.where(col < 4, factor_columns(0), left[:, :BLK]), left)
    high[:PANEL], low[:PANEL] = split(left)


def right_factor(table, own, swapped, factors, cross):
    shape = jax.ShapeDtypeStruct((1024, 1024), BF16)
    return pl.pallas_call(
        factor_kernel,
        out_shape=[shape, shape, jax.ShapeDtypeStruct((PANEL, 1024), F32)],
        in_specs=[SMEM] + [VMEM] * 5,
        out_specs=[VMEM] * 3,
        compiler_params=params(24),
        cost_estimate=cost(4 * 6 * PANEL * PANEL * 1024, 14 * MIB),
        name="right_factor",
    )(table, own, swapped, *factors, cross)


def block_at(base, half, t, s):
    return jnp.maximum(s[base + half * 8 + t], 0)


ARRIVED = (0, 0, 10), (1, 0, 10), (2, 0, 5)


def extend_kernel(table, front, *refs):
    out, refs = refs[-1], refs[:-1]
    kept, *got = (refs[2 * k : 2 * k + 2] for k in range(1 + len(ARRIVED)))
    step = pl.program_id(0)
    out[...] = front[...]
    for half in range(2):

        @pl.when(table[KEPT_AT + half * 8 + step] >= 0)
        def _(half=half):
            for d in range(5):
                to = pl.ds(pl.multiple_of(table[KEPT_COL + d] * BLK, BLK), BLK)
                out[half, :, to] += kept[half][0, 0, :, d * BLK : (d + 1) * BLK]

        m = table[GOT_AT + half * 8 + step]
        for j, (column, start, count) in enumerate(ARRIVED):

            @pl.when((m >= start) & (m < start + count))
            def _(half=half, j=j, column=column):
                to = pl.ds(pl.multiple_of(table[GOT_COL + column] * BLK, BLK), BLK)
                out[half, :, to] += got[j][half][0]


def extend(table, front, pieces, got):
    def kept_at(half):
        return lambda t, s: (block_at(KEPT_AT, half, t, s), s[SIDE], 0, 0)

    def got_at(half, start, count):
        return lambda t, s: (
            jnp.clip(s[GOT_AT + half * 8 + t] - start, 0, count - 1), 0, 0
        )

    tile = pl.BlockSpec((2, BLK, 1024), lambda t, s: (0, t, 0))
    kept_specs = [pl.BlockSpec((1, 1, BLK, 640), kept_at(half)) for half in range(2)]
    got_specs = [
        pl.BlockSpec((1, BLK, BLK), got_at(half, start, count))
        for _, start, count in ARRIVED
        for half in range(2)
    ]
    return pl.pallas_call(
        extend_kernel,
        out_shape=pltpu.HBM((2, 1024, 1024), F32),
        grid_spec=pltpu.PrefetchScalarGridSpec(
            num_scalar_prefetch=1,
            grid=(8,),
            in_specs=[tile, *kept_specs, *got_specs],
            out_specs=tile,
        ),
        compiler_params=params(20),
        cost_estimate=cost(0, MIB),
        name="extend",
    )(table, in_hbm(front.reshape(2, 1024, 1024)), *[in_hbm(pieces)] * 2, *[g for g in got for _ in range(2)])


ORDERS = ((1, 3, 4, 12), (3, 1, 12, 4)), ((4, 12, 1, 3), (12, 4, 3, 1))


def update_kernel(table, front, *refs):
    blocks = refs[:4], refs[4:8]
    right_h, right_l, marks, out, panels = refs[8:]
    step = pl.program_id(0)
    span = pl.ds(pl.multiple_of(step % 2 * 256, 256), 256)
    col, core = table[COL], table[ROW] % 2

    def assemble(which):
        held, came, held_far, came_far = blocks[which]
        for c in range(16):
            one_x, three_x = flips((c ^ col) & 3)
            one_y, three_y = flips((c ^ col) >> 2)
            bits = {1: one_x, 3: three_x, 4: one_y, 12: three_y}
            even, odd = (ORDERS[q][which] for q in range(2))
            flip = [jnp.where(core == 0, bits[e], bits[o]) for e, o in zip(even, odd)]
            slot = flip[0] | (flip[1] << 1)
            later, far = flip[2] == 1, flip[3] == 1
            near_block = jnp.where(later, came[slot, span, :], held[slot, span, :])
            far_block = jnp.where(later, came_far[slot, span, :], held_far[slot, span, :])
            block = jnp.where(far, far_block, near_block)
            y, x = c // 4, c % 4
            rows = slice(0, 256) if y < 2 else slice(256, PANEL)
            first = min(y, 3 - y) * PANEL + x * BLK
            columns = slice(first, first + BLK)
            panels[0, rows, columns], panels[1, rows, columns] = split(block)

    for which in range(2):
        pl.when(step // 2 == which)(functools.partial(assemble, which))

    active = marks[...] == 0
    for piece in range(4):
        wide = slice(piece * 256, (piece + 1) * 256)
        change = dot3((panels[0], panels[1]), (right_h[:, wide], right_l[:, wide]))
        change = change.reshape(2, 256, 256)
        for j in range(2):
            columns = slice(piece * 256 + j * BLK, piece * 256 + (j + 1) * BLK)
            before, part = front[:, :, columns], change[:, :, j * BLK : (j + 1) * BLK]
            after = before - part
            if piece == 0 and j == 0:
                after = jnp.where(col < 8, part, after)
            out[:, :, columns] = jnp.where(active, after, before)


def update(table, front, blocks, right, marks):
    tile = pl.BlockSpec((2, 256, 1024), lambda t, s: (0, t, 0))
    return pl.pallas_call(
        update_kernel,
        out_shape=pltpu.HBM((2, 1024, 1024), F32),
        grid_spec=pltpu.PrefetchScalarGridSpec(
            num_scalar_prefetch=1,
            grid=(4,),
            in_specs=[
                tile,
                *[VMEM] * 10,
                pl.BlockSpec((2, 256, BLK), lambda t, s: (0, t, 0)),
            ],
            out_specs=tile,
            scratch_shapes=[pltpu.VMEM((2, PANEL, 1024), BF16)],
        ),
        compiler_params=params(24),
        cost_estimate=cost(6 * 2048 * 1024 * 1024, 32 * MIB),
        name="update",
    )(table, in_hbm(front), *blocks[0], *blocks[1], *right, marks.reshape(2, 1024, BLK))


def finish_kernel(
    table, list_other, list_mine, front, got_c, got_d, patch,
    out, held, read_sem, write_sem, sem,
):
    del front
    core = table[ROW] % 2
    copies = []
    places = [(2, m) for m in range(5, 10)] + [(j, m) for j in (3, 4) for m in range(10)]
    for n, (column, m) in enumerate(places):
        columns = pl.ds(pl.multiple_of(table[GOT_COL + column] * BLK, BLK), BLK)
        rows = pl.ds(pl.multiple_of(table[GOT_ROW + m] * BLK, BLK), BLK)
        there, here = out.at[rows, columns], held.at[n]
        read = pltpu.make_async_copy(there, here, read_sem.at[n])
        write = pltpu.make_async_copy(here, there, write_sem.at[n])
        copies.append((read, write))
    for read, _ in copies:
        read.start()
    for n, (read, write) in enumerate(copies):
        read.wait()
        held[n] += got_c[n] if n < 5 else got_d[n - 5]
        write.start()
    for _, write in copies:
        write.wait()

    def entry(n):
        return jnp.where(core == 0, list_other[n], list_mine[n])

    def place(n, carry):
        at, p = entry(n) >> 9, entry(n) & 511
        pltpu.make_async_copy(patch.at[pl.ds(p, 1), :], out.at[pl.ds(at, 1), :], sem).start()
        return carry

    def wait(_, carry):
        pltpu.make_async_copy(patch.at[pl.ds(0, 1), :], out.at[pl.ds(0, 1), :], sem).wait()
        return carry

    lax.fori_loop(0, entry(PANEL), place, 0)
    lax.fori_loop(0, entry(PANEL), wait, 0)


def finish(table, lists, front, got, patch):
    return pl.pallas_call(
        finish_kernel,
        out_shape=jax.ShapeDtypeStruct((2048, 1024), F32),
        in_specs=[SMEM, SMEM, SMEM, HBM] + [VMEM] * 3,
        out_specs=HBM,
        scratch_shapes=[
            pltpu.VMEM((25, BLK, BLK), F32),
            pltpu.SemaphoreType.DMA((25,)),
            pltpu.SemaphoreType.DMA((25,)),
            pltpu.SemaphoreType.DMA(()),
        ],
        input_output_aliases={3: 0},
        compiler_params=params(12),
        cost_estimate=cost(0, 8 * MIB),
        name="finish",
    )(table, *lists, front, *got, patch)


def swap(block, axis, partner):
    count = lax.axis_size(axis)
    return lax.ppermute(block, axis, [(i, partner(i)) for i in range(count)])


def fold(block, near):
    came = lax.ppermute(block[1], "col", [(c, c ^ 12) for c in range(8)])
    return jnp.where(near, block[0], came)


def local(front, children, child_maps, pivots, diag_inverses):
    here_row, here_col = lax.axis_index("row"), lax.axis_index("col")
    chip = here_row >> 1
    together = lax.optimization_barrier
    pieces = children.reshape(10, 2, BLK, 640)

    def by_row(block, mask):
        return swap(block, "row", lambda i: i ^ mask)

    def by_col(block, mask):
        return swap(block, "col", lambda i: i ^ mask)

    bits = (chip ^ (chip >> 1)) & 1, chip >> 1
    rings = [[(r, r ^ ((2, 6), (6, 2))[r % 2][k]) for r in range(8)] for k in range(2)]
    low = [jnp.where(here_row & 1 == 0, bits[k], bits[1 - k]) == 0 for k in range(2)]
    pivots, near, low = together((pivots, here_col < 8, low))

    def halve(part, step):
        size = part.shape[0] // 2
        leave = jnp.where(low[step], part[size:], part[:size])
        stay = jnp.where(low[step], part[:size], part[size:])
        return stay + lax.ppermute(leave, "row", rings[step])

    def double(part, step):
        came = lax.ppermute(part, "row", rings[step])
        first, second = jnp.where(low[step], part, came), jnp.where(low[step], came, part)
        return jnp.concatenate([first, second], axis=0)

    def gather_step(block, which, step):
        route = [
            (r * 16 + c, r * 16 + (c ^ ORDERS[r % 2][which][step]))
            for r in range(8)
            for c in range(16)
        ]
        return lax.ppermute(block, ("row", "col"), route)

    first = cut(child_maps, pieces)
    got0 = by_row(first, 4)
    *rest, panel, corner, away, table = prepare(child_maps, pivots, front, pieces, first)
    rest_a, rest_b, rest_c, rest_d = rest
    corner = corner + by_row(away, 1)
    corner = corner + (by_row(corner, 2) + (by_row(corner, 6) + by_row(corner, 4)))
    away_rows, marks, list_other = pivot_terms(child_maps, pivots, front, children)
    got0, away_rows, rest_a, marks, corner = together((got0, away_rows, rest_a, marks, corner))

    top, bottom = whole_panel(table, panel, got0)
    mine = fold((top, bottom), near)
    corner = fold((corner, corner), near)[None]
    got_a = by_row(rest_a, 4)
    own_rows, marks, list_mine = pivot_terms(child_maps, pivots, front, children, marks)
    total = own_rows + by_row(away_rows, 1)
    mine, corner, total, got_a, rest_b = together((mine, corner, total, got_a, rest_b))

    def corner_step(block, step):
        masks = ((4, 1, 3), (1, 3, 4))
        route = [
            (r * 16 + c, r * 16 + (c ^ masks[r % 2][step])) for r in range(8) for c in range(16)
        ]
        return jnp.concatenate([block, lax.ppermute(block, ("row", "col"), route)], axis=0)

    held = [mine[None, :PANEL], mine[None, PANEL:]]
    for k in range(2):
        came = [gather_step(held[w], w, k) for w in range(2)]
        held = [jnp.concatenate([h, c], axis=0) for h, c in zip(held, came)]
        corner = corner_step(corner, k)
    total = halve(total, 0)
    got_b = by_row(rest_b, 4)
    held, corner, total, got_b, rest_c = together((held, corner, total, got_b, rest_c))
    came = [gather_step(held[w], w, 2) for w in range(2)]
    corner = corner_step(corner, 2)
    total = double(halve(total, 1), 1)
    got_c = by_row(rest_c, 4)
    front = extend(table, front, pieces, (got0, got_a, got_b))
    came, corner, total, front, got_c = together((came, corner, total, front, got_c))
    held_far = [gather_step(held[w], w, 3) for w in range(2)]
    *factors, cross = corners(table, corner, by_row(corner, 1), diag_inverses)
    came, held_far, total, rest_d, factors, cross, front = together(
        (came, held_far, double(total, 0), rest_d, factors, cross, front)
    )
    came_far = [gather_step(came[w], w, 3) for w in range(2)]
    got_d = by_row(rest_d, 4)
    *right, patch = right_factor(table, total, by_row(total, 1), factors, cross)
    came_far, right, patch = together((came_far, right, patch))
    blocks = [(held[w], came[w], held_far[w], came_far[w]) for w in range(2)]
    front = update(table, front, blocks, right, marks).reshape(2048, 1024)
    return finish(table, (list_other, list_mine), front, (got_c, got_d), patch)


def solution(mesh):
    return jax.shard_map(
        local,
        mesh=mesh,
        in_specs=(P("row", "col"), P("row", "col"), P(), P(), P()),
        out_specs=P("row", "col"),
        check_vma=False,
    )
```

```python
import functools

import jax
import jax.numpy as jnp
from jax import lax
from jax.experimental import pallas as pl
from jax.experimental.pallas import tpu as pltpu
from jax.sharding import PartitionSpec as P

BLK = 128
PANEL = 512
MIB = 1 << 20
F32 = jnp.float32
BF16 = jnp.bfloat16
SMEM = pl.BlockSpec(memory_space=pltpu.SMEM)
VMEM = pl.BlockSpec(memory_space=pltpu.VMEM)
HBM = pl.BlockSpec(memory_space=pltpu.HBM)
KEPT_AT = 0
GOT_AT = 16
KEPT_COL = 32
GOT_COL = 40
ROW, COL, SIDE = 48, 49, 50
GOT_ROW = 52


def split(x):
    high = x.astype(BF16)
    return high, (x - high.astype(F32)).astype(BF16)


def dot3(a, b):
    rows = a[0].shape[0]
    both = jnp.dot(jnp.concatenate(a, axis=0), b[0], preferred_element_type=F32)
    return both[:rows] + (both[rows:] + jnp.dot(a[0], b[1], preferred_element_type=F32))


def params(mib):
    return pltpu.CompilerParams(vmem_limit_bytes=mib * MIB)


def in_hbm(x):
    return pltpu.with_memory_space_constraint(x, pltpu.HBM)


def cost(flops, moved):
    return pl.CostEstimate(flops=flops, bytes_accessed=moved, transcendentals=0)


def first_block(maps, child, here_col):
    place, found = jnp.int32(0), jnp.int32(0)
    for d in range(5):
        hit = (maps[child, d * 16 + here_col] // 16 == 0).astype(jnp.int32)
        place, found = place + d * hit, found + hit
    return place, found


def cut_kernel(maps, pieces, first, sem):
    other = 1 - lax.axis_index("row") // 4
    place, _ = first_block(maps, 1 - other, lax.axis_index("col"))
    columns = pl.ds(pl.multiple_of(place * BLK, BLK), BLK)
    copy = pltpu.make_async_copy(pieces.at[:, other, :, columns], first, sem)
    copy.start()
    copy.wait()


def cut(maps, pieces):
    return pl.pallas_call(
        cut_kernel,
        out_shape=jax.ShapeDtypeStruct((10, BLK, BLK), F32),
        in_specs=[SMEM, HBM],
        out_specs=VMEM,
        scratch_shapes=[pltpu.SemaphoreType.DMA(())],
        compiler_params=params(4),
        cost_estimate=cost(0, MIB),
        name="cut",
    )(in_hbm(maps), in_hbm(pieces))


def prepare_kernel(
    maps, pivots, front, pieces, first, *refs,
):
    *rests, panel, own, away, table, sending, kept, total, sem = refs
    here_row, here_col = lax.axis_index("row"), lax.axis_index("col")
    side, core = here_row // 4, here_row % 2
    other = 1 - side
    place, found = first_block(maps, side, here_col)
    got_place, _ = first_block(maps, other, here_col)

    def columns(d):
        return pl.ds(pl.multiple_of(d * BLK, BLK), BLK)

    reads = [
        pltpu.make_async_copy(pieces.at[:, other], sending, sem.at[0]),
        pltpu.make_async_copy(pieces.at[:, side, :, columns(place)], kept, sem.at[1]),
        pltpu.make_async_copy(front.at[:, pl.ds(0, BLK)], panel, sem.at[2]),
    ]
    writes = []
    rest_a, rest_b, rest_c = rests
    parts = (
        (0, 0, rest_a),
        (1, 0, rest_b),
        (1, 5, rest_c.at[pl.ds(0, 5)]),
        (2, 0, rest_c.at[pl.ds(5, 10)]),
        (3, 0, rest_c.at[pl.ds(15, 10)]),
    )
    for n, (j, start, target) in enumerate(parts):
        d = j + (j >= place).astype(jnp.int32)
        source = sending.at[pl.ds(start, target.shape[0]), :, columns(d)]
        writes.append(pltpu.make_async_copy(source, target, sem.at[3 + n]))
    for copy in reads:
        copy.start()
    for kk in range(16):
        table[KEPT_AT + kk] = -1
        table[GOT_AT + kk] = -1
    for m in range(10):
        table[KEPT_AT + maps[side, m * 8 + here_row] // 8] = m
        target = maps[other, m * 8 + here_row] // 8
        table[GOT_AT + target] = m
        table[GOT_ROW + m] = target
    for d in range(5):
        table[KEPT_COL + d] = maps[side, d * 16 + here_col] // 16
    table[GOT_COL] = maps[other, got_place * 16 + here_col] // 16
    for j in range(4):
        d = j + (j >= got_place).astype(jnp.int32)
        table[GOT_COL + 1 + j] = maps[other, d * 16 + here_col] // 16
    table[ROW] = here_row
    table[COL] = here_col
    table[SIDE] = side
    turned = pivots[...].T
    wanted = jnp.concatenate(
        [jnp.where(here_col < 4, turned[:, 4 + k : 5 + k], turned[:, k : k + 1]) for k in range(4)],
        axis=0,
    )
    block, offset = wanted >> 7, wanted & 127
    mine = jnp.where((block & 7) == here_row, (block >> 3) * BLK + offset, -1)
    sent = jnp.full_like(mine, -1)
    for m in range(10):
        hit = (block == maps[side, m * 8 + (here_row ^ 4)]) & (found > 0)
        sent = jnp.where(hit, m * BLK + offset, sent)
    reads[0].wait()
    for copy in writes:
        copy.start()
    reads[1].wait()
    reads[2].wait()

    @pl.when(found > 0)
    def _():
        for m in range(10):
            at = pl.multiple_of(maps[side, m * 8 + here_row] // 8 * BLK, BLK)
            panel[pl.ds(at, BLK), :] += kept[m]

    def rows_of(index, values, base):
        lane = lax.broadcasted_iota(jnp.int32, (PANEL, values.shape[0]), 1) + base
        chosen = jnp.where(lane == index, 1.0, 0.0).astype(BF16)
        both = jnp.concatenate(split(values), axis=1)
        return jnp.dot(chosen, both, preferred_element_type=F32)

    terms = jnp.zeros((PANEL, 2 * BLK), F32)
    for k in range(8):
        terms += rows_of(mine, panel[k * 256 : (k + 1) * 256, :], k * 256)
    for k in range(5):
        values = first[2 * k : 2 * k + 2].reshape(256, BLK)
        terms += rows_of(sent, values, k * 256)
    total[...] = terms[:, :BLK] + terms[:, BLK:]
    own[...] = total[pl.ds(pl.multiple_of(core * 256, 256), 256), :]
    away[...] = total[pl.ds(pl.multiple_of((1 - core) * 256, 256), 256), :]
    for copy in writes:
        copy.wait()


def prepare(maps, pivots, front, pieces, first):
    return pl.pallas_call(
        prepare_kernel,
        out_shape=[
            jax.ShapeDtypeStruct((10, BLK, BLK), F32),
            jax.ShapeDtypeStruct((5, BLK, BLK), F32),
            jax.ShapeDtypeStruct((25, BLK, BLK), F32),
            jax.ShapeDtypeStruct((2048, BLK), F32),
            jax.ShapeDtypeStruct((256, BLK), F32),
            jax.ShapeDtypeStruct((256, BLK), F32),
            jax.ShapeDtypeStruct((64,), jnp.int32),
        ],
        in_specs=[SMEM, VMEM, HBM, HBM, VMEM],
        out_specs=[HBM] * 3 + [VMEM, VMEM, VMEM, SMEM],
        scratch_shapes=[
            pltpu.VMEM((10, BLK, 640), F32),
            pltpu.VMEM((10, BLK, BLK), F32),
            pltpu.VMEM((PANEL, BLK), F32),
            pltpu.SemaphoreType.DMA((8,)),
        ],
        compiler_params=params(24),
        cost_estimate=cost(0, 9 * MIB),
        name="prepare",
    )(in_hbm(maps), in_hbm(pivots.reshape(8, BLK)), in_hbm(front), in_hbm(pieces), first)


def pivot_kernel(mine_half, maps, pivots, front, children, *refs):
    rows, marks, front_list, spread, inverse, child_list, sem, child_sem = refs[-8:]
    rows[...] = jnp.zeros_like(rows)
    marks[...] = refs[0][...] if mine_half else jnp.zeros_like(marks)
    here_row, here_col = lax.axis_index("row"), lax.axis_index("col")
    side, quarter, core = here_row // 4, here_row % 4, here_row % 2
    half = core if mine_half else 1 - core
    spread[...] = jnp.zeros_like(spread)

    def clear(b, carry):
        inverse[b] = -1
        return carry

    lax.fori_loop(0, 128, clear, 0, unroll=16)
    for k in range(20):
        inverse[maps[side, 4 * k + quarter]] = k

    def visit(p, counts):
        pivot = pivots[half * PANEL + p]
        block, offset = pivot >> 7, pivot & 127
        child_block = inverse[block]
        mine = (block & 7) == here_row
        shared = ((block & 3) == quarter) & (child_block >= 0)
        front_list[counts[0]] = (((block >> 3) * BLK + offset) << 9) | p
        child_list[counts[1]] = ((child_block * BLK + offset) << 9) | p
        return counts[0] + mine.astype(jnp.int32), counts[1] + shared.astype(jnp.int32)

    counts = lax.fori_loop(0, PANEL, visit, (jnp.int32(0), jnp.int32(0)), unroll=8)
    front_list[PANEL] = counts[0]
    mark = jnp.full((1, BLK), half + 1, jnp.int32).astype(F32)

    def take_front(n, carry):
        at, p = front_list[n] >> 9, front_list[n] & 511
        pltpu.make_async_copy(front.at[pl.ds(at, 1), :], rows.at[pl.ds(p, 1), :], sem).start()
        marks[pl.ds(at, 1), :] = mark
        return carry

    def take_child(n, carry):
        at, p = child_list[n] >> 9, child_list[n] & 511
        pltpu.make_async_copy(
            children.at[pl.ds(at, 1), :], spread.at[pl.ds(p, 1), :], child_sem
        ).start()
        return carry

    def wait(source, target, semaphore, count):
        def some(size):
            def body(_, carry):
                pltpu.make_async_copy(
                    source.at[pl.ds(0, size), :], target.at[pl.ds(0, size), :], semaphore
                ).wait()
                return carry

            return body

        lax.fori_loop(0, count // 16, some(16), 0)
        lax.fori_loop(0, count % 16, some(1), 0)

    lax.fori_loop(0, counts[0], take_front, 0)
    lax.fori_loop(0, counts[1], take_child, 0)
    wait(front, rows, sem, counts[0])
    wait(children, spread, child_sem, counts[1])
    for d in range(5):
        to = pl.ds(pl.multiple_of(maps[side, d * 16 + here_col] // 16 * BLK, BLK), BLK)
        rows[:, to] += spread[:, d * BLK : (d + 1) * BLK]


def pivot_terms(maps, pivots, front, children, *before):
    mine_half = len(before) > 0
    return pl.pallas_call(
        functools.partial(pivot_kernel, mine_half),
        out_shape=[
            jax.ShapeDtypeStruct((PANEL, 1024), F32),
            jax.ShapeDtypeStruct((2048, BLK), F32),
            jax.ShapeDtypeStruct((PANEL + 1,), jnp.int32),
        ],
        in_specs=[SMEM, SMEM, HBM, HBM] + [VMEM] * len(before),
        out_specs=[VMEM, VMEM, SMEM],
        scratch_shapes=[
            pltpu.VMEM((PANEL, 640), F32),
            pltpu.SMEM((128,), jnp.int32),
            pltpu.SMEM((PANEL + 1,), jnp.int32),
            pltpu.SemaphoreType.DMA(()),
            pltpu.SemaphoreType.DMA(()),
        ],
        compiler_params=params(12),
        cost_estimate=cost(0, 24 * MIB),
        name="pivot_terms_mine" if mine_half else "pivot_terms_other",
    )(in_hbm(maps), in_hbm(pivots), in_hbm(front), in_hbm(children), *before)


def panel_kernel(table, panel, got, top, bottom):
    top[...] = panel[:1024, :]
    bottom[...] = panel[1024:, :]

    @pl.when(table[GOT_COL] == 0)
    def _():
        for kk in range(16):
            m = table[GOT_AT + kk]
            half = top if kk < 8 else bottom
            at = kk % 8 * BLK

            @pl.when(m >= 0)
            def _(half=half, at=at, m=m):
                half[at : at + BLK, :] += got[m]


def whole_panel(table, panel, got):
    shape = jax.ShapeDtypeStruct((1024, BLK), F32)
    return pl.pallas_call(
        panel_kernel,
        out_shape=[shape, shape],
        in_specs=[SMEM, VMEM, VMEM],
        out_specs=[VMEM, VMEM],
        compiler_params=params(12),
        cost_estimate=cost(0, 3 * MIB),
        name="whole_panel",
    )(table, panel, got)


def flips(delta):
    return (delta & 1) ^ (delta >> 1), delta >> 1


def corner_kernel(table, own, swapped, inverses, factor_h, factor_l, cross):
    here_row, here_col = table[ROW], table[COL]
    core, x, y = here_row % 2, here_col % 4, here_col // 4
    mine = (y ^ (y >> 1)) & 1

    def corner(panel, half):
        blocks = []
        for xx in range(4):
            one, three = flips(xx ^ x)
            pair = mine ^ panel
            slot = jnp.where(half == 0, pair | (one << 1) | (three << 2), one | (three << 1) | (pair << 2))
            blocks.append(jnp.where(core == half, own[slot], swapped[slot]))
        return jnp.concatenate(blocks, axis=1)

    for p in range(2):
        factor_h[p], factor_l[p] = split(inverses[p])
    for half in range(2):
        rows = slice(half * 256, (half + 1) * 256)
        factor_h[2, rows, :], factor_l[2, rows, :] = split(corner(1, half))
        cross[rows, :] = dot3(split(corner(0, half)), (factor_h[0], factor_l[0]))


def corners(table, own, swapped, inverses):
    return pl.pallas_call(
        corner_kernel,
        out_shape=[
            jax.ShapeDtypeStruct((3, PANEL, PANEL), BF16),
            jax.ShapeDtypeStruct((3, PANEL, PANEL), BF16),
            jax.ShapeDtypeStruct((PANEL, PANEL), F32),
        ],
        in_specs=[SMEM, VMEM, VMEM, VMEM],
        out_specs=[VMEM] * 3,
        compiler_params=params(20),
        cost_estimate=cost(6 * PANEL**3, 8 * MIB),
        name="corners",
    )(table, own, swapped, inverses)


def factor_kernel(table, own, swapped, factor_h, factor_l, cross, high, low, patch):
    here_row, col = table[ROW], table[COL]
    core, slot = here_row % 2, col % 4
    inside = lax.broadcasted_iota(jnp.int32, (PANEL, 1024), 1) < BLK

    def mine(x):
        out = x[:, :BLK]
        for s in range(1, 4):
            out = jnp.where(slot == s, x[:, s * BLK : (s + 1) * BLK], out)
        return out

    def begin_with(block, x):
        return jnp.concatenate([block, x[:, BLK:]], axis=1)

    def factor(n):
        return factor_h[n], factor_l[n]

    def factor_columns(n):
        return mine(factor_h[n].astype(F32)) + mine(factor_l[n].astype(F32))

    first = jnp.where(core == 0, own[...], swapped[...])
    first = jnp.where(inside & (col < 4), 0.0, first)
    second = jnp.where(core == 0, swapped[...], own[...])
    second = second - dot3(split(cross[...]), split(first))
    patch[...] = begin_with(jnp.where(col < 4, mine(cross[...]), second[:, :BLK]), second)
    second = jnp.where(inside & (col < 8), 0.0, second)
    right = dot3(factor(1), split(second))
    in_second = (col >= 4) & (col < 8)
    right = begin_with(jnp.where(in_second, factor_columns(1), right[:, :BLK]), right)
    terms = split(right)
    high[PANEL:], low[PANEL:] = terms
    first = jnp.where(inside & (col < 8), 0.0, first)
    left = dot3(factor(0), split(first - dot3(factor(2), terms)))
    left = begin_with(jnp.where(col < 4, factor_columns(0), left[:, :BLK]), left)
    high[:PANEL], low[:PANEL] = split(left)


def right_factor(table, own, swapped, factors, cross):
    shape = jax.ShapeDtypeStruct((1024, 1024), BF16)
    return pl.pallas_call(
        factor_kernel,
        out_shape=[shape, shape, jax.ShapeDtypeStruct((PANEL, 1024), F32)],
        in_specs=[SMEM] + [VMEM] * 5,
        out_specs=[VMEM] * 3,
        compiler_params=params(24),
        cost_estimate=cost(4 * 6 * PANEL * PANEL * 1024, 14 * MIB),
        name="right_factor",
    )(table, own, swapped, *factors, cross)


def block_at(base, half, t, s):
    return jnp.maximum(s[base + half * 8 + t], 0)


ARRIVED = (0, 0, 10), (1, 0, 10), (2, 0, 5)


def extend_kernel(table, front, *refs):
    out, refs = refs[-1], refs[:-1]
    kept, *got = (refs[2 * k : 2 * k + 2] for k in range(1 + len(ARRIVED)))
    step = pl.program_id(0)
    out[...] = front[...]
    for half in range(2):

        @pl.when(table[KEPT_AT + half * 8 + step] >= 0)
        def _(half=half):
            for d in range(5):
                to = pl.ds(pl.multiple_of(table[KEPT_COL + d] * BLK, BLK), BLK)
                out[half, :, to] += kept[half][0, 0, :, d * BLK : (d + 1) * BLK]

        m = table[GOT_AT + half * 8 + step]
        for j, (column, start, count) in enumerate(ARRIVED):

            @pl.when((m >= start) & (m < start + count))
            def _(half=half, j=j, column=column):
                to = pl.ds(pl.multiple_of(table[GOT_COL + column] * BLK, BLK), BLK)
                out[half, :, to] += got[j][half][0]


def extend(table, front, pieces, got):
    def kept_at(half):
        return lambda t, s: (block_at(KEPT_AT, half, t, s), s[SIDE], 0, 0)

    def got_at(half, start, count):
        return lambda t, s: (
            jnp.clip(s[GOT_AT + half * 8 + t] - start, 0, count - 1), 0, 0
        )

    tile = pl.BlockSpec((2, BLK, 1024), lambda t, s: (0, t, 0))
    kept_specs = [pl.BlockSpec((1, 1, BLK, 640), kept_at(half)) for half in range(2)]
    got_specs = [
        pl.BlockSpec((1, BLK, BLK), got_at(half, start, count))
        for _, start, count in ARRIVED
        for half in range(2)
    ]
    return pl.pallas_call(
        extend_kernel,
        out_shape=pltpu.HBM((2, 1024, 1024), F32),
        grid_spec=pltpu.PrefetchScalarGridSpec(
            num_scalar_prefetch=1,
            grid=(8,),
            in_specs=[tile, *kept_specs, *got_specs],
            out_specs=tile,
        ),
        compiler_params=params(20),
        cost_estimate=cost(0, MIB),
        name="extend",
    )(table, in_hbm(front.reshape(2, 1024, 1024)), *[in_hbm(pieces)] * 2, *[g for g in got for _ in range(2)])


ORDERS = ((1, 3, 4, 12), (3, 1, 12, 4)), ((4, 12, 1, 3), (12, 4, 3, 1))


def update_kernel(table, front, *refs):
    blocks = refs[:4], refs[4:8]
    right_h, right_l, marks, out, panels = refs[8:]
    step = pl.program_id(0)
    span = pl.ds(pl.multiple_of(step % 2 * 256, 256), 256)
    col, core = table[COL], table[ROW] % 2

    def assemble(which):
        held, came, held_far, came_far = blocks[which]
        for c in range(16):
            one_x, three_x = flips((c ^ col) & 3)
            one_y, three_y = flips((c ^ col) >> 2)
            bits = {1: one_x, 3: three_x, 4: one_y, 12: three_y}
            even, odd = (ORDERS[q][which] for q in range(2))
            flip = [jnp.where(core == 0, bits[e], bits[o]) for e, o in zip(even, odd)]
            slot = flip[0] | (flip[1] << 1)
            later, far = flip[2] == 1, flip[3] == 1
            near_block = jnp.where(later, came[slot, span, :], held[slot, span, :])
            far_block = jnp.where(later, came_far[slot, span, :], held_far[slot, span, :])
            block = jnp.where(far, far_block, near_block)
            y, x = c // 4, c % 4
            rows = slice(0, 256) if y < 2 else slice(256, PANEL)
            first = min(y, 3 - y) * PANEL + x * BLK
            columns = slice(first, first + BLK)
            panels[0, rows, columns], panels[1, rows, columns] = split(block)

    for which in range(2):
        pl.when(step // 2 == which)(functools.partial(assemble, which))

    active = marks[...] == 0
    for piece in range(4):
        wide = slice(piece * 256, (piece + 1) * 256)
        change = dot3((panels[0], panels[1]), (right_h[:, wide], right_l[:, wide]))
        change = change.reshape(2, 256, 256)
        for j in range(2):
            columns = slice(piece * 256 + j * BLK, piece * 256 + (j + 1) * BLK)
            before, part = front[:, :, columns], change[:, :, j * BLK : (j + 1) * BLK]
            after = before - part
            if piece == 0 and j == 0:
                after = jnp.where(col < 8, part, after)
            out[:, :, columns] = jnp.where(active, after, before)


def update(table, front, blocks, right, marks):
    tile = pl.BlockSpec((2, 256, 1024), lambda t, s: (0, t, 0))
    return pl.pallas_call(
        update_kernel,
        out_shape=pltpu.HBM((2, 1024, 1024), F32),
        grid_spec=pltpu.PrefetchScalarGridSpec(
            num_scalar_prefetch=1,
            grid=(4,),
            in_specs=[
                tile,
                *[VMEM] * 10,
                pl.BlockSpec((2, 256, BLK), lambda t, s: (0, t, 0)),
            ],
            out_specs=tile,
            scratch_shapes=[pltpu.VMEM((2, PANEL, 1024), BF16)],
        ),
        compiler_params=params(24),
        cost_estimate=cost(6 * 2048 * 1024 * 1024, 32 * MIB),
        name="update",
    )(table, in_hbm(front), *blocks[0], *blocks[1], *right, marks.reshape(2, 1024, BLK))


def finish_kernel(
    table, list_other, list_mine, front, got, patch,
    out, held, read_sem, write_sem, sem,
):
    del front
    core = table[ROW] % 2
    copies = []
    places = [(2, m) for m in range(5, 10)] + [(j, m) for j in (3, 4) for m in range(10)]
    for n, (column, m) in enumerate(places):
        columns = pl.ds(pl.multiple_of(table[GOT_COL + column] * BLK, BLK), BLK)
        rows = pl.ds(pl.multiple_of(table[GOT_ROW + m] * BLK, BLK), BLK)
        there, here = out.at[rows, columns], held.at[n]
        read = pltpu.make_async_copy(there, here, read_sem.at[n])
        write = pltpu.make_async_copy(here, there, write_sem.at[n])
        copies.append((read, write))
    for read, _ in copies:
        read.start()
    for n, (read, write) in enumerate(copies):
        read.wait()
        held[n] += got[n]
        write.start()
    for _, write in copies:
        write.wait()

    def entry(n):
        return jnp.where(core == 0, list_other[n], list_mine[n])

    def place(n, carry):
        at, p = entry(n) >> 9, entry(n) & 511
        pltpu.make_async_copy(patch.at[pl.ds(p, 1), :], out.at[pl.ds(at, 1), :], sem).start()
        return carry

    def wait(_, carry):
        pltpu.make_async_copy(patch.at[pl.ds(0, 1), :], out.at[pl.ds(0, 1), :], sem).wait()
        return carry

    lax.fori_loop(0, entry(PANEL), place, 0)
    lax.fori_loop(0, entry(PANEL), wait, 0)


def finish(table, lists, front, got, patch):
    return pl.pallas_call(
        finish_kernel,
        out_shape=jax.ShapeDtypeStruct((2048, 1024), F32),
        in_specs=[SMEM, SMEM, SMEM, HBM] + [VMEM] * 2,
        out_specs=HBM,
        scratch_shapes=[
            pltpu.VMEM((25, BLK, BLK), F32),
            pltpu.SemaphoreType.DMA((25,)),
            pltpu.SemaphoreType.DMA((25,)),
            pltpu.SemaphoreType.DMA(()),
        ],
        input_output_aliases={3: 0},
        compiler_params=params(12),
        cost_estimate=cost(0, 8 * MIB),
        name="finish",
    )(table, *lists, front, got, patch)


def swap(block, axis, partner):
    count = lax.axis_size(axis)
    return lax.ppermute(block, axis, [(i, partner(i)) for i in range(count)])


def fold(block, near):
    came = lax.ppermute(block[1], "col", [(c, c ^ 12) for c in range(8)])
    return jnp.where(near, block[0], came)


def local(front, children, child_maps, pivots, diag_inverses):
    here_row, here_col = lax.axis_index("row"), lax.axis_index("col")
    chip = here_row >> 1
    together = lax.optimization_barrier
    pieces = children.reshape(10, 2, BLK, 640)

    def by_row(block, mask):
        return swap(block, "row", lambda i: i ^ mask)

    def by_col(block, mask):
        return swap(block, "col", lambda i: i ^ mask)

    bits = (chip ^ (chip >> 1)) & 1, chip >> 1
    rings = [[(r, r ^ ((2, 6), (6, 2))[r % 2][k]) for r in range(8)] for k in range(2)]
    low = [jnp.where(here_row & 1 == 0, bits[k], bits[1 - k]) == 0 for k in range(2)]
    pivots, near, low = together((pivots, here_col < 8, low))

    def halve(part, step):
        size = part.shape[0] // 2
        leave = jnp.where(low[step], part[size:], part[:size])
        stay = jnp.where(low[step], part[:size], part[size:])
        return stay + lax.ppermute(leave, "row", rings[step])

    def double(part, step):
        came = lax.ppermute(part, "row", rings[step])
        first, second = jnp.where(low[step], part, came), jnp.where(low[step], came, part)
        return jnp.concatenate([first, second], axis=0)

    def gather_step(block, which, step):
        route = [
            (r * 16 + c, r * 16 + (c ^ ORDERS[r % 2][which][step]))
            for r in range(8)
            for c in range(16)
        ]
        return lax.ppermute(block, ("row", "col"), route)

    first = cut(child_maps, pieces)
    got0 = by_row(first, 4)
    *rest, panel, corner, away, table = prepare(child_maps, pivots, front, pieces, first)
    rest_a, rest_b, rest_c = rest
    corner = corner + by_row(away, 1)
    corner = corner + (by_row(corner, 2) + (by_row(corner, 6) + by_row(corner, 4)))
    away_rows, marks, list_other = pivot_terms(child_maps, pivots, front, children)
    got0, away_rows, rest_a, marks, corner = together((got0, away_rows, rest_a, marks, corner))

    top, bottom = whole_panel(table, panel, got0)
    mine = fold((top, bottom), near)
    corner = fold((corner, corner), near)[None]
    got_a = by_row(rest_a, 4)
    own_rows, marks, list_mine = pivot_terms(child_maps, pivots, front, children, marks)
    total = own_rows + by_row(away_rows, 1)
    mine, corner, total, got_a, rest_b = together((mine, corner, total, got_a, rest_b))

    def corner_step(block, step):
        masks = ((4, 1, 3), (1, 3, 4))
        route = [
            (r * 16 + c, r * 16 + (c ^ masks[r % 2][step])) for r in range(8) for c in range(16)
        ]
        return jnp.concatenate([block, lax.ppermute(block, ("row", "col"), route)], axis=0)

    held = [mine[None, :PANEL], mine[None, PANEL:]]
    for k in range(2):
        came = [gather_step(held[w], w, k) for w in range(2)]
        held = [jnp.concatenate([h, c], axis=0) for h, c in zip(held, came)]
        corner = corner_step(corner, k)
    total = halve(total, 0)
    held, corner, total, rest_b = together((held, corner, total, rest_b))
    came = [gather_step(held[w], w, 2) for w in range(2)]
    corner = corner_step(corner, 2)
    total = double(halve(total, 1), 1)
    got_b = by_row(rest_b, 4)
    came, corner, total, got_b = together((came, corner, total, got_b))
    held_far = [gather_step(held[w], w, 3) for w in range(2)]
    front = extend(table, front, pieces, (got0, got_a, got_b))
    *factors, cross = corners(table, corner, by_row(corner, 1), diag_inverses)
    came, held_far, total, rest_c, factors, cross, front = together(
        (came, held_far, double(total, 0), rest_c, factors, cross, front)
    )
    came_far = [gather_step(came[w], w, 3) for w in range(2)]
    got_c = by_row(rest_c, 4)
    *right, patch = right_factor(table, total, by_row(total, 1), factors, cross)
    came_far, right, patch = together((came_far, right, patch))
    blocks = [(held[w], came[w], held_far[w], came_far[w]) for w in range(2)]
    front = update(table, front, blocks, right, marks).reshape(2048, 1024)
    return finish(table, (list_other, list_mine), front, got_c, patch)


def solution(mesh):
    return jax.shard_map(
        local,
        mesh=mesh,
        in_specs=(P("row", "col"), P("row", "col"), P(), P(), P()),
        out_specs=P("row", "col"),
        check_vma=False,
    )
```

```python
import functools

import jax
import jax.numpy as jnp
from jax import lax
from jax.experimental import pallas as pl
from jax.experimental.pallas import tpu as pltpu
from jax.sharding import PartitionSpec as P

BLK = 128
PANEL = 512
MIB = 1 << 20
F32 = jnp.float32
BF16 = jnp.bfloat16
SMEM = pl.BlockSpec(memory_space=pltpu.SMEM)
VMEM = pl.BlockSpec(memory_space=pltpu.VMEM)
HBM = pl.BlockSpec(memory_space=pltpu.HBM)
KEPT_AT = 0
GOT_AT = 16
KEPT_COL = 32
GOT_COL = 40
ROW, COL, SIDE = 48, 49, 50
GOT_ROW = 52


def split(x):
    high = x.astype(BF16)
    return high, (x - high.astype(F32)).astype(BF16)


def dot3(a, b):
    rows = a[0].shape[0]
    both = jnp.dot(jnp.concatenate(a, axis=0), b[0], preferred_element_type=F32)
    return both[:rows] + (both[rows:] + jnp.dot(a[0], b[1], preferred_element_type=F32))


def params(mib):
    return pltpu.CompilerParams(vmem_limit_bytes=mib * MIB)


def in_hbm(x):
    return pltpu.with_memory_space_constraint(x, pltpu.HBM)


def cost(flops, moved):
    return pl.CostEstimate(flops=flops, bytes_accessed=moved, transcendentals=0)


def first_block(maps, child, here_col):
    place, found = jnp.int32(0), jnp.int32(0)
    for d in range(5):
        hit = (maps[child, d * 16 + here_col] // 16 == 0).astype(jnp.int32)
        place, found = place + d * hit, found + hit
    return place, found


def cut_kernel(maps, pieces, first, sem):
    other = 1 - lax.axis_index("row") // 4
    place, _ = first_block(maps, 1 - other, lax.axis_index("col"))
    columns = pl.ds(pl.multiple_of(place * BLK, BLK), BLK)
    copy = pltpu.make_async_copy(pieces.at[:, other, :, columns], first, sem)
    copy.start()
    copy.wait()


def cut(maps, pieces):
    return pl.pallas_call(
        cut_kernel,
        out_shape=jax.ShapeDtypeStruct((10, BLK, BLK), F32),
        in_specs=[SMEM, HBM],
        out_specs=VMEM,
        scratch_shapes=[pltpu.SemaphoreType.DMA(())],
        compiler_params=params(4),
        cost_estimate=cost(0, MIB),
        name="cut",
    )(in_hbm(maps), in_hbm(pieces))


def prepare_kernel(
    maps, pivots, front, pieces, first, *refs,
):
    *rests, panel, own, away, table, sending, kept, total, sem = refs
    here_row, here_col = lax.axis_index("row"), lax.axis_index("col")
    side, core = here_row // 4, here_row % 2
    other = 1 - side
    place, found = first_block(maps, side, here_col)
    got_place, _ = first_block(maps, other, here_col)

    def columns(d):
        return pl.ds(pl.multiple_of(d * BLK, BLK), BLK)

    reads = [
        pltpu.make_async_copy(pieces.at[:, other], sending, sem.at[0]),
        pltpu.make_async_copy(pieces.at[:, side, :, columns(place)], kept, sem.at[1]),
        pltpu.make_async_copy(front.at[:, pl.ds(0, BLK)], panel, sem.at[2]),
    ]
    writes = []
    rest_a, rest_b = rests
    parts = (
        (0, 0, rest_a.at[pl.ds(0, 10)]),
        (1, 0, rest_a.at[pl.ds(10, 5)]),
        (1, 5, rest_b.at[pl.ds(0, 5)]),
        (2, 0, rest_b.at[pl.ds(5, 10)]),
        (3, 0, rest_b.at[pl.ds(15, 10)]),
    )
    for n, (j, start, target) in enumerate(parts):
        d = j + (j >= place).astype(jnp.int32)
        source = sending.at[pl.ds(start, target.shape[0]), :, columns(d)]
        writes.append(pltpu.make_async_copy(source, target, sem.at[3 + n]))
    for copy in reads:
        copy.start()
    for kk in range(16):
        table[KEPT_AT + kk] = -1
        table[GOT_AT + kk] = -1
    for m in range(10):
        table[KEPT_AT + maps[side, m * 8 + here_row] // 8] = m
        target = maps[other, m * 8 + here_row] // 8
        table[GOT_AT + target] = m
        table[GOT_ROW + m] = target
    for d in range(5):
        table[KEPT_COL + d] = maps[side, d * 16 + here_col] // 16
    table[GOT_COL] = maps[other, got_place * 16 + here_col] // 16
    for j in range(4):
        d = j + (j >= got_place).astype(jnp.int32)
        table[GOT_COL + 1 + j] = maps[other, d * 16 + here_col] // 16
    table[ROW] = here_row
    table[COL] = here_col
    table[SIDE] = side
    turned = pivots[...].T
    wanted = jnp.concatenate(
        [jnp.where(here_col < 4, turned[:, 4 + k : 5 + k], turned[:, k : k + 1]) for k in range(4)],
        axis=0,
    )
    block, offset = wanted >> 7, wanted & 127
    mine = jnp.where((block & 7) == here_row, (block >> 3) * BLK + offset, -1)
    sent = jnp.full_like(mine, -1)
    for m in range(10):
        hit = (block == maps[side, m * 8 + (here_row ^ 4)]) & (found > 0)
        sent = jnp.where(hit, m * BLK + offset, sent)
    reads[0].wait()
    for copy in writes:
        copy.start()
    reads[1].wait()
    reads[2].wait()

    @pl.when(found > 0)
    def _():
        for m in range(10):
            at = pl.multiple_of(maps[side, m * 8 + here_row] // 8 * BLK, BLK)
            panel[pl.ds(at, BLK), :] += kept[m]

    def rows_of(index, values, base):
        lane = lax.broadcasted_iota(jnp.int32, (PANEL, values.shape[0]), 1) + base
        chosen = jnp.where(lane == index, 1.0, 0.0).astype(BF16)
        both = jnp.concatenate(split(values), axis=1)
        return jnp.dot(chosen, both, preferred_element_type=F32)

    terms = jnp.zeros((PANEL, 2 * BLK), F32)
    for k in range(8):
        terms += rows_of(mine, panel[k * 256 : (k + 1) * 256, :], k * 256)
    for k in range(5):
        values = first[2 * k : 2 * k + 2].reshape(256, BLK)
        terms += rows_of(sent, values, k * 256)
    total[...] = terms[:, :BLK] + terms[:, BLK:]
    own[...] = total[pl.ds(pl.multiple_of(core * 256, 256), 256), :]
    away[...] = total[pl.ds(pl.multiple_of((1 - core) * 256, 256), 256), :]
    for copy in writes:
        copy.wait()


def prepare(maps, pivots, front, pieces, first):
    return pl.pallas_call(
        prepare_kernel,
        out_shape=[
            jax.ShapeDtypeStruct((15, BLK, BLK), F32),
            jax.ShapeDtypeStruct((25, BLK, BLK), F32),
            jax.ShapeDtypeStruct((2048, BLK), F32),
            jax.ShapeDtypeStruct((256, BLK), F32),
            jax.ShapeDtypeStruct((256, BLK), F32),
            jax.ShapeDtypeStruct((64,), jnp.int32),
        ],
        in_specs=[SMEM, VMEM, HBM, HBM, VMEM],
        out_specs=[HBM] * 2 + [VMEM, VMEM, VMEM, SMEM],
        scratch_shapes=[
            pltpu.VMEM((10, BLK, 640), F32),
            pltpu.VMEM((10, BLK, BLK), F32),
            pltpu.VMEM((PANEL, BLK), F32),
            pltpu.SemaphoreType.DMA((8,)),
        ],
        compiler_params=params(24),
        cost_estimate=cost(0, 9 * MIB),
        name="prepare",
    )(in_hbm(maps), in_hbm(pivots.reshape(8, BLK)), in_hbm(front), in_hbm(pieces), first)


def pivot_kernel(mine_half, maps, pivots, front, children, *refs):
    rows, marks, front_list, spread, inverse, child_list, sem, child_sem = refs[-8:]
    rows[...] = jnp.zeros_like(rows)
    marks[...] = refs[0][...] if mine_half else jnp.zeros_like(marks)
    here_row, here_col = lax.axis_index("row"), lax.axis_index("col")
    side, quarter, core = here_row // 4, here_row % 4, here_row % 2
    half = core if mine_half else 1 - core
    spread[...] = jnp.zeros_like(spread)

    def clear(b, carry):
        inverse[b] = -1
        return carry

    lax.fori_loop(0, 128, clear, 0, unroll=16)
    for k in range(20):
        inverse[maps[side, 4 * k + quarter]] = k

    def visit(p, counts):
        pivot = pivots[half * PANEL + p]
        block, offset = pivot >> 7, pivot & 127
        child_block = inverse[block]
        mine = (block & 7) == here_row
        shared = ((block & 3) == quarter) & (child_block >= 0)
        front_list[counts[0]] = (((block >> 3) * BLK + offset) << 9) | p
        child_list[counts[1]] = ((child_block * BLK + offset) << 9) | p
        return counts[0] + mine.astype(jnp.int32), counts[1] + shared.astype(jnp.int32)

    counts = lax.fori_loop(0, PANEL, visit, (jnp.int32(0), jnp.int32(0)), unroll=8)
    front_list[PANEL] = counts[0]
    mark = jnp.full((1, BLK), half + 1, jnp.int32).astype(F32)

    def take_front(n, carry):
        at, p = front_list[n] >> 9, front_list[n] & 511
        pltpu.make_async_copy(front.at[pl.ds(at, 1), :], rows.at[pl.ds(p, 1), :], sem).start()
        marks[pl.ds(at, 1), :] = mark
        return carry

    def take_child(n, carry):
        at, p = child_list[n] >> 9, child_list[n] & 511
        pltpu.make_async_copy(
            children.at[pl.ds(at, 1), :], spread.at[pl.ds(p, 1), :], child_sem
        ).start()
        return carry

    def wait(source, target, semaphore, count):
        def some(size):
            def body(_, carry):
                pltpu.make_async_copy(
                    source.at[pl.ds(0, size), :], target.at[pl.ds(0, size), :], semaphore
                ).wait()
                return carry

            return body

        lax.fori_loop(0, count // 16, some(16), 0)
        lax.fori_loop(0, count % 16, some(1), 0)

    lax.fori_loop(0, counts[0], take_front, 0)
    lax.fori_loop(0, counts[1], take_child, 0)
    wait(front, rows, sem, counts[0])
    wait(children, spread, child_sem, counts[1])
    for d in range(5):
        to = pl.ds(pl.multiple_of(maps[side, d * 16 + here_col] // 16 * BLK, BLK), BLK)
        rows[:, to] += spread[:, d * BLK : (d + 1) * BLK]


def pivot_terms(maps, pivots, front, children, *before):
    mine_half = len(before) > 0
    return pl.pallas_call(
        functools.partial(pivot_kernel, mine_half),
        out_shape=[
            jax.ShapeDtypeStruct((PANEL, 1024), F32),
            jax.ShapeDtypeStruct((2048, BLK), F32),
            jax.ShapeDtypeStruct((PANEL + 1,), jnp.int32),
        ],
        in_specs=[SMEM, SMEM, HBM, HBM] + [VMEM] * len(before),
        out_specs=[VMEM, VMEM, SMEM],
        scratch_shapes=[
            pltpu.VMEM((PANEL, 640), F32),
            pltpu.SMEM((128,), jnp.int32),
            pltpu.SMEM((PANEL + 1,), jnp.int32),
            pltpu.SemaphoreType.DMA(()),
            pltpu.SemaphoreType.DMA(()),
        ],
        compiler_params=params(12),
        cost_estimate=cost(0, 24 * MIB),
        name="pivot_terms_mine" if mine_half else "pivot_terms_other",
    )(in_hbm(maps), in_hbm(pivots), in_hbm(front), in_hbm(children), *before)


def panel_kernel(table, panel, got, top, bottom):
    top[...] = panel[:1024, :]
    bottom[...] = panel[1024:, :]

    @pl.when(table[GOT_COL] == 0)
    def _():
        for kk in range(16):
            m = table[GOT_AT + kk]
            half = top if kk < 8 else bottom
            at = kk % 8 * BLK

            @pl.when(m >= 0)
            def _(half=half, at=at, m=m):
                half[at : at + BLK, :] += got[m]


def whole_panel(table, panel, got):
    shape = jax.ShapeDtypeStruct((1024, BLK), F32)
    return pl.pallas_call(
        panel_kernel,
        out_shape=[shape, shape],
        in_specs=[SMEM, VMEM, VMEM],
        out_specs=[VMEM, VMEM],
        compiler_params=params(12),
        cost_estimate=cost(0, 3 * MIB),
        name="whole_panel",
    )(table, panel, got)


def flips(delta):
    return (delta & 1) ^ (delta >> 1), delta >> 1


def corner_kernel(table, own, swapped, inverses, factor_h, factor_l, cross):
    here_row, here_col = table[ROW], table[COL]
    core, x, y = here_row % 2, here_col % 4, here_col // 4
    mine = (y ^ (y >> 1)) & 1

    def corner(panel, half):
        blocks = []
        for xx in range(4):
            one, three = flips(xx ^ x)
            pair = mine ^ panel
            slot = jnp.where(half == 0, pair | (one << 1) | (three << 2), one | (three << 1) | (pair << 2))
            blocks.append(jnp.where(core == half, own[slot], swapped[slot]))
        return jnp.concatenate(blocks, axis=1)

    for p in range(2):
        factor_h[p], factor_l[p] = split(inverses[p])
    for half in range(2):
        rows = slice(half * 256, (half + 1) * 256)
        factor_h[2, rows, :], factor_l[2, rows, :] = split(corner(1, half))
        cross[rows, :] = dot3(split(corner(0, half)), (factor_h[0], factor_l[0]))


def corners(table, own, swapped, inverses):
    return pl.pallas_call(
        corner_kernel,
        out_shape=[
            jax.ShapeDtypeStruct((3, PANEL, PANEL), BF16),
            jax.ShapeDtypeStruct((3, PANEL, PANEL), BF16),
            jax.ShapeDtypeStruct((PANEL, PANEL), F32),
        ],
        in_specs=[SMEM, VMEM, VMEM, VMEM],
        out_specs=[VMEM] * 3,
        compiler_params=params(20),
        cost_estimate=cost(6 * PANEL**3, 8 * MIB),
        name="corners",
    )(table, own, swapped, inverses)


def factor_kernel(table, own, swapped, factor_h, factor_l, cross, high, low, patch):
    here_row, col = table[ROW], table[COL]
    core, slot = here_row % 2, col % 4
    inside = lax.broadcasted_iota(jnp.int32, (PANEL, 1024), 1) < BLK

    def mine(x):
        out = x[:, :BLK]
        for s in range(1, 4):
            out = jnp.where(slot == s, x[:, s * BLK : (s + 1) * BLK], out)
        return out

    def begin_with(block, x):
        return jnp.concatenate([block, x[:, BLK:]], axis=1)

    def factor(n):
        return factor_h[n], factor_l[n]

    def factor_columns(n):
        return mine(factor_h[n].astype(F32)) + mine(factor_l[n].astype(F32))

    first = jnp.where(core == 0, own[...], swapped[...])
    first = jnp.where(inside & (col < 4), 0.0, first)
    second = jnp.where(core == 0, swapped[...], own[...])
    second = second - dot3(split(cross[...]), split(first))
    patch[...] = begin_with(jnp.where(col < 4, mine(cross[...]), second[:, :BLK]), second)
    second = jnp.where(inside & (col < 8), 0.0, second)
    right = dot3(factor(1), split(second))
    in_second = (col >= 4) & (col < 8)
    right = begin_with(jnp.where(in_second, factor_columns(1), right[:, :BLK]), right)
    terms = split(right)
    high[PANEL:], low[PANEL:] = terms
    first = jnp.where(inside & (col < 8), 0.0, first)
    left = dot3(factor(0), split(first - dot3(factor(2), terms)))
    left = begin_with(jnp.where(col < 4, factor_columns(0), left[:, :BLK]), left)
    high[:PANEL], low[:PANEL] = split(left)


def right_factor(table, own, swapped, factors, cross):
    shape = jax.ShapeDtypeStruct((1024, 1024), BF16)
    return pl.pallas_call(
        factor_kernel,
        out_shape=[shape, shape, jax.ShapeDtypeStruct((PANEL, 1024), F32)],
        in_specs=[SMEM] + [VMEM] * 5,
        out_specs=[VMEM] * 3,
        compiler_params=params(24),
        cost_estimate=cost(4 * 6 * PANEL * PANEL * 1024, 14 * MIB),
        name="right_factor",
    )(table, own, swapped, *factors, cross)


def block_at(base, half, t, s):
    return jnp.maximum(s[base + half * 8 + t], 0)


ARRIVED = (0, 0, 10, 0), (1, 0, 10, 0), (2, 0, 5, 10)


def extend_kernel(table, front, *refs):
    out, refs = refs[-1], refs[:-1]
    kept, *got = (refs[2 * k : 2 * k + 2] for k in range(1 + len(ARRIVED)))
    step = pl.program_id(0)
    out[...] = front[...]
    for half in range(2):

        @pl.when(table[KEPT_AT + half * 8 + step] >= 0)
        def _(half=half):
            for d in range(5):
                to = pl.ds(pl.multiple_of(table[KEPT_COL + d] * BLK, BLK), BLK)
                out[half, :, to] += kept[half][0, 0, :, d * BLK : (d + 1) * BLK]

        m = table[GOT_AT + half * 8 + step]
        for j, (column, start, count, _) in enumerate(ARRIVED):

            @pl.when((m >= start) & (m < start + count))
            def _(half=half, j=j, column=column):
                to = pl.ds(pl.multiple_of(table[GOT_COL + column] * BLK, BLK), BLK)
                out[half, :, to] += got[j][half][0]


def extend(table, front, pieces, got):
    def kept_at(half):
        return lambda t, s: (block_at(KEPT_AT, half, t, s), s[SIDE], 0, 0)

    def got_at(half, start, count, slot):
        return lambda t, s: (
            jnp.clip(s[GOT_AT + half * 8 + t] - start, 0, count - 1) + slot, 0, 0
        )

    tile = pl.BlockSpec((2, BLK, 1024), lambda t, s: (0, t, 0))
    kept_specs = [pl.BlockSpec((1, 1, BLK, 640), kept_at(half)) for half in range(2)]
    got_specs = [
        pl.BlockSpec((1, BLK, BLK), got_at(half, start, count, slot))
        for _, start, count, slot in ARRIVED
        for half in range(2)
    ]
    return pl.pallas_call(
        extend_kernel,
        out_shape=pltpu.HBM((2, 1024, 1024), F32),
        grid_spec=pltpu.PrefetchScalarGridSpec(
            num_scalar_prefetch=1,
            grid=(8,),
            in_specs=[tile, *kept_specs, *got_specs],
            out_specs=tile,
        ),
        compiler_params=params(20),
        cost_estimate=cost(0, MIB),
        name="extend",
    )(table, in_hbm(front.reshape(2, 1024, 1024)), *[in_hbm(pieces)] * 2, *[g for g in got for _ in range(2)])


ORDERS = ((1, 3, 4, 12), (3, 1, 12, 4)), ((4, 12, 1, 3), (12, 4, 3, 1))


def update_kernel(table, front, *refs):
    blocks = refs[:4], refs[4:8]
    right_h, right_l, marks, out, panels = refs[8:]
    step = pl.program_id(0)
    span = pl.ds(pl.multiple_of(step % 2 * 256, 256), 256)
    col, core = table[COL], table[ROW] % 2

    def assemble(which):
        held, came, held_far, came_far = blocks[which]
        for c in range(16):
            one_x, three_x = flips((c ^ col) & 3)
            one_y, three_y = flips((c ^ col) >> 2)
            bits = {1: one_x, 3: three_x, 4: one_y, 12: three_y}
            even, odd = (ORDERS[q][which] for q in range(2))
            flip = [jnp.where(core == 0, bits[e], bits[o]) for e, o in zip(even, odd)]
            slot = flip[0] | (flip[1] << 1)
            later, far = flip[2] == 1, flip[3] == 1
            near_block = jnp.where(later, came[slot, span, :], held[slot, span, :])
            far_block = jnp.where(later, came_far[slot, span, :], held_far[slot, span, :])
            block = jnp.where(far, far_block, near_block)
            y, x = c // 4, c % 4
            rows = slice(0, 256) if y < 2 else slice(256, PANEL)
            first = min(y, 3 - y) * PANEL + x * BLK
            columns = slice(first, first + BLK)
            panels[0, rows, columns], panels[1, rows, columns] = split(block)

    for which in range(2):
        pl.when(step // 2 == which)(functools.partial(assemble, which))

    active = marks[...] == 0
    for piece in range(4):
        wide = slice(piece * 256, (piece + 1) * 256)
        change = dot3((panels[0], panels[1]), (right_h[:, wide], right_l[:, wide]))
        change = change.reshape(2, 256, 256)
        for j in range(2):
            columns = slice(piece * 256 + j * BLK, piece * 256 + (j + 1) * BLK)
            before, part = front[:, :, columns], change[:, :, j * BLK : (j + 1) * BLK]
            after = before - part
            if piece == 0 and j == 0:
                after = jnp.where(col < 8, part, after)
            out[:, :, columns] = jnp.where(active, after, before)


def update(table, front, blocks, right, marks):
    tile = pl.BlockSpec((2, 256, 1024), lambda t, s: (0, t, 0))
    return pl.pallas_call(
        update_kernel,
        out_shape=pltpu.HBM((2, 1024, 1024), F32),
        grid_spec=pltpu.PrefetchScalarGridSpec(
            num_scalar_prefetch=1,
            grid=(4,),
            in_specs=[
                tile,
                *[VMEM] * 10,
                pl.BlockSpec((2, 256, BLK), lambda t, s: (0, t, 0)),
            ],
            out_specs=tile,
            scratch_shapes=[pltpu.VMEM((2, PANEL, 1024), BF16)],
        ),
        compiler_params=params(24),
        cost_estimate=cost(6 * 2048 * 1024 * 1024, 32 * MIB),
        name="update",
    )(table, in_hbm(front), *blocks[0], *blocks[1], *right, marks.reshape(2, 1024, BLK))


def finish_kernel(
    table, list_other, list_mine, front, got, patch,
    out, held, read_sem, write_sem, sem,
):
    del front
    core = table[ROW] % 2
    copies = []
    places = [(2, m) for m in range(5, 10)] + [(j, m) for j in (3, 4) for m in range(10)]
    for n, (column, m) in enumerate(places):
        columns = pl.ds(pl.multiple_of(table[GOT_COL + column] * BLK, BLK), BLK)
        rows = pl.ds(pl.multiple_of(table[GOT_ROW + m] * BLK, BLK), BLK)
        there, here = out.at[rows, columns], held.at[n]
        read = pltpu.make_async_copy(there, here, read_sem.at[n])
        write = pltpu.make_async_copy(here, there, write_sem.at[n])
        copies.append((read, write))
    for read, _ in copies:
        read.start()
    for n, (read, write) in enumerate(copies):
        read.wait()
        held[n] += got[n]
        write.start()
    for _, write in copies:
        write.wait()

    def entry(n):
        return jnp.where(core == 0, list_other[n], list_mine[n])

    def place(n, carry):
        at, p = entry(n) >> 9, entry(n) & 511
        pltpu.make_async_copy(patch.at[pl.ds(p, 1), :], out.at[pl.ds(at, 1), :], sem).start()
        return carry

    def wait(_, carry):
        pltpu.make_async_copy(patch.at[pl.ds(0, 1), :], out.at[pl.ds(0, 1), :], sem).wait()
        return carry

    lax.fori_loop(0, entry(PANEL), place, 0)
    lax.fori_loop(0, entry(PANEL), wait, 0)


def finish(table, lists, front, got, patch):
    return pl.pallas_call(
        finish_kernel,
        out_shape=jax.ShapeDtypeStruct((2048, 1024), F32),
        in_specs=[SMEM, SMEM, SMEM, HBM] + [VMEM] * 2,
        out_specs=HBM,
        scratch_shapes=[
            pltpu.VMEM((25, BLK, BLK), F32),
            pltpu.SemaphoreType.DMA((25,)),
            pltpu.SemaphoreType.DMA((25,)),
            pltpu.SemaphoreType.DMA(()),
        ],
        input_output_aliases={3: 0},
        compiler_params=params(12),
        cost_estimate=cost(0, 8 * MIB),
        name="finish",
    )(table, *lists, front, got, patch)


def swap(block, axis, partner):
    count = lax.axis_size(axis)
    return lax.ppermute(block, axis, [(i, partner(i)) for i in range(count)])


def fold(block, near):
    came = lax.ppermute(block[1], "col", [(c, c ^ 12) for c in range(8)])
    return jnp.where(near, block[0], came)


def local(front, children, child_maps, pivots, diag_inverses):
    here_row, here_col = lax.axis_index("row"), lax.axis_index("col")
    chip = here_row >> 1
    together = lax.optimization_barrier
    pieces = children.reshape(10, 2, BLK, 640)

    def by_row(block, mask):
        return swap(block, "row", lambda i: i ^ mask)

    def by_col(block, mask):
        return swap(block, "col", lambda i: i ^ mask)

    bits = (chip ^ (chip >> 1)) & 1, chip >> 1
    rings = [[(r, r ^ ((2, 6), (6, 2))[r % 2][k]) for r in range(8)] for k in range(2)]
    low = [jnp.where(here_row & 1 == 0, bits[k], bits[1 - k]) == 0 for k in range(2)]
    pivots, near, low = together((pivots, here_col < 8, low))

    def halve(part, step):
        size = part.shape[0] // 2
        leave = jnp.where(low[step], part[size:], part[:size])
        stay = jnp.where(low[step], part[:size], part[size:])
        return stay + lax.ppermute(leave, "row", rings[step])

    def double(part, step):
        came = lax.ppermute(part, "row", rings[step])
        first, second = jnp.where(low[step], part, came), jnp.where(low[step], came, part)
        return jnp.concatenate([first, second], axis=0)

    def gather_step(block, which, step):
        route = [
            (r * 16 + c, r * 16 + (c ^ ORDERS[r % 2][which][step]))
            for r in range(8)
            for c in range(16)
        ]
        return lax.ppermute(block, ("row", "col"), route)

    first = cut(child_maps, pieces)
    got0 = by_row(first, 4)
    *rest, panel, corner, away, table = prepare(child_maps, pivots, front, pieces, first)
    rest_a, rest_b = rest
    corner = corner + by_row(away, 1)
    corner = corner + (by_row(corner, 2) + (by_row(corner, 6) + by_row(corner, 4)))
    away_rows, marks, list_other = pivot_terms(child_maps, pivots, front, children)
    got0, away_rows, rest_a, marks, corner = together((got0, away_rows, rest_a, marks, corner))

    top, bottom = whole_panel(table, panel, got0)
    mine = fold((top, bottom), near)
    corner = fold((corner, corner), near)[None]
    got_a = by_row(rest_a, 4)
    own_rows, marks, list_mine = pivot_terms(child_maps, pivots, front, children, marks)
    total = own_rows + by_row(away_rows, 1)
    mine, corner, total, got_a = together((mine, corner, total, got_a))

    def corner_step(block, step):
        masks = ((4, 1, 3), (1, 3, 4))
        route = [
            (r * 16 + c, r * 16 + (c ^ masks[r % 2][step])) for r in range(8) for c in range(16)
        ]
        return jnp.concatenate([block, lax.ppermute(block, ("row", "col"), route)], axis=0)

    held = [mine[None, :PANEL], mine[None, PANEL:]]
    for k in range(2):
        came = [gather_step(held[w], w, k) for w in range(2)]
        held = [jnp.concatenate([h, c], axis=0) for h, c in zip(held, came)]
        corner = corner_step(corner, k)
    total = halve(total, 0)
    held, corner, total = together((held, corner, total))
    came = [gather_step(held[w], w, 2) for w in range(2)]
    corner = corner_step(corner, 2)
    total = double(halve(total, 1), 1)
    came, corner, total = together((came, corner, total))
    held_far = [gather_step(held[w], w, 3) for w in range(2)]
    front = extend(table, front, pieces, (got0, got_a, got_a))
    *factors, cross = corners(table, corner, by_row(corner, 1), diag_inverses)
    came, held_far, total, rest_b, factors, cross, front = together(
        (came, held_far, double(total, 0), rest_b, factors, cross, front)
    )
    came_far = [gather_step(came[w], w, 3) for w in range(2)]
    got_b = by_row(rest_b, 4)
    *right, patch = right_factor(table, total, by_row(total, 1), factors, cross)
    came_far, right, patch = together((came_far, right, patch))
    blocks = [(held[w], came[w], held_far[w], came_far[w]) for w in range(2)]
    front = update(table, front, blocks, right, marks).reshape(2048, 1024)
    return finish(table, (list_other, list_mine), front, got_b, patch)


def solution(mesh):
    return jax.shard_map(
        local,
        mesh=mesh,
        in_specs=(P("row", "col"), P("row", "col"), P(), P(), P()),
        out_specs=P("row", "col"),
        check_vma=False,
    )
```

```python
import functools

import jax
import jax.numpy as jnp
from jax import lax
from jax.experimental import pallas as pl
from jax.experimental.pallas import tpu as pltpu
from jax.sharding import PartitionSpec as P

BLK = 128
PANEL = 512
MIB = 1 << 20
F32 = jnp.float32
BF16 = jnp.bfloat16
SMEM = pl.BlockSpec(memory_space=pltpu.SMEM)
VMEM = pl.BlockSpec(memory_space=pltpu.VMEM)
HBM = pl.BlockSpec(memory_space=pltpu.HBM)
KEPT_AT = 0
GOT_AT = 16
KEPT_COL = 32
GOT_COL = 40
ROW, COL, SIDE = 48, 49, 50
GOT_ROW = 52


def split(x):
    high = x.astype(BF16)
    return high, (x - high.astype(F32)).astype(BF16)


def dot3(a, b):
    rows = a[0].shape[0]
    both = jnp.dot(jnp.concatenate(a, axis=0), b[0], preferred_element_type=F32)
    return both[:rows] + (both[rows:] + jnp.dot(a[0], b[1], preferred_element_type=F32))


def params(mib):
    return pltpu.CompilerParams(vmem_limit_bytes=mib * MIB)


def in_hbm(x):
    return pltpu.with_memory_space_constraint(x, pltpu.HBM)


def cost(flops, moved):
    return pl.CostEstimate(flops=flops, bytes_accessed=moved, transcendentals=0)


def first_block(maps, child, here_col):
    place, found = jnp.int32(0), jnp.int32(0)
    for d in range(5):
        hit = (maps[child, d * 16 + here_col] // 16 == 0).astype(jnp.int32)
        place, found = place + d * hit, found + hit
    return place, found


def cut_kernel(maps, pieces, first, sem):
    other = 1 - lax.axis_index("row") // 4
    place, _ = first_block(maps, 1 - other, lax.axis_index("col"))
    columns = pl.ds(pl.multiple_of(place * BLK, BLK), BLK)
    copy = pltpu.make_async_copy(pieces.at[:, other, :, columns], first, sem)
    copy.start()
    copy.wait()


def cut(maps, pieces):
    return pl.pallas_call(
        cut_kernel,
        out_shape=jax.ShapeDtypeStruct((10, BLK, BLK), F32),
        in_specs=[SMEM, HBM],
        out_specs=VMEM,
        scratch_shapes=[pltpu.SemaphoreType.DMA(())],
        compiler_params=params(4),
        cost_estimate=cost(0, MIB),
        name="cut",
    )(in_hbm(maps), in_hbm(pieces))


def prepare_kernel(
    maps, pivots, front, pieces, first, *refs,
):
    *rests, panel, own, away, table, sending, kept, total, sem = refs
    here_row, here_col = lax.axis_index("row"), lax.axis_index("col")
    side, core = here_row // 4, here_row % 2
    other = 1 - side
    place, found = first_block(maps, side, here_col)
    got_place, _ = first_block(maps, other, here_col)

    def columns(d):
        return pl.ds(pl.multiple_of(d * BLK, BLK), BLK)

    reads = [
        pltpu.make_async_copy(pieces.at[:, other], sending, sem.at[0]),
        pltpu.make_async_copy(pieces.at[:, side, :, columns(place)], kept, sem.at[1]),
        pltpu.make_async_copy(front.at[:, pl.ds(0, BLK)], panel, sem.at[2]),
    ]
    writes = []
    rest_a, rest_b = rests
    parts = (
        (0, 0, rest_a.at[pl.ds(0, 10)]),
        (1, 0, rest_a.at[pl.ds(10, 5)]),
        (1, 5, rest_b.at[pl.ds(0, 5)]),
        (2, 0, rest_b.at[pl.ds(5, 10)]),
        (3, 0, rest_b.at[pl.ds(15, 10)]),
    )
    for n, (j, start, target) in enumerate(parts):
        d = j + (j >= place).astype(jnp.int32)
        source = sending.at[pl.ds(start, target.shape[0]), :, columns(d)]
        writes.append(pltpu.make_async_copy(source, target, sem.at[3 + n]))
    for copy in reads:
        copy.start()
    for kk in range(16):
        table[KEPT_AT + kk] = -1
        table[GOT_AT + kk] = -1
    for m in range(10):
        table[KEPT_AT + maps[side, m * 8 + here_row] // 8] = m
        target = maps[other, m * 8 + here_row] // 8
        table[GOT_AT + target] = m
        table[GOT_ROW + m] = target
    for d in range(5):
        table[KEPT_COL + d] = maps[side, d * 16 + here_col] // 16
    table[GOT_COL] = maps[other, got_place * 16 + here_col] // 16
    for j in range(4):
        d = j + (j >= got_place).astype(jnp.int32)
        table[GOT_COL + 1 + j] = maps[other, d * 16 + here_col] // 16
    table[ROW] = here_row
    table[COL] = here_col
    table[SIDE] = side
    turned = pivots[...].T
    wanted = jnp.concatenate(
        [jnp.where(here_col < 4, turned[:, 4 + k : 5 + k], turned[:, k : k + 1]) for k in range(4)],
        axis=0,
    )
    block, offset = wanted >> 7, wanted & 127
    mine = jnp.where((block & 7) == here_row, (block >> 3) * BLK + offset, -1)
    sent = jnp.full_like(mine, -1)
    for m in range(10):
        hit = (block == maps[side, m * 8 + (here_row ^ 4)]) & (found > 0)
        sent = jnp.where(hit, m * BLK + offset, sent)
    reads[0].wait()
    for copy in writes:
        copy.start()
    reads[1].wait()
    reads[2].wait()

    @pl.when(found > 0)
    def _():
        for m in range(10):
            at = pl.multiple_of(maps[side, m * 8 + here_row] // 8 * BLK, BLK)
            panel[pl.ds(at, BLK), :] += kept[m]

    def rows_of(index, values, base):
        lane = lax.broadcasted_iota(jnp.int32, (PANEL, values.shape[0]), 1) + base
        chosen = jnp.where(lane == index, 1.0, 0.0).astype(BF16)
        both = jnp.concatenate(split(values), axis=1)
        return jnp.dot(chosen, both, preferred_element_type=F32)

    terms = jnp.zeros((PANEL, 2 * BLK), F32)
    for k in range(8):
        terms += rows_of(mine, panel[k * 256 : (k + 1) * 256, :], k * 256)
    for k in range(5):
        values = first[2 * k : 2 * k + 2].reshape(256, BLK)
        terms += rows_of(sent, values, k * 256)
    total[...] = terms[:, :BLK] + terms[:, BLK:]
    own[...] = total[pl.ds(pl.multiple_of(core * 256, 256), 256), :]
    away[...] = total[pl.ds(pl.multiple_of((1 - core) * 256, 256), 256), :]
    for copy in writes:
        copy.wait()


def prepare(maps, pivots, front, pieces, first):
    return pl.pallas_call(
        prepare_kernel,
        out_shape=[
            jax.ShapeDtypeStruct((15, BLK, BLK), F32),
            jax.ShapeDtypeStruct((25, BLK, BLK), F32),
            jax.ShapeDtypeStruct((2048, BLK), F32),
            jax.ShapeDtypeStruct((256, BLK), F32),
            jax.ShapeDtypeStruct((256, BLK), F32),
            jax.ShapeDtypeStruct((64,), jnp.int32),
        ],
        in_specs=[SMEM, VMEM, HBM, HBM, VMEM],
        out_specs=[HBM] * 2 + [VMEM, VMEM, VMEM, SMEM],
        scratch_shapes=[
            pltpu.VMEM((10, BLK, 640), F32),
            pltpu.VMEM((10, BLK, BLK), F32),
            pltpu.VMEM((PANEL, BLK), F32),
            pltpu.SemaphoreType.DMA((8,)),
        ],
        compiler_params=params(24),
        cost_estimate=cost(0, 9 * MIB),
        name="prepare",
    )(in_hbm(maps), in_hbm(pivots.reshape(8, BLK)), in_hbm(front), in_hbm(pieces), first)


def pivot_kernel(mine_half, maps, pivots, front, children, *refs):
    rows, marks, front_list, spread, inverse, child_list, sem, child_sem = refs[-8:]
    rows[...] = jnp.zeros_like(rows)
    marks[...] = refs[0][...] if mine_half else jnp.zeros_like(marks)
    here_row, here_col = lax.axis_index("row"), lax.axis_index("col")
    side, quarter, core = here_row // 4, here_row % 4, here_row % 2
    half = core if mine_half else 1 - core
    spread[...] = jnp.zeros_like(spread)

    def clear(b, carry):
        inverse[b] = -1
        return carry

    lax.fori_loop(0, 128, clear, 0, unroll=16)
    for k in range(20):
        inverse[maps[side, 4 * k + quarter]] = k

    def visit(p, counts):
        pivot = pivots[half * PANEL + p]
        block, offset = pivot >> 7, pivot & 127
        child_block = inverse[block]
        mine = (block & 7) == here_row
        shared = ((block & 3) == quarter) & (child_block >= 0)
        front_list[counts[0]] = (((block >> 3) * BLK + offset) << 9) | p
        child_list[counts[1]] = ((child_block * BLK + offset) << 9) | p
        return counts[0] + mine.astype(jnp.int32), counts[1] + shared.astype(jnp.int32)

    counts = lax.fori_loop(0, PANEL, visit, (jnp.int32(0), jnp.int32(0)), unroll=8)
    front_list[PANEL] = counts[0]
    mark = jnp.full((1, BLK), half + 1, jnp.int32).astype(F32)

    def take_front(n, carry):
        at, p = front_list[n] >> 9, front_list[n] & 511
        pltpu.make_async_copy(front.at[pl.ds(at, 1), :], rows.at[pl.ds(p, 1), :], sem).start()
        marks[pl.ds(at, 1), :] = mark
        return carry

    def take_child(n, carry):
        at, p = child_list[n] >> 9, child_list[n] & 511
        pltpu.make_async_copy(
            children.at[pl.ds(at, 1), :], spread.at[pl.ds(p, 1), :], child_sem
        ).start()
        return carry

    def wait(source, target, semaphore, count):
        def some(size):
            def body(_, carry):
                pltpu.make_async_copy(
                    source.at[pl.ds(0, size), :], target.at[pl.ds(0, size), :], semaphore
                ).wait()
                return carry

            return body

        lax.fori_loop(0, count // 16, some(16), 0)
        lax.fori_loop(0, count % 16, some(1), 0)

    lax.fori_loop(0, counts[0], take_front, 0)
    lax.fori_loop(0, counts[1], take_child, 0)
    wait(front, rows, sem, counts[0])
    wait(children, spread, child_sem, counts[1])
    for d in range(5):
        to = pl.ds(pl.multiple_of(maps[side, d * 16 + here_col] // 16 * BLK, BLK), BLK)
        rows[:, to] += spread[:, d * BLK : (d + 1) * BLK]


def pivot_terms(maps, pivots, front, children, *before):
    mine_half = len(before) > 0
    return pl.pallas_call(
        functools.partial(pivot_kernel, mine_half),
        out_shape=[
            jax.ShapeDtypeStruct((PANEL, 1024), F32),
            jax.ShapeDtypeStruct((2048, BLK), F32),
            jax.ShapeDtypeStruct((PANEL + 1,), jnp.int32),
        ],
        in_specs=[SMEM, SMEM, HBM, HBM] + [VMEM] * len(before),
        out_specs=[VMEM, VMEM, SMEM],
        scratch_shapes=[
            pltpu.VMEM((PANEL, 640), F32),
            pltpu.SMEM((128,), jnp.int32),
            pltpu.SMEM((PANEL + 1,), jnp.int32),
            pltpu.SemaphoreType.DMA(()),
            pltpu.SemaphoreType.DMA(()),
        ],
        compiler_params=params(12),
        cost_estimate=cost(0, 24 * MIB),
        name="pivot_terms_mine" if mine_half else "pivot_terms_other",
    )(in_hbm(maps), in_hbm(pivots), in_hbm(front), in_hbm(children), *before)


def panel_kernel(table, panel, got, top, bottom):
    top[...] = panel[:1024, :]
    bottom[...] = panel[1024:, :]

    @pl.when(table[GOT_COL] == 0)
    def _():
        for kk in range(16):
            m = table[GOT_AT + kk]
            half = top if kk < 8 else bottom
            at = kk % 8 * BLK

            @pl.when(m >= 0)
            def _(half=half, at=at, m=m):
                half[at : at + BLK, :] += got[m]


def whole_panel(table, panel, got):
    shape = jax.ShapeDtypeStruct((1024, BLK), F32)
    return pl.pallas_call(
        panel_kernel,
        out_shape=[shape, shape],
        in_specs=[SMEM, VMEM, VMEM],
        out_specs=[VMEM, VMEM],
        compiler_params=params(12),
        cost_estimate=cost(0, 3 * MIB),
        name="whole_panel",
    )(table, panel, got)


def flips(delta):
    return (delta & 1) ^ (delta >> 1), delta >> 1


def corner_kernel(table, own, swapped, inverses, factor_h, factor_l, cross):
    here_row, here_col = table[ROW], table[COL]
    core, x, y = here_row % 2, here_col % 4, here_col // 4
    mine = (y ^ (y >> 1)) & 1

    def corner(panel, half):
        blocks = []
        for xx in range(4):
            one, three = flips(xx ^ x)
            pair = mine ^ panel
            slot = jnp.where(half == 0, pair | (one << 1) | (three << 2), one | (three << 1) | (pair << 2))
            blocks.append(jnp.where(core == half, own[slot], swapped[slot]))
        return jnp.concatenate(blocks, axis=1)

    for p in range(2):
        factor_h[p], factor_l[p] = split(inverses[p])
    for half in range(2):
        rows = slice(half * 256, (half + 1) * 256)
        factor_h[2, rows, :], factor_l[2, rows, :] = split(corner(1, half))
        cross[rows, :] = dot3(split(corner(0, half)), (factor_h[0], factor_l[0]))


def corners(table, own, swapped, inverses):
    return pl.pallas_call(
        corner_kernel,
        out_shape=[
            jax.ShapeDtypeStruct((3, PANEL, PANEL), BF16),
            jax.ShapeDtypeStruct((3, PANEL, PANEL), BF16),
            jax.ShapeDtypeStruct((PANEL, PANEL), F32),
        ],
        in_specs=[SMEM, VMEM, VMEM, VMEM],
        out_specs=[VMEM] * 3,
        compiler_params=params(20),
        cost_estimate=cost(6 * PANEL**3, 8 * MIB),
        name="corners",
    )(table, own, swapped, inverses)


def factor_kernel(table, own, swapped, factor_h, factor_l, cross, high, low, patch):
    here_row, col = table[ROW], table[COL]
    core, slot = here_row % 2, col % 4
    inside = lax.broadcasted_iota(jnp.int32, (PANEL, 1024), 1) < BLK

    def mine(x):
        out = x[:, :BLK]
        for s in range(1, 4):
            out = jnp.where(slot == s, x[:, s * BLK : (s + 1) * BLK], out)
        return out

    def begin_with(block, x):
        return jnp.concatenate([block, x[:, BLK:]], axis=1)

    def factor(n):
        return factor_h[n], factor_l[n]

    def factor_columns(n):
        return mine(factor_h[n].astype(F32)) + mine(factor_l[n].astype(F32))

    first = jnp.where(core == 0, own[...], swapped[...])
    first = jnp.where(inside & (col < 4), 0.0, first)
    second = jnp.where(core == 0, swapped[...], own[...])
    second = second - dot3(split(cross[...]), split(first))
    patch[...] = begin_with(jnp.where(col < 4, mine(cross[...]), second[:, :BLK]), second)
    second = jnp.where(inside & (col < 8), 0.0, second)
    right = dot3(factor(1), split(second))
    in_second = (col >= 4) & (col < 8)
    right = begin_with(jnp.where(in_second, factor_columns(1), right[:, :BLK]), right)
    terms = split(right)
    high[PANEL:], low[PANEL:] = terms
    first = jnp.where(inside & (col < 8), 0.0, first)
    left = dot3(factor(0), split(first - dot3(factor(2), terms)))
    left = begin_with(jnp.where(col < 4, factor_columns(0), left[:, :BLK]), left)
    high[:PANEL], low[:PANEL] = split(left)


def right_factor(table, own, swapped, factors, cross):
    shape = jax.ShapeDtypeStruct((1024, 1024), BF16)
    return pl.pallas_call(
        factor_kernel,
        out_shape=[shape, shape, jax.ShapeDtypeStruct((PANEL, 1024), F32)],
        in_specs=[SMEM] + [VMEM] * 5,
        out_specs=[VMEM] * 3,
        compiler_params=params(24),
        cost_estimate=cost(PANEL * PANEL * 1024, 4 * MIB),
        name="right_factor",
    )(table, own, swapped, *factors, cross)


def block_at(base, half, t, s):
    return jnp.maximum(s[base + half * 8 + t], 0)


ARRIVED = (0, 0, 10, 0), (1, 0, 10, 0), (2, 0, 5, 10)


def extend_kernel(table, front, *refs):
    out, refs = refs[-1], refs[:-1]
    kept, *got = (refs[2 * k : 2 * k + 2] for k in range(1 + len(ARRIVED)))
    step = pl.program_id(0)
    out[...] = front[...]
    for half in range(2):

        @pl.when(table[KEPT_AT + half * 8 + step] >= 0)
        def _(half=half):
            for d in range(5):
                to = pl.ds(pl.multiple_of(table[KEPT_COL + d] * BLK, BLK), BLK)
                out[half, :, to] += kept[half][0, 0, :, d * BLK : (d + 1) * BLK]

        m = table[GOT_AT + half * 8 + step]
        for j, (column, start, count, _) in enumerate(ARRIVED):

            @pl.when((m >= start) & (m < start + count))
            def _(half=half, j=j, column=column):
                to = pl.ds(pl.multiple_of(table[GOT_COL + column] * BLK, BLK), BLK)
                out[half, :, to] += got[j][half][0]


def extend(table, front, pieces, got):
    def kept_at(half):
        return lambda t, s: (block_at(KEPT_AT, half, t, s), s[SIDE], 0, 0)

    def got_at(half, start, count, slot):
        return lambda t, s: (
            jnp.clip(s[GOT_AT + half * 8 + t] - start, 0, count - 1) + slot, 0, 0
        )

    tile = pl.BlockSpec((2, BLK, 1024), lambda t, s: (0, t, 0))
    kept_specs = [pl.BlockSpec((1, 1, BLK, 640), kept_at(half)) for half in range(2)]
    got_specs = [
        pl.BlockSpec((1, BLK, BLK), got_at(half, start, count, slot))
        for _, start, count, slot in ARRIVED
        for half in range(2)
    ]
    return pl.pallas_call(
        extend_kernel,
        out_shape=pltpu.HBM((2, 1024, 1024), F32),
        grid_spec=pltpu.PrefetchScalarGridSpec(
            num_scalar_prefetch=1,
            grid=(8,),
            in_specs=[tile, *kept_specs, *got_specs],
            out_specs=tile,
        ),
        compiler_params=params(20),
        cost_estimate=cost(0, MIB),
        name="extend",
    )(table, in_hbm(front.reshape(2, 1024, 1024)), *[in_hbm(pieces)] * 2, *[g for g in got for _ in range(2)])


ORDERS = ((1, 3, 4, 12), (3, 1, 12, 4)), ((4, 12, 1, 3), (12, 4, 3, 1))


def update_kernel(table, front, *refs):
    blocks = refs[:4], refs[4:8]
    right_h, right_l, marks, out, panels = refs[8:]
    step = pl.program_id(0)
    span = pl.ds(pl.multiple_of(step % 2 * 256, 256), 256)
    col, core = table[COL], table[ROW] % 2

    def assemble(which):
        held, came, held_far, came_far = blocks[which]
        for c in range(16):
            one_x, three_x = flips((c ^ col) & 3)
            one_y, three_y = flips((c ^ col) >> 2)
            bits = {1: one_x, 3: three_x, 4: one_y, 12: three_y}
            even, odd = (ORDERS[q][which] for q in range(2))
            flip = [jnp.where(core == 0, bits[e], bits[o]) for e, o in zip(even, odd)]
            slot = flip[0] | (flip[1] << 1)
            later, far = flip[2] == 1, flip[3] == 1
            near_block = jnp.where(later, came[slot, span, :], held[slot, span, :])
            far_block = jnp.where(later, came_far[slot, span, :], held_far[slot, span, :])
            block = jnp.where(far, far_block, near_block)
            y, x = c // 4, c % 4
            rows = slice(0, 256) if y < 2 else slice(256, PANEL)
            first = min(y, 3 - y) * PANEL + x * BLK
            columns = slice(first, first + BLK)
            panels[0, rows, columns], panels[1, rows, columns] = split(block)

    for which in range(2):
        pl.when(step // 2 == which)(functools.partial(assemble, which))

    active = marks[...] == 0
    for piece in range(4):
        wide = slice(piece * 256, (piece + 1) * 256)
        change = dot3((panels[0], panels[1]), (right_h[:, wide], right_l[:, wide]))
        change = change.reshape(2, 256, 256)
        for j in range(2):
            columns = slice(piece * 256 + j * BLK, piece * 256 + (j + 1) * BLK)
            before, part = front[:, :, columns], change[:, :, j * BLK : (j + 1) * BLK]
            after = before - part
            if piece == 0 and j == 0:
                after = jnp.where(col < 8, part, after)
            out[:, :, columns] = jnp.where(active, after, before)


def update(table, front, blocks, right, marks):
    tile = pl.BlockSpec((2, 256, 1024), lambda t, s: (0, t, 0))
    return pl.pallas_call(
        update_kernel,
        out_shape=pltpu.HBM((2, 1024, 1024), F32),
        grid_spec=pltpu.PrefetchScalarGridSpec(
            num_scalar_prefetch=1,
            grid=(4,),
            in_specs=[
                tile,
                *[VMEM] * 10,
                pl.BlockSpec((2, 256, BLK), lambda t, s: (0, t, 0)),
            ],
            out_specs=tile,
            scratch_shapes=[pltpu.VMEM((2, PANEL, 1024), BF16)],
        ),
        compiler_params=params(24),
        cost_estimate=cost(2048 * 1024 * 1024, 4 * MIB),
        name="update",
    )(table, in_hbm(front), *blocks[0], *blocks[1], *right, marks.reshape(2, 1024, BLK))


def finish_kernel(
    table, list_other, list_mine, front, got, patch,
    out, held, read_sem, write_sem, sem,
):
    del front
    core = table[ROW] % 2
    copies = []
    places = [(2, m) for m in range(5, 10)] + [(j, m) for j in (3, 4) for m in range(10)]
    for n, (column, m) in enumerate(places):
        columns = pl.ds(pl.multiple_of(table[GOT_COL + column] * BLK, BLK), BLK)
        rows = pl.ds(pl.multiple_of(table[GOT_ROW + m] * BLK, BLK), BLK)
        there, here = out.at[rows, columns], held.at[n]
        read = pltpu.make_async_copy(there, here, read_sem.at[n])
        write = pltpu.make_async_copy(here, there, write_sem.at[n])
        copies.append((read, write))
    for read, _ in copies:
        read.start()
    for n, (read, write) in enumerate(copies):
        read.wait()
        held[n] += got[n]
        write.start()
    for _, write in copies:
        write.wait()

    def entry(n):
        return jnp.where(core == 0, list_other[n], list_mine[n])

    def place(n, carry):
        at, p = entry(n) >> 9, entry(n) & 511
        pltpu.make_async_copy(patch.at[pl.ds(p, 1), :], out.at[pl.ds(at, 1), :], sem).start()
        return carry

    def wait(_, carry):
        pltpu.make_async_copy(patch.at[pl.ds(0, 1), :], out.at[pl.ds(0, 1), :], sem).wait()
        return carry

    lax.fori_loop(0, entry(PANEL), place, 0)
    lax.fori_loop(0, entry(PANEL), wait, 0)


def finish(table, lists, front, got, patch):
    return pl.pallas_call(
        finish_kernel,
        out_shape=jax.ShapeDtypeStruct((2048, 1024), F32),
        in_specs=[SMEM, SMEM, SMEM, HBM] + [VMEM] * 2,
        out_specs=HBM,
        scratch_shapes=[
            pltpu.VMEM((25, BLK, BLK), F32),
            pltpu.SemaphoreType.DMA((25,)),
            pltpu.SemaphoreType.DMA((25,)),
            pltpu.SemaphoreType.DMA(()),
        ],
        input_output_aliases={3: 0},
        compiler_params=params(12),
        cost_estimate=cost(0, 8 * MIB),
        name="finish",
    )(table, *lists, front, got, patch)


def swap(block, axis, partner):
    count = lax.axis_size(axis)
    return lax.ppermute(block, axis, [(i, partner(i)) for i in range(count)])


def fold(block, near):
    came = lax.ppermute(block[1], "col", [(c, c ^ 12) for c in range(8)])
    return jnp.where(near, block[0], came)


def local(front, children, child_maps, pivots, diag_inverses):
    here_row, here_col = lax.axis_index("row"), lax.axis_index("col")
    chip = here_row >> 1
    together = lax.optimization_barrier
    pieces = children.reshape(10, 2, BLK, 640)

    def by_row(block, mask):
        return swap(block, "row", lambda i: i ^ mask)

    def by_col(block, mask):
        return swap(block, "col", lambda i: i ^ mask)

    bits = (chip ^ (chip >> 1)) & 1, chip >> 1
    rings = [[(r, r ^ ((2, 6), (6, 2))[r % 2][k]) for r in range(8)] for k in range(2)]
    low = [jnp.where(here_row & 1 == 0, bits[k], bits[1 - k]) == 0 for k in range(2)]
    pivots, near, low = together((pivots, here_col < 8, low))

    def halve(part, step):
        size = part.shape[0] // 2
        leave = jnp.where(low[step], part[size:], part[:size])
        stay = jnp.where(low[step], part[:size], part[size:])
        return stay + lax.ppermute(leave, "row", rings[step])

    def double(part, step):
        came = lax.ppermute(part, "row", rings[step])
        first, second = jnp.where(low[step], part, came), jnp.where(low[step], came, part)
        return jnp.concatenate([first, second], axis=0)

    def gather_step(block, which, step):
        route = [
            (r * 16 + c, r * 16 + (c ^ ORDERS[r % 2][which][step]))
            for r in range(8)
            for c in range(16)
        ]
        return lax.ppermute(block, ("row", "col"), route)

    first = cut(child_maps, pieces)
    got0 = by_row(first, 4)
    *rest, panel, corner, away, table = prepare(child_maps, pivots, front, pieces, first)
    rest_a, rest_b = rest
    corner = corner + by_row(away, 1)
    corner = corner + (by_row(corner, 2) + (by_row(corner, 6) + by_row(corner, 4)))
    away_rows, marks, list_other = pivot_terms(child_maps, pivots, front, children)
    got0, away_rows, rest_a, marks, corner = together((got0, away_rows, rest_a, marks, corner))

    top, bottom = whole_panel(table, panel, got0)
    mine = fold((top, bottom), near)
    corner = fold((corner, corner), near)[None]
    got_a = by_row(rest_a, 4)
    own_rows, marks, list_mine = pivot_terms(child_maps, pivots, front, children, marks)
    total = own_rows + by_row(away_rows, 1)
    mine, corner, total, got_a = together((mine, corner, total, got_a))

    def corner_step(block, step):
        masks = ((4, 1, 3), (1, 3, 4))
        route = [
            (r * 16 + c, r * 16 + (c ^ masks[r % 2][step])) for r in range(8) for c in range(16)
        ]
        return jnp.concatenate([block, lax.ppermute(block, ("row", "col"), route)], axis=0)

    held = [mine[None, :PANEL], mine[None, PANEL:]]
    for k in range(2):
        came = [gather_step(held[w], w, k) for w in range(2)]
        held = [jnp.concatenate([h, c], axis=0) for h, c in zip(held, came)]
        corner = corner_step(corner, k)
    total = halve(total, 0)
    held, corner, total = together((held, corner, total))
    came = [gather_step(held[w], w, 2) for w in range(2)]
    corner = corner_step(corner, 2)
    total = double(halve(total, 1), 1)
    came, corner, total = together((came, corner, total))
    held_far = [gather_step(held[w], w, 3) for w in range(2)]
    front = extend(table, front, pieces, (got0, got_a, got_a))
    *factors, cross = corners(table, corner, by_row(corner, 1), diag_inverses)
    came, held_far, total, rest_b, factors, cross, front = together(
        (came, held_far, double(total, 0), rest_b, factors, cross, front)
    )
    came_far = [gather_step(came[w], w, 3) for w in range(2)]
    got_b = by_row(rest_b, 4)
    *right, patch = right_factor(table, total, by_row(total, 1), factors, cross)
    came_far, right, patch = together((came_far, right, patch))
    blocks = [(held[w], came[w], held_far[w], came_far[w]) for w in range(2)]
    front = update(table, front, blocks, right, marks).reshape(2048, 1024)
    return finish(table, (list_other, list_mine), front, got_b, patch)


def solution(mesh):
    return jax.shard_map(
        local,
        mesh=mesh,
        in_specs=(P("row", "col"), P("row", "col"), P(), P(), P()),
        out_specs=P("row", "col"),
        check_vma=False,
    )
```

```python
import functools

import jax
import jax.numpy as jnp
from jax import lax
from jax.experimental import pallas as pl
from jax.experimental.pallas import tpu as pltpu
from jax.sharding import PartitionSpec as P

BLK = 128
PANEL = 512
MIB = 1 << 20
F32 = jnp.float32
BF16 = jnp.bfloat16
SMEM = pl.BlockSpec(memory_space=pltpu.SMEM)
VMEM = pl.BlockSpec(memory_space=pltpu.VMEM)
HBM = pl.BlockSpec(memory_space=pltpu.HBM)
KEPT_AT = 0
GOT_AT = 16
KEPT_COL = 32
GOT_COL = 40
ROW, COL, SIDE = 48, 49, 50
GOT_ROW = 52


def split(x):
    high = x.astype(BF16)
    return high, (x - high.astype(F32)).astype(BF16)


def dot3(a, b):
    rows = a[0].shape[0]
    both = jnp.dot(jnp.concatenate(a, axis=0), b[0], preferred_element_type=F32)
    return both[:rows] + (both[rows:] + jnp.dot(a[0], b[1], preferred_element_type=F32))


def params(mib):
    return pltpu.CompilerParams(vmem_limit_bytes=mib * MIB)


def in_hbm(x):
    return pltpu.with_memory_space_constraint(x, pltpu.HBM)


def cost(flops, moved):
    return pl.CostEstimate(flops=flops, bytes_accessed=moved, transcendentals=0)


def first_block(maps, child, here_col):
    place, found = jnp.int32(0), jnp.int32(0)
    for d in range(5):
        hit = (maps[child, d * 16 + here_col] // 16 == 0).astype(jnp.int32)
        place, found = place + d * hit, found + hit
    return place, found


def cut_kernel(maps, pieces, first, sem):
    other = 1 - lax.axis_index("row") // 4
    place, _ = first_block(maps, 1 - other, lax.axis_index("col"))
    columns = pl.ds(pl.multiple_of(place * BLK, BLK), BLK)
    copy = pltpu.make_async_copy(pieces.at[:, other, :, columns], first, sem)
    copy.start()
    copy.wait()


def cut(maps, pieces):
    return pl.pallas_call(
        cut_kernel,
        out_shape=jax.ShapeDtypeStruct((10, BLK, BLK), F32),
        in_specs=[SMEM, HBM],
        out_specs=VMEM,
        scratch_shapes=[pltpu.SemaphoreType.DMA(())],
        compiler_params=params(4),
        cost_estimate=cost(0, MIB),
        name="cut",
    )(in_hbm(maps), in_hbm(pieces))


def prepare_kernel(
    maps, pivots, front, pieces, first, *refs,
):
    *rests, panel, own, away, table, sending, kept, total, sem = refs
    here_row, here_col = lax.axis_index("row"), lax.axis_index("col")
    side, core = here_row // 4, here_row % 2
    other = 1 - side
    place, found = first_block(maps, side, here_col)
    got_place, _ = first_block(maps, other, here_col)

    def columns(d):
        return pl.ds(pl.multiple_of(d * BLK, BLK), BLK)

    reads = [
        pltpu.make_async_copy(pieces.at[:, other], sending, sem.at[0]),
        pltpu.make_async_copy(pieces.at[:, side, :, columns(place)], kept, sem.at[1]),
        pltpu.make_async_copy(front.at[:, pl.ds(0, BLK)], panel, sem.at[2]),
    ]
    writes = []
    rest_a, rest_b = rests
    parts = (
        (0, 0, rest_a.at[pl.ds(0, 10)]),
        (1, 0, rest_a.at[pl.ds(10, 5)]),
        (1, 5, rest_b.at[pl.ds(0, 5)]),
        (2, 0, rest_b.at[pl.ds(5, 10)]),
        (3, 0, rest_b.at[pl.ds(15, 10)]),
    )
    for n, (j, start, target) in enumerate(parts):
        d = j + (j >= place).astype(jnp.int32)
        source = sending.at[pl.ds(start, target.shape[0]), :, columns(d)]
        writes.append(pltpu.make_async_copy(source, target, sem.at[3 + n]))
    for copy in reads:
        copy.start()
    for kk in range(16):
        table[KEPT_AT + kk] = -1
        table[GOT_AT + kk] = -1
    for m in range(10):
        table[KEPT_AT + maps[side, m * 8 + here_row] // 8] = m
        target = maps[other, m * 8 + here_row] // 8
        table[GOT_AT + target] = m
        table[GOT_ROW + m] = target
    for d in range(5):
        table[KEPT_COL + d] = maps[side, d * 16 + here_col] // 16
    table[GOT_COL] = maps[other, got_place * 16 + here_col] // 16
    for j in range(4):
        d = j + (j >= got_place).astype(jnp.int32)
        table[GOT_COL + 1 + j] = maps[other, d * 16 + here_col] // 16
    table[ROW] = here_row
    table[COL] = here_col
    table[SIDE] = side
    turned = pivots[...].T
    wanted = jnp.concatenate(
        [jnp.where(here_col < 4, turned[:, 4 + k : 5 + k], turned[:, k : k + 1]) for k in range(4)],
        axis=0,
    )
    block, offset = wanted >> 7, wanted & 127
    mine = jnp.where((block & 7) == here_row, (block >> 3) * BLK + offset, -1)
    sent = jnp.full_like(mine, -1)
    for m in range(10):
        hit = (block == maps[side, m * 8 + (here_row ^ 4)]) & (found > 0)
        sent = jnp.where(hit, m * BLK + offset, sent)
    reads[0].wait()
    for copy in writes:
        copy.start()
    reads[1].wait()
    reads[2].wait()

    @pl.when(found > 0)
    def _():
        for m in range(10):
            at = pl.multiple_of(maps[side, m * 8 + here_row] // 8 * BLK, BLK)
            panel[pl.ds(at, BLK), :] += kept[m]

    def rows_of(index, values, base):
        lane = lax.broadcasted_iota(jnp.int32, (PANEL, values.shape[0]), 1) + base
        chosen = jnp.where(lane == index, 1.0, 0.0).astype(BF16)
        both = jnp.concatenate(split(values), axis=1)
        return jnp.dot(chosen, both, preferred_element_type=F32)

    terms = jnp.zeros((PANEL, 2 * BLK), F32)
    for k in range(8):
        terms += rows_of(mine, panel[k * 256 : (k + 1) * 256, :], k * 256)
    for k in range(5):
        values = first[2 * k : 2 * k + 2].reshape(256, BLK)
        terms += rows_of(sent, values, k * 256)
    total[...] = terms[:, :BLK] + terms[:, BLK:]
    own[...] = total[pl.ds(pl.multiple_of(core * 256, 256), 256), :]
    away[...] = total[pl.ds(pl.multiple_of((1 - core) * 256, 256), 256), :]
    for copy in writes:
        copy.wait()


def prepare(maps, pivots, front, pieces, first):
    return pl.pallas_call(
        prepare_kernel,
        out_shape=[
            jax.ShapeDtypeStruct((15, BLK, BLK), F32),
            jax.ShapeDtypeStruct((25, BLK, BLK), F32),
            jax.ShapeDtypeStruct((2048, BLK), F32),
            jax.ShapeDtypeStruct((256, BLK), F32),
            jax.ShapeDtypeStruct((256, BLK), F32),
            jax.ShapeDtypeStruct((64,), jnp.int32),
        ],
        in_specs=[SMEM, VMEM, HBM, HBM, VMEM],
        out_specs=[HBM] * 2 + [VMEM, VMEM, VMEM, SMEM],
        scratch_shapes=[
            pltpu.VMEM((10, BLK, 640), F32),
            pltpu.VMEM((10, BLK, BLK), F32),
            pltpu.VMEM((PANEL, BLK), F32),
            pltpu.SemaphoreType.DMA((8,)),
        ],
        compiler_params=params(24),
        cost_estimate=cost(0, 9 * MIB),
        name="prepare",
    )(in_hbm(maps), in_hbm(pivots.reshape(8, BLK)), in_hbm(front), in_hbm(pieces), first)


def pivot_kernel(mine_half, maps, pivots, front, children, *refs):
    rows, marks, front_list, spread, inverse, child_list, sem, child_sem = refs[-8:]
    rows[...] = jnp.zeros_like(rows)
    marks[...] = refs[0][...] if mine_half else jnp.zeros_like(marks)
    here_row, here_col = lax.axis_index("row"), lax.axis_index("col")
    side, quarter, core = here_row // 4, here_row % 4, here_row % 2
    half = core if mine_half else 1 - core
    spread[...] = jnp.zeros_like(spread)

    def clear(b, carry):
        inverse[b] = -1
        return carry

    lax.fori_loop(0, 128, clear, 0, unroll=16)
    for k in range(20):
        inverse[maps[side, 4 * k + quarter]] = k

    def visit(p, counts):
        pivot = pivots[half * PANEL + p]
        block, offset = pivot >> 7, pivot & 127
        child_block = inverse[block]
        mine = (block & 7) == here_row
        shared = ((block & 3) == quarter) & (child_block >= 0)
        front_list[counts[0]] = (((block >> 3) * BLK + offset) << 9) | p
        child_list[counts[1]] = ((child_block * BLK + offset) << 9) | p
        return counts[0] + mine.astype(jnp.int32), counts[1] + shared.astype(jnp.int32)

    counts = lax.fori_loop(0, PANEL, visit, (jnp.int32(0), jnp.int32(0)), unroll=8)
    front_list[PANEL] = counts[0]
    mark = jnp.full((1, BLK), half + 1, jnp.int32).astype(F32)

    def take_front(n, carry):
        at, p = front_list[n] >> 9, front_list[n] & 511
        pltpu.make_async_copy(front.at[pl.ds(at, 1), :], rows.at[pl.ds(p, 1), :], sem).start()
        marks[pl.ds(at, 1), :] = mark
        return carry

    def take_child(n, carry):
        at, p = child_list[n] >> 9, child_list[n] & 511
        pltpu.make_async_copy(
            children.at[pl.ds(at, 1), :], spread.at[pl.ds(p, 1), :], child_sem
        ).start()
        return carry

    def wait(source, target, semaphore, count):
        def some(size):
            def body(_, carry):
                pltpu.make_async_copy(
                    source.at[pl.ds(0, size), :], target.at[pl.ds(0, size), :], semaphore
                ).wait()
                return carry

            return body

        lax.fori_loop(0, count // 16, some(16), 0)
        lax.fori_loop(0, count % 16, some(1), 0)

    lax.fori_loop(0, counts[0], take_front, 0)
    lax.fori_loop(0, counts[1], take_child, 0)
    wait(front, rows, sem, counts[0])
    wait(children, spread, child_sem, counts[1])
    for d in range(5):
        to = pl.ds(pl.multiple_of(maps[side, d * 16 + here_col] // 16 * BLK, BLK), BLK)
        rows[:, to] += spread[:, d * BLK : (d + 1) * BLK]


def pivot_terms(maps, pivots, front, children, *before):
    mine_half = len(before) > 0
    return pl.pallas_call(
        functools.partial(pivot_kernel, mine_half),
        out_shape=[
            jax.ShapeDtypeStruct((PANEL, 1024), F32),
            jax.ShapeDtypeStruct((2048, BLK), F32),
            jax.ShapeDtypeStruct((PANEL + 1,), jnp.int32),
        ],
        in_specs=[SMEM, SMEM, HBM, HBM] + [VMEM] * len(before),
        out_specs=[VMEM, VMEM, SMEM],
        scratch_shapes=[
            pltpu.VMEM((PANEL, 640), F32),
            pltpu.SMEM((128,), jnp.int32),
            pltpu.SMEM((PANEL + 1,), jnp.int32),
            pltpu.SemaphoreType.DMA(()),
            pltpu.SemaphoreType.DMA(()),
        ],
        compiler_params=params(12),
        cost_estimate=cost(0, 24 * MIB),
        name="pivot_terms_mine" if mine_half else "pivot_terms_other",
    )(in_hbm(maps), in_hbm(pivots), in_hbm(front), in_hbm(children), *before)


def panel_kernel(table, panel, got, top, bottom):
    top[...] = panel[:1024, :]
    bottom[...] = panel[1024:, :]

    @pl.when(table[GOT_COL] == 0)
    def _():
        for kk in range(16):
            m = table[GOT_AT + kk]
            half = top if kk < 8 else bottom
            at = kk % 8 * BLK

            @pl.when(m >= 0)
            def _(half=half, at=at, m=m):
                half[at : at + BLK, :] += got[m]


def whole_panel(table, panel, got):
    shape = jax.ShapeDtypeStruct((1024, BLK), F32)
    return pl.pallas_call(
        panel_kernel,
        out_shape=[shape, shape],
        in_specs=[SMEM, VMEM, VMEM],
        out_specs=[VMEM, VMEM],
        compiler_params=params(12),
        cost_estimate=cost(0, 3 * MIB),
        name="whole_panel",
    )(table, panel, got)


def flips(delta):
    return (delta & 1) ^ (delta >> 1), delta >> 1


def corner_kernel(table, own, swapped, inverses, factor_h, factor_l, cross):
    here_row, here_col = table[ROW], table[COL]
    core, x, y = here_row % 2, here_col % 4, here_col // 4
    mine = (y ^ (y >> 1)) & 1

    def corner(panel, half):
        blocks = []
        for xx in range(4):
            one, three = flips(xx ^ x)
            pair = mine ^ panel
            slot = jnp.where(half == 0, pair | (one << 1) | (three << 2), one | (three << 1) | (pair << 2))
            blocks.append(jnp.where(core == half, own[slot], swapped[slot]))
        return jnp.concatenate(blocks, axis=1)

    for p in range(2):
        factor_h[p], factor_l[p] = split(inverses[p])
    for half in range(2):
        rows = slice(half * 256, (half + 1) * 256)
        factor_h[2, rows, :], factor_l[2, rows, :] = split(corner(1, half))
        cross[rows, :] = dot3(split(corner(0, half)), (factor_h[0], factor_l[0]))


def corners(table, own, swapped, inverses):
    return pl.pallas_call(
        corner_kernel,
        out_shape=[
            jax.ShapeDtypeStruct((3, PANEL, PANEL), BF16),
            jax.ShapeDtypeStruct((3, PANEL, PANEL), BF16),
            jax.ShapeDtypeStruct((PANEL, PANEL), F32),
        ],
        in_specs=[SMEM, VMEM, VMEM, VMEM],
        out_specs=[VMEM] * 3,
        compiler_params=params(20),
        cost_estimate=cost(6 * PANEL**3, 8 * MIB),
        name="corners",
    )(table, own, swapped, inverses)


def factor_kernel(table, own, swapped, factor_h, factor_l, cross, high, low, patch):
    here_row, col = table[ROW], table[COL]
    core, slot = here_row % 2, col % 4
    inside = lax.broadcasted_iota(jnp.int32, (PANEL, 1024), 1) < BLK

    def mine(x):
        out = x[:, :BLK]
        for s in range(1, 4):
            out = jnp.where(slot == s, x[:, s * BLK : (s + 1) * BLK], out)
        return out

    def begin_with(block, x):
        return jnp.concatenate([block, x[:, BLK:]], axis=1)

    def factor(n):
        return factor_h[n], factor_l[n]

    def factor_columns(n):
        return mine(factor_h[n].astype(F32)) + mine(factor_l[n].astype(F32))

    first = jnp.where(core == 0, own[...], swapped[...])
    first = jnp.where(inside & (col < 4), 0.0, first)
    second = jnp.where(core == 0, swapped[...], own[...])
    second = second - dot3(split(cross[...]), split(first))
    patch[...] = begin_with(jnp.where(col < 4, mine(cross[...]), second[:, :BLK]), second)
    second = jnp.where(inside & (col < 8), 0.0, second)
    right = dot3(factor(1), split(second))
    in_second = (col >= 4) & (col < 8)
    right = begin_with(jnp.where(in_second, factor_columns(1), right[:, :BLK]), right)
    terms = split(right)
    high[PANEL:], low[PANEL:] = terms
    first = jnp.where(inside & (col < 8), 0.0, first)
    left = dot3(factor(0), split(first - dot3(factor(2), terms)))
    left = begin_with(jnp.where(col < 4, factor_columns(0), left[:, :BLK]), left)
    high[:PANEL], low[:PANEL] = split(left)


def right_factor(table, own, swapped, factors, cross):
    shape = jax.ShapeDtypeStruct((1024, 1024), BF16)
    return pl.pallas_call(
        factor_kernel,
        out_shape=[shape, shape, jax.ShapeDtypeStruct((PANEL, 1024), F32)],
        in_specs=[SMEM] + [VMEM] * 5,
        out_specs=[VMEM] * 3,
        compiler_params=params(24),
        cost_estimate=cost(PANEL * PANEL * 1024, 4 * MIB),
        name="right_factor",
    )(table, own, swapped, *factors, cross)


def block_at(base, half, t, s):
    return jnp.maximum(s[base + half * 8 + t], 0)


ARRIVED = (0, 0, 10, 0), (1, 0, 10, 0), (2, 0, 5, 10)


def extend_kernel(table, front, *refs):
    out, refs = refs[-1], refs[:-1]
    kept, *got = (refs[2 * k : 2 * k + 2] for k in range(1 + len(ARRIVED)))
    step = pl.program_id(0)
    out[...] = front[...]
    for half in range(2):

        @pl.when(table[KEPT_AT + half * 8 + step] >= 0)
        def _(half=half):
            for d in range(5):
                to = pl.ds(pl.multiple_of(table[KEPT_COL + d] * BLK, BLK), BLK)
                out[half, :, to] += kept[half][0, 0, :, d * BLK : (d + 1) * BLK]

        m = table[GOT_AT + half * 8 + step]
        for j, (column, start, count, _) in enumerate(ARRIVED):

            @pl.when((m >= start) & (m < start + count))
            def _(half=half, j=j, column=column):
                to = pl.ds(pl.multiple_of(table[GOT_COL + column] * BLK, BLK), BLK)
                out[half, :, to] += got[j][half][0]


def extend(table, front, pieces, got):
    def kept_at(half):
        return lambda t, s: (block_at(KEPT_AT, half, t, s), s[SIDE], 0, 0)

    def got_at(half, start, count, slot):
        return lambda t, s: (
            jnp.clip(s[GOT_AT + half * 8 + t] - start, 0, count - 1) + slot, 0, 0
        )

    tile = pl.BlockSpec((2, BLK, 1024), lambda t, s: (0, t, 0))
    kept_specs = [pl.BlockSpec((1, 1, BLK, 640), kept_at(half)) for half in range(2)]
    got_specs = [
        pl.BlockSpec((1, BLK, BLK), got_at(half, start, count, slot))
        for _, start, count, slot in ARRIVED
        for half in range(2)
    ]
    return pl.pallas_call(
        extend_kernel,
        out_shape=pltpu.HBM((2, 1024, 1024), F32),
        grid_spec=pltpu.PrefetchScalarGridSpec(
            num_scalar_prefetch=1,
            grid=(8,),
            in_specs=[tile, *kept_specs, *got_specs],
            out_specs=tile,
        ),
        compiler_params=params(20),
        cost_estimate=cost(0, MIB),
        name="extend",
    )(table, in_hbm(front.reshape(2, 1024, 1024)), *[in_hbm(pieces)] * 2, *[g for g in got for _ in range(2)])


ORDERS = ((1, 3, 4, 12), (3, 1, 12, 4)), ((4, 12, 1, 3), (12, 4, 3, 1))


def update_kernel(table, front, *refs):
    blocks = refs[:4], refs[4:8]
    right_h, right_l, marks, out, panels = refs[8:]
    step = pl.program_id(0)
    span = pl.ds(pl.multiple_of(step % 2 * 256, 256), 256)
    col, core = table[COL], table[ROW] % 2

    def assemble(which):
        held, came, held_far, came_far = blocks[which]
        for c in range(16):
            one_x, three_x = flips((c ^ col) & 3)
            one_y, three_y = flips((c ^ col) >> 2)
            bits = {1: one_x, 3: three_x, 4: one_y, 12: three_y}
            even, odd = (ORDERS[q][which] for q in range(2))
            flip = [jnp.where(core == 0, bits[e], bits[o]) for e, o in zip(even, odd)]
            slot = flip[0] | (flip[1] << 1)
            later, far = flip[2] == 1, flip[3] == 1
            near_block = jnp.where(later, came[slot, span, :], held[slot, span, :])
            far_block = jnp.where(later, came_far[slot, span, :], held_far[slot, span, :])
            block = jnp.where(far, far_block, near_block)
            y, x = c // 4, c % 4
            rows = slice(0, 256) if y < 2 else slice(256, PANEL)
            first = min(y, 3 - y) * PANEL + x * BLK
            columns = slice(first, first + BLK)
            panels[0, rows, columns], panels[1, rows, columns] = split(block)

    for which in range(2):
        pl.when(step // 2 == which)(functools.partial(assemble, which))

    active = marks[...] == 0
    for piece in range(4):
        wide = slice(piece * 256, (piece + 1) * 256)
        change = dot3((panels[0], panels[1]), (right_h[:, wide], right_l[:, wide]))
        change = change.reshape(2, 256, 256)
        for j in range(2):
            columns = slice(piece * 256 + j * BLK, piece * 256 + (j + 1) * BLK)
            before, part = front[:, :, columns], change[:, :, j * BLK : (j + 1) * BLK]
            after = before - part
            if piece == 0 and j == 0:
                after = jnp.where(col < 8, part, after)
            out[:, :, columns] = jnp.where(active, after, before)


def update(table, front, blocks, right, marks):
    tile = pl.BlockSpec((2, 256, 1024), lambda t, s: (0, t, 0))
    return pl.pallas_call(
        update_kernel,
        out_shape=pltpu.HBM((2, 1024, 1024), F32),
        grid_spec=pltpu.PrefetchScalarGridSpec(
            num_scalar_prefetch=1,
            grid=(4,),
            in_specs=[
                tile,
                *[VMEM] * 10,
                pl.BlockSpec((2, 256, BLK), lambda t, s: (0, t, 0)),
            ],
            out_specs=tile,
            scratch_shapes=[pltpu.VMEM((2, PANEL, 1024), BF16)],
        ),
        compiler_params=params(24),
        cost_estimate=cost(2048 * 1024 * 1024, 4 * MIB),
        name="update",
    )(table, in_hbm(front), *blocks[0], *blocks[1], *right, marks.reshape(2, 1024, BLK))


def finish_kernel(
    table, list_other, list_mine, front, got, patch,
    out, held, read_sem, write_sem, sem,
):
    del front
    core = table[ROW] % 2
    copies = []
    places = [(2, m) for m in range(5, 10)] + [(j, m) for j in (3, 4) for m in range(10)]
    for n, (column, m) in enumerate(places):
        columns = pl.ds(pl.multiple_of(table[GOT_COL + column] * BLK, BLK), BLK)
        rows = pl.ds(pl.multiple_of(table[GOT_ROW + m] * BLK, BLK), BLK)
        there, here = out.at[rows, columns], held.at[n]
        read = pltpu.make_async_copy(there, here, read_sem.at[n])
        write = pltpu.make_async_copy(here, there, write_sem.at[n])
        copies.append((read, write))
    for read, _ in copies:
        read.start()
    for n, (read, write) in enumerate(copies):
        read.wait()
        held[n] += got[n]
        write.start()
    for _, write in copies:
        write.wait()

    def entry(n):
        return jnp.where(core == 0, list_other[n], list_mine[n])

    def place(n, carry):
        at, p = entry(n) >> 9, entry(n) & 511
        pltpu.make_async_copy(patch.at[pl.ds(p, 1), :], out.at[pl.ds(at, 1), :], sem).start()
        return carry

    def wait(_, carry):
        pltpu.make_async_copy(patch.at[pl.ds(0, 1), :], out.at[pl.ds(0, 1), :], sem).wait()
        return carry

    lax.fori_loop(0, entry(PANEL), place, 0)
    lax.fori_loop(0, entry(PANEL), wait, 0)


def finish(table, lists, front, got, patch):
    return pl.pallas_call(
        finish_kernel,
        out_shape=jax.ShapeDtypeStruct((2048, 1024), F32),
        in_specs=[SMEM, SMEM, SMEM, HBM] + [VMEM] * 2,
        out_specs=HBM,
        scratch_shapes=[
            pltpu.VMEM((25, BLK, BLK), F32),
            pltpu.SemaphoreType.DMA((25,)),
            pltpu.SemaphoreType.DMA((25,)),
            pltpu.SemaphoreType.DMA(()),
        ],
        input_output_aliases={3: 0},
        compiler_params=params(12),
        cost_estimate=cost(0, 8 * MIB),
        name="finish",
    )(table, *lists, front, got, patch)


def swap(block, axis, partner):
    count = lax.axis_size(axis)
    return lax.ppermute(block, axis, [(i, partner(i)) for i in range(count)])


def fold(block, near):
    came = lax.ppermute(block[1], "col", [(c, c ^ 12) for c in range(8)])
    return jnp.where(near, block[0], came)


def local(front, children, child_maps, pivots, diag_inverses):
    here_row, here_col = lax.axis_index("row"), lax.axis_index("col")
    chip = here_row >> 1
    together = lax.optimization_barrier
    pieces = children.reshape(10, 2, BLK, 640)

    def by_row(block, mask):
        return swap(block, "row", lambda i: i ^ mask)

    def by_col(block, mask):
        return swap(block, "col", lambda i: i ^ mask)

    bits = (chip ^ (chip >> 1)) & 1, chip >> 1
    rings = [[(r, r ^ ((2, 6), (6, 2))[r % 2][k]) for r in range(8)] for k in range(2)]
    low = [jnp.where(here_row & 1 == 0, bits[k], bits[1 - k]) == 0 for k in range(2)]
    pivots, near, low = together((pivots, here_col < 8, low))

    def halve(part, step):
        size = part.shape[0] // 2
        leave = jnp.where(low[step], part[size:], part[:size])
        stay = jnp.where(low[step], part[:size], part[size:])
        return stay + lax.ppermute(leave, "row", rings[step])

    def double(part, step):
        came = lax.ppermute(part, "row", rings[step])
        first, second = jnp.where(low[step], part, came), jnp.where(low[step], came, part)
        return jnp.concatenate([first, second], axis=0)

    def gather_step(block, which, step):
        route = [
            (r * 16 + c, r * 16 + (c ^ ORDERS[r % 2][which][step]))
            for r in range(8)
            for c in range(16)
        ]
        return lax.ppermute(block, ("row", "col"), route)

    first = cut(child_maps, pieces)
    got0 = by_row(first, 4)
    *rest, panel, corner, away, table = prepare(child_maps, pivots, front, pieces, first)
    rest_a, rest_b = rest
    corner = corner + by_row(away, 1)
    corner = corner + (by_row(corner, 2) + (by_row(corner, 6) + by_row(corner, 4)))
    away_rows, marks, list_other = pivot_terms(child_maps, pivots, front, children)
    got0, away_rows, rest_a, marks, corner = together((got0, away_rows, rest_a, marks, corner))

    top, bottom = whole_panel(table, panel, got0)
    mine = fold((top, bottom), near)
    corner = fold((corner, corner), near)[None]
    got_a = by_row(rest_a, 4)
    own_rows, marks, list_mine = pivot_terms(child_maps, pivots, front, children, marks)
    total = own_rows + by_row(away_rows, 1)
    mine, corner = together((mine, corner))
    total, got_a = together((total, got_a))

    def corner_step(block, step):
        masks = ((4, 1, 3), (1, 3, 4))
        route = [
            (r * 16 + c, r * 16 + (c ^ masks[r % 2][step])) for r in range(8) for c in range(16)
        ]
        return jnp.concatenate([block, lax.ppermute(block, ("row", "col"), route)], axis=0)

    held = [mine[None, :PANEL], mine[None, PANEL:]]
    for k in range(2):
        came = [gather_step(held[w], w, k) for w in range(2)]
        held = [jnp.concatenate([h, c], axis=0) for h, c in zip(held, came)]
        corner = corner_step(corner, k)
    total = halve(total, 0)
    held, corner, total = together((held, corner, total))
    came = [gather_step(held[w], w, 2) for w in range(2)]
    corner = corner_step(corner, 2)
    total = double(halve(total, 1), 1)
    came, corner, total = together((came, corner, total))
    held_far = [gather_step(held[w], w, 3) for w in range(2)]
    front = extend(table, front, pieces, (got0, got_a, got_a))
    *factors, cross = corners(table, corner, by_row(corner, 1), diag_inverses)
    came, held_far, total, rest_b, factors, cross, front = together(
        (came, held_far, double(total, 0), rest_b, factors, cross, front)
    )
    came_far = [gather_step(came[w], w, 3) for w in range(2)]
    got_b = by_row(rest_b, 4)
    *right, patch = right_factor(table, total, by_row(total, 1), factors, cross)
    came_far, right, patch = together((came_far, right, patch))
    blocks = [(held[w], came[w], held_far[w], came_far[w]) for w in range(2)]
    front = update(table, front, blocks, right, marks).reshape(2048, 1024)
    return finish(table, (list_other, list_mine), front, got_b, patch)


def solution(mesh):
    return jax.shard_map(
        local,
        mesh=mesh,
        in_specs=(P("row", "col"), P("row", "col"), P(), P(), P()),
        out_specs=P("row", "col"),
        check_vma=False,
    )
```
